32 devices in a mesh: seq: 8 (over z, y), mlp: 4 (over x, core).
Axes of the slice: x: 2, y: 2, z: 4, core: 2. Of those that a mesh axis runs over, the one named last changes fastest.
Arguments:
- residual: bfloat16 [8, 512, 3072], P('seq', None, 'mlp'), may hold values from -24 to 24
- spatial_qkv: bfloat16 [8, 512, 3, 1536], P('seq', None, None, 'mlp'), may hold values from -12 to 12
- spatial_out: bfloat16 [1536, 3072], P('mlp'), may hold values from -0.21875 to 0.21875
- temporal_qkv: bfloat16 [3072, 3, 1536], P(None, None, 'mlp'), may hold values from -0.5 to 0.5
- temporal_norm_shift: float32 [3072], replicated, may hold values from -3 to 3
- norm_scale: float32 [3072], replicated, may hold values from -3 to 3
- branch_gate: float32 [3072], replicated, may hold values from 0.5 to 1.5
Outputs:
- updated: bfloat16 [8, 512, 3072], P('seq', None, 'mlp')
- temporal_mix: bfloat16 [8, 512, 1536], P('seq', None, 'mlp')
The draws below stay inside these ranges and needn't reach their ends.
All inputs are finite; a program needn't handle non-finite values.
Results may differ from the reference program's by a relative error of at most 0.02.
Values may be sent and summed in bfloat16 or wider, within the bound.
No kernel may reach another device: no remote copies, remote signals or barrier semaphores. Data moves between devices by JAX's collectives and lax.ppermute only.
A program may use at most 64 MiB of HBM per device.

```python
import math
import jax
import jax.numpy as jnp
from jax import lax

D = 3072
HEADS = 12
HEAD_DIM = 128
PATCHES = 512
FRAMES = 8
N_MLP = 4


def draw_residual(key, part):
    keys_all = jax.random.split(key, 3)
    columns = jnp.arange(D, dtype=jnp.float32)
    rising = 1.0 + 2.0 * columns / (D - 1)
    base_draw = jax.random.normal(keys_all[0], (FRAMES, PATCHES, D), jnp.float32)
    col_scales = jnp.exp(jax.random.uniform(keys_all[2], (D,), jnp.float32, math.log(0.5), math.log(2.0)))
    values_out = base_draw * col_scales * rising * 0.5
    return jnp.clip(values_out, -24.0, 24.0).astype(jnp.bfloat16)


def draw_spatial_qkv(key, part):
    keys_all = jax.random.split(key, 1)
    width_all = HEADS * HEAD_DIM
    base_draw = 2.0 * jax.random.normal(keys_all[0], (FRAMES, PATCHES, 3, width_all), jnp.float32)
    return jnp.clip(base_draw, -12.0, 12.0).astype(jnp.bfloat16)


def draw_temporal_qkv(key, part):
    keys_all = jax.random.split(key, 1)
    width_all = HEADS * HEAD_DIM
    base_draw = jax.random.normal(keys_all[0], (D, 3, width_all), jnp.float32) / math.sqrt(D)
    return jnp.clip(base_draw, -0.5, 0.5).astype(jnp.bfloat16)


def strengthened(entries, stream_key, source, target, shards_of, factor):
    def block_of(axis_at):
        return (jnp.arange(entries.shape[axis_at]) // (entries.shape[axis_at] // shards_of)).reshape((-1,) + (1,) * (entries.ndim - 1 - axis_at))

    first = jax.random.permutation(stream_key, shards_of)[block_of(target)]
    far = (block_of(target) + shards_of // 2) % shards_of
    return jnp.where((block_of(source) == first) | (block_of(source) == far), factor * entries, entries)


def block_scale(key, extent, shards, low, largest):
    gain = 1.0
    for dim, shards_of in shards:
        heights = jax.random.uniform(jax.random.fold_in(jax.random.fold_in(key, 6), dim), (shards_of,), jnp.float32, low / len(shards), largest / len(shards))
        gain = gain * jnp.repeat(jnp.exp(heights), extent[dim] // shards_of).reshape((-1,) + (1,) * (len(extent) - 1 - dim))
    return gain


def normal_values(key, shape, scale, bound, cuts=(), kind=jnp.bfloat16):
    values = jax.random.normal(key, shape, jnp.float32) * scale
    if len(cuts) > 0:
        values = block_scale(key, shape, cuts, -0.22, 0.18) * values
    return jnp.clip(values, min=-bound, max=bound).astype(kind)


def bell_draw_with(key, extent, deviation, limit, cuts, heavy, kind=jnp.bfloat16):
    result = deviation * jax.random.normal(key, extent, jnp.float32)
    if cuts:
        result = result * block_scale(key, extent, cuts, -0.22, 0.18)
    return jnp.clip(strengthened(result, jax.random.fold_in(key, 3), *heavy), -limit, limit).astype(kind)


def setup_inputs(seed: int = 0) -> dict:
    streams_of = jax.random.split(jax.random.key(seed), 8)
    return {
        "residual": draw_residual(jax.random.fold_in(streams_of[7], 71), 0),
        "spatial_qkv": draw_spatial_qkv(jax.random.fold_in(streams_of[7], 71), 0),
        "spatial_out": bell_draw_with(streams_of[2], (HEADS * HEAD_DIM, D), (HEADS * HEAD_DIM) ** -0.5, 0.21875, ((0, 4),), (0, 1, 4, 2.0)),
        "temporal_qkv": draw_temporal_qkv(jax.random.fold_in(streams_of[7], 71), 0),
        "temporal_norm_shift": normal_values(streams_of[4], (D,), 0.5, 3.0, (), jnp.float32),
        "norm_scale": normal_values(streams_of[5], (D,), 0.5, 3.0, (), jnp.float32),
        "branch_gate": jnp.clip(jax.random.uniform(streams_of[6], (D,), jnp.float32, 0.5, 1.5), 0.5, 1.5),
    }


epsilon = 1e-06

def softmax_weights(attention_logits):
    row_top = lax.optimization_barrier(jnp.max(attention_logits, axis=-1, keepdims=True))
    exponent = jnp.exp(attention_logits - row_top)
    return (exponent / lax.optimization_barrier(jnp.sum(exponent, axis=-1, keepdims=True))).astype(jnp.bfloat16)

def attend(query_rows, key_matrix_rows, value_matrix_rows):
    attention_logits = jnp.einsum('xkj,ckj->kxc', query_rows.astype(jnp.float32), key_matrix_rows.astype(jnp.float32)) / math.sqrt(query_rows.shape[-1])
    attention_probs = softmax_weights(attention_logits)
    blended_head_output = jnp.einsum('kvb,bkx->vkx', attention_probs.astype(jnp.float32), value_matrix_rows.astype(jnp.float32))
    return blended_head_output.astype(jnp.bfloat16)

def rotation_rates(head_size):
    return 10000.0 ** (-2.0 * jnp.arange(head_size // 2, dtype=jnp.float32) / head_size)

def rotary(stacked, angles):
    half_size = stacked.shape[-1] // 2
    first_half = stacked[..., :half_size]
    second_half = stacked[..., half_size:]
    cosine = jnp.cos(angles)
    sine_part = jnp.sin(angles)
    return jnp.concatenate([first_half * cosine - second_half * sine_part, second_half * cosine + first_half * sine_part], axis=-1)

def modulate(row_data, temporal_norm_shift, norm_scale):
    values = row_data.astype(jnp.float32)
    row_mean = lax.optimization_barrier(jnp.mean(values, axis=-1, keepdims=True))
    spread = lax.optimization_barrier(jnp.mean(values * values, axis=-1, keepdims=True)) - row_mean * row_mean
    return ((values - row_mean) * lax.rsqrt(spread + epsilon) * (1.0 + norm_scale) + temporal_norm_shift).astype(jnp.bfloat16)

def reference(residual, spatial_qkv, spatial_out, temporal_qkv, temporal_norm_shift, norm_scale, branch_gate):
    full_width = HEADS * HEAD_DIM
    group_width = full_width // N_MLP

    def frame_heads(stacked):
        split_parts = stacked.reshape(PATCHES, 3, HEADS, HEAD_DIM)
        return attend(split_parts[:, 0], split_parts[:, 1], split_parts[:, 2]).reshape(PATCHES, full_width)
    spatial = lax.map(frame_heads, spatial_qkv)
    flat_heads = spatial.reshape(FRAMES * PATCHES, full_width)
    branch = jnp.zeros((FRAMES * PATCHES, D), jnp.float32)
    for group_index in range(N_MLP):
        lower = group_index * group_width
        group_term = jnp.dot(flat_heads[:, lower:lower + group_width], spatial_out[lower:lower + group_width], preferred_element_type=jnp.float32) * branch_gate
        branch = branch + lax.optimization_barrier(group_term.astype(jnp.bfloat16)).astype(jnp.float32)
    updated = (residual.reshape(FRAMES * PATCHES, D).astype(jnp.float32) + branch).astype(jnp.bfloat16)
    normed = modulate(updated, temporal_norm_shift, norm_scale).reshape(FRAMES, PATCHES, D)
    rates = rotation_rates(HEAD_DIM)
    weight_wide = temporal_qkv.astype(jnp.float32)

    def frame_project(inputs):
        row_data, places = inputs
        projected = jnp.einsum('pd,dch->pch', row_data.astype(jnp.float32), weight_wide).reshape(PATCHES, 3, HEADS, HEAD_DIM)
        turned = rotary(projected[:, :2], places * rates)
        return jnp.concatenate([turned, projected[:, 2:]], axis=1).astype(jnp.bfloat16)
    positions = jnp.arange(FRAMES, dtype=jnp.float32)
    temporal_proj = lax.map(frame_project, (normed, positions))
    by_patch = jnp.transpose(temporal_proj, (1, 0, 2, 3, 4))

    def patch_heads(stacked):
        return attend(stacked[:, 0], stacked[:, 1], stacked[:, 2])
    mixed = lax.map(patch_heads, by_patch)
    temporal_mix = jnp.transpose(mixed, (1, 0, 2, 3)).reshape(FRAMES, PATCHES, full_width)
    return (updated.reshape(FRAMES, PATCHES, D), temporal_mix)
```

```python
import functools
import math

import jax
import jax.numpy as jnp
from jax import lax
from jax.experimental import pallas as pl
from jax.experimental.pallas import tpu as pltpu
from jax.sharding import PartitionSpec as P

HEAD_DIM = 128
EPSILON = 1e-06
CHUNKS = 2
GROUP = 16
MASKED = -1e30
VMEM_LIMIT = 28 * 1024 * 1024
EXP2_SCALE = math.log2(math.e) / math.sqrt(HEAD_DIM)


def call(body, outs, flops, moved, exps=0):
    return pl.pallas_call(
        body,
        out_shape=outs,
        compiler_params=pltpu.CompilerParams(vmem_limit_bytes=VMEM_LIMIT),
        cost_estimate=pl.CostEstimate(
            flops=int(flops), bytes_accessed=int(moved), transcendentals=int(exps)
        ),
    )


def dot(a, b):
    return jnp.dot(a, b, preferred_element_type=jnp.float32)


def dot_nt(a, b):
    return lax.dot_general(a, b, (((1,), (1,)), ((), ())), preferred_element_type=jnp.float32)


def attend(query, key, value, same=None):
    logits = dot_nt(query, key)
    if same is not None:
        logits = jnp.where(same, logits, MASKED)
    top = jnp.max(logits, axis=-1, keepdims=True)
    weights = jnp.exp2((logits - top) * EXP2_SCALE)
    total = jnp.sum(weights, axis=-1, keepdims=True)
    return (dot(weights.astype(jnp.bfloat16), value) / total).astype(jnp.bfloat16)


def spatial_kernel(qkv_ref, out_ref, *, first):
    rows, width = out_ref.shape
    for lane in range(0, width, HEAD_DIM):
        head = slice(lane, lane + HEAD_DIM)
        out_ref[:, head] = attend(
            qkv_ref[0, first : first + rows, head], qkv_ref[1, :, head], qkv_ref[2, :, head]
        )


def send_kernel(own_ref, other_ref, own_w_ref, other_w_ref, gate_ref, out_ref):
    term = dot(own_ref[...], own_w_ref[...]) + dot(other_ref[...], other_w_ref[...])
    out_ref[...] = (term * gate_ref[...]).astype(out_ref.dtype)


def keep_kernel(own_ref, other_ref, own_w_ref, other_w_ref, gate_ref, residual_ref, out_ref):
    term = dot(own_ref[...], own_w_ref[...]) + dot(other_ref[...], other_w_ref[...])
    out_ref[...] = residual_ref[...].astype(jnp.float32) + term * gate_ref[...]


def update_kernel(place_ref, base_ref, arrived_ref, whole_ref, *piece_refs):
    whole_ref[...] = (base_ref[...] + arrived_ref[...].astype(jnp.float32)).astype(whole_ref.dtype)
    count = piece_refs[0].shape[0]
    for k, piece_ref in enumerate(piece_refs):
        start = pl.multiple_of((place_ref[0] ^ k) * count, count)
        piece_ref[...] = whole_ref[pl.ds(start, count), :]


def temporal_kernel(
    place_ref, u0, u1, u2, u3, w_ref, gain_ref, shift_ref, cos_ref, sin_ref, *rest, frames
):
    *out_refs, normed_ref, proj_ref = rest
    rows, share = u0.shape
    count = rows // frames
    width = w_ref.shape[-1]
    blocks = (u0, u1, u2, u3)
    total = jnp.zeros((rows, 1), jnp.float32)
    square = jnp.zeros((rows, 1), jnp.float32)
    for ref in blocks:
        values = ref[...].astype(jnp.float32)
        total += jnp.sum(values, axis=-1, keepdims=True)
        square += jnp.sum(values * values, axis=-1, keepdims=True)
    features = share * len(blocks)
    mean = total / features
    rate = lax.rsqrt(square / features - mean * mean + EPSILON)
    starts = [pl.multiple_of((place_ref[0] ^ k) * share, share) for k in range(len(blocks))]
    for k, ref in enumerate(blocks):
        gain = 1.0 + gain_ref[:, pl.ds(starts[k], share)]
        shift = shift_ref[:, pl.ds(starts[k], share)]
        normed_ref[k] = ((ref[...].astype(jnp.float32) - mean) * rate * gain + shift).astype(
            normed_ref.dtype
        )
    for part in range(3):
        acc = dot(normed_ref[0], w_ref[part, pl.ds(starts[0], share), :])
        for k in range(1, len(blocks)):
            acc += dot(normed_ref[k], w_ref[part, pl.ds(starts[k], share), :])
        if part == 2:
            proj_ref[part] = acc.astype(proj_ref.dtype)
            continue
        shaped = acc.reshape(frames, count, width)
        cosine = cos_ref[...][:, None, :]
        sine = sin_ref[...][:, None, :]
        for lane in range(0, width, HEAD_DIM):
            head = shaped[:, :, lane : lane + HEAD_DIM]
            turned = pltpu.roll(head.reshape(rows, HEAD_DIM), HEAD_DIM // 2, 1).reshape(head.shape)
            proj_ref[part, :, lane : lane + HEAD_DIM] = (
                (head * cosine + turned * sine).reshape(rows, HEAD_DIM).astype(proj_ref.dtype)
            )
    step = GROUP if count % GROUP == 0 else count
    size = step * frames
    patch_of = lambda axis: lax.rem(lax.broadcasted_iota(jnp.int32, (size, size), axis), step)
    same = patch_of(0) == patch_of(1)
    for low in range(0, count, step):
        for lane in range(0, width, HEAD_DIM):
            head = slice(lane, lane + HEAD_DIM)

            def gathered(part):
                if step == count:
                    return proj_ref[part, :, head]
                return jnp.concatenate(
                    [
                        proj_ref[part, f * count + low : f * count + low + step, head]
                        for f in range(frames)
                    ],
                    axis=0,
                )

            mixed = attend(gathered(0), gathered(1), gathered(2), same)
            if len(out_refs) == 1:
                out_refs[0][:, head] = mixed
            else:
                for f, out_ref in enumerate(out_refs):
                    out_ref[low : low + step, head] = mixed[f * step : (f + 1) * step]


def gather_kernel(place_ref, *rest, chunks):
    *piece_refs, out_ref = rest
    many = len(piece_refs) // chunks
    count = piece_refs[0].shape[0]
    for c in range(chunks):
        for k in range(many):
            start = pl.multiple_of(c * many * count + (place_ref[0] ^ k) * count, count)
            out_ref[pl.ds(start, count), :] = piece_refs[c * many + k][...]


def swap(value, axis, size, k):
    return lax.ppermute(value, axis, [(i, i ^ k) for i in range(size)])


def smem(count):
    return [pl.BlockSpec(memory_space=pltpu.SMEM)] * count


def on_device(
    residual, spatial_qkv, spatial_out, temporal_qkv, shift, scale, gate, *, n_seq, n_mlp
):
    frames, patches, share = residual.shape
    width = spatial_qkv.shape[-1]
    features = share * n_mlp
    tokens = frames * patches
    pairwise = n_seq == 8 and frames == 1 and patches % (n_seq * CHUNKS * GROUP) == 0
    chunks = CHUNKS if pairwise else 1
    rows = tokens // chunks
    count = rows // n_seq
    seq, mlp = lax.axis_index("seq"), lax.axis_index("mlp")
    seq_place, mlp_place = seq.reshape(1), mlp.reshape(1)
    flat_residual = residual.reshape(tokens, share)
    qkv = spatial_qkv.transpose(2, 0, 1, 3).reshape(3, tokens, width)
    weights = temporal_qkv.transpose(1, 0, 2)
    vm = pl.BlockSpec(memory_space=pltpu.VMEM)
    bf16, f32 = jnp.bfloat16, jnp.float32

    def columns(array, block):
        return lax.dynamic_slice_in_dim(array, block * share, share, 1)

    gate_row = gate.reshape(1, features)
    own_send, own_keep = columns(spatial_out, mlp ^ 2), columns(spatial_out, mlp)
    other_send = swap(columns(spatial_out, mlp ^ 3), "mlp", n_mlp, 1)
    other_keep = swap(columns(spatial_out, mlp ^ 1), "mlp", n_mlp, 1)
    gate_send, gate_keep = columns(gate_row, mlp ^ 2), columns(gate_row, mlp)

    rates = 10000.0 ** (-2.0 * jnp.arange(HEAD_DIM // 2, dtype=f32) / HEAD_DIM)
    order = jnp.arange(n_seq) ^ seq if pairwise else jnp.arange(n_seq)
    angles = order.astype(f32)[:, None] * rates
    cosine = jnp.concatenate([jnp.cos(angles)] * 2, axis=1)
    sine = jnp.concatenate([-jnp.sin(angles), jnp.sin(angles)], axis=1)

    matmul_bytes = 4 * share * width + 4 * rows * width + 6 * rows * share
    updates, results = [], []
    for c in range(chunks):
        heads = call(
            functools.partial(spatial_kernel, first=c * rows),
            jax.ShapeDtypeStruct((rows, width), bf16),
            4 * rows * tokens * width,
            2 * (3 * tokens * width),
            rows * tokens * width // HEAD_DIM,
        )(qkv)
        others = swap(heads, "mlp", n_mlp, 1)
        sent = call(
            send_kernel,
            jax.ShapeDtypeStruct((rows, share), bf16),
            4 * rows * width * share,
            matmul_bytes,
        )(heads, others, own_send, other_send, gate_send)
        arrived = swap(sent, "mlp", n_mlp, 2)
        base = call(
            keep_kernel,
            jax.ShapeDtypeStruct((rows, share), f32),
            4 * rows * width * share,
            matmul_bytes,
        )(heads, others, own_keep, other_keep, gate_keep, flat_residual[c * rows : (c + 1) * rows])
        if pairwise:
            updated, *pieces = pl.pallas_call(
                update_kernel,
                out_shape=[jax.ShapeDtypeStruct((rows, share), bf16)]
                + [jax.ShapeDtypeStruct((count, share), bf16)] * n_seq,
                in_specs=smem(1) + [vm] * 2,
                out_specs=[vm] * (1 + n_seq),
                compiler_params=pltpu.CompilerParams(vmem_limit_bytes=VMEM_LIMIT),
                cost_estimate=pl.CostEstimate(
                    flops=rows * share, bytes_accessed=10 * rows * share, transcendentals=0
                ),
            )(seq_place, base, arrived)
            pieces = [pieces[0]] + [swap(pieces[k], "seq", n_seq, k) for k in range(1, n_seq)]
            mine = jnp.concatenate(pieces, axis=0)
        else:
            updated = (base + arrived.astype(f32)).astype(bf16)
            mine = lax.all_to_all(
                updated.reshape(n_seq, count, share), "seq", 0, 0, tiled=True
            ).reshape(rows, share)
        updates.append(updated)
        across = swap(mine, "mlp", n_mlp, 2)
        beside = swap(mine, "mlp", n_mlp, 1)
        diagonal = swap(across, "mlp", n_mlp, 1)
        outs = (
            [jax.ShapeDtypeStruct((count, width), bf16)] * n_seq
            if pairwise
            else [jax.ShapeDtypeStruct((rows, width), bf16)]
        )
        mixed = pl.pallas_call(
            functools.partial(temporal_kernel, frames=n_seq),
            out_shape=outs,
            in_specs=smem(1) + [vm] * 9,
            out_specs=[vm] * len(outs),
            scratch_shapes=[
                pltpu.VMEM((n_mlp, rows, share), bf16),
                pltpu.VMEM((3, rows, width), bf16),
            ],
            compiler_params=pltpu.CompilerParams(vmem_limit_bytes=VMEM_LIMIT),
            cost_estimate=pl.CostEstimate(
                flops=6 * rows * features * width,
                bytes_accessed=6 * features * width + 2 * rows * features,
                transcendentals=rows * 128 * width // HEAD_DIM,
            ),
        )(
            mlp_place, mine, beside, across, diagonal, weights,
            scale.reshape(1, features), shift.reshape(1, features), cosine, sine,
        )
        if pairwise:
            results += [mixed[0]] + [swap(mixed[k], "seq", n_seq, k) for k in range(1, n_seq)]
        else:
            back = lax.all_to_all(
                mixed[0].reshape(n_seq, count, width), "seq", 0, 0, tiled=True
            )
            results.append(back.reshape(rows, width))
    if pairwise:
        result = pl.pallas_call(
            functools.partial(gather_kernel, chunks=chunks),
            out_shape=jax.ShapeDtypeStruct((tokens, width), bf16),
            in_specs=smem(1) + [vm] * len(results),
            out_specs=vm,
            compiler_params=pltpu.CompilerParams(vmem_limit_bytes=VMEM_LIMIT),
        )(seq_place, *results)
    else:
        result = results[0]
    return (
        jnp.concatenate(updates, axis=0).reshape(frames, patches, share),
        result.reshape(frames, patches, width),
    )


def solution(mesh):
    return jax.shard_map(
        functools.partial(on_device, n_seq=mesh.shape["seq"], n_mlp=mesh.shape["mlp"]),
        mesh=mesh,
        in_specs=(
            P("seq", None, "mlp"),
            P("seq", None, None, "mlp"),
            P("mlp", None),
            P(None, None, "mlp"),
            P(),
            P(),
            P(),
        ),
        out_specs=(P("seq", None, "mlp"), P("seq", None, "mlp")),
        check_vma=False,
    )
```

```python
import functools
import math

import jax
import jax.numpy as jnp
from jax import lax
from jax.experimental import pallas as pl
from jax.experimental.pallas import tpu as pltpu
from jax.sharding import PartitionSpec as P

HEAD_DIM = 128
EPSILON = 1e-06
CHUNKS = 2
GROUP = 16
MASKED = -1e30
VMEM_LIMIT = 28 * 1024 * 1024
EXP2_SCALE = math.log2(math.e) / math.sqrt(HEAD_DIM)


def call(body, outs, flops, moved, exps=0):
    return pl.pallas_call(
        body,
        out_shape=outs,
        compiler_params=pltpu.CompilerParams(vmem_limit_bytes=VMEM_LIMIT),
        cost_estimate=pl.CostEstimate(
            flops=int(flops), bytes_accessed=int(moved), transcendentals=int(exps)
        ),
    )


def dot(a, b):
    return jnp.dot(a, b, preferred_element_type=jnp.float32)


def dot_nt(a, b):
    return lax.dot_general(a, b, (((1,), (1,)), ((), ())), preferred_element_type=jnp.float32)


def attend(query, key, value, same=None):
    logits = dot_nt(query, key)
    if same is not None:
        logits = jnp.where(same, logits, MASKED)
    top = jnp.max(logits, axis=-1, keepdims=True)
    weights = jnp.exp2((logits - top) * EXP2_SCALE)
    total = jnp.sum(weights, axis=-1, keepdims=True)
    return (dot(weights.astype(jnp.bfloat16), value) / total).astype(jnp.bfloat16)


def spatial_kernel(qkv_ref, out_ref, *, first):
    rows, width = out_ref.shape
    for lane in range(0, width, HEAD_DIM):
        head = slice(lane, lane + HEAD_DIM)
        out_ref[:, head] = attend(
            qkv_ref[0, first : first + rows, head], qkv_ref[1, :, head], qkv_ref[2, :, head]
        )


def send_kernel(own_ref, other_ref, own_w_ref, other_w_ref, gate_ref, out_ref):
    term = dot(own_ref[...], own_w_ref[...]) + dot(other_ref[...], other_w_ref[...])
    out_ref[...] = (term * gate_ref[...]).astype(out_ref.dtype)


def keep_kernel(own_ref, other_ref, own_w_ref, other_w_ref, gate_ref, residual_ref, out_ref):
    term = dot(own_ref[...], own_w_ref[...]) + dot(other_ref[...], other_w_ref[...])
    out_ref[...] = residual_ref[...].astype(jnp.float32) + term * gate_ref[...]


def temporal_kernel(
    place_ref, u0, u1, u2, u3, w_ref, gain_ref, shift_ref, cos_ref, sin_ref, out_ref,
    normed_ref, proj_ref, *, frames
):
    rows, share = u0.shape
    count = rows // frames
    width = w_ref.shape[-1]
    blocks = (u0, u1, u2, u3)
    total = jnp.zeros((rows, 1), jnp.float32)
    square = jnp.zeros((rows, 1), jnp.float32)
    for ref in blocks:
        values = ref[...].astype(jnp.float32)
        total += jnp.sum(values, axis=-1, keepdims=True)
        square += jnp.sum(values * values, axis=-1, keepdims=True)
    features = share * len(blocks)
    mean = total / features
    rate = lax.rsqrt(square / features - mean * mean + EPSILON)
    starts = [pl.multiple_of((place_ref[0] ^ k) * share, share) for k in range(len(blocks))]
    for k, ref in enumerate(blocks):
        gain = 1.0 + gain_ref[:, pl.ds(starts[k], share)]
        shift = shift_ref[:, pl.ds(starts[k], share)]
        normed_ref[k] = ((ref[...].astype(jnp.float32) - mean) * rate * gain + shift).astype(
            normed_ref.dtype
        )
    for part in range(3):
        acc = dot(normed_ref[0], w_ref[part, pl.ds(starts[0], share), :])
        for k in range(1, len(blocks)):
            acc += dot(normed_ref[k], w_ref[part, pl.ds(starts[k], share), :])
        if part == 2:
            proj_ref[part] = acc.astype(proj_ref.dtype)
            continue
        shaped = acc.reshape(frames, count, width)
        cosine = cos_ref[...][:, None, :]
        sine = sin_ref[...][:, None, :]
        for lane in range(0, width, HEAD_DIM):
            head = shaped[:, :, lane : lane + HEAD_DIM]
            turned = pltpu.roll(head.reshape(rows, HEAD_DIM), HEAD_DIM // 2, 1).reshape(head.shape)
            proj_ref[part, :, lane : lane + HEAD_DIM] = (
                (head * cosine + turned * sine).reshape(rows, HEAD_DIM).astype(proj_ref.dtype)
            )
    step = GROUP if count % GROUP == 0 else count
    size = step * frames
    patch_of = lambda axis: lax.rem(lax.broadcasted_iota(jnp.int32, (size, size), axis), step)
    same = patch_of(0) == patch_of(1)
    for low in range(0, count, step):
        for lane in range(0, width, HEAD_DIM):
            head = slice(lane, lane + HEAD_DIM)

            def gathered(part):
                if step == count:
                    return proj_ref[part, :, head]
                return jnp.concatenate(
                    [
                        proj_ref[part, f * count + low : f * count + low + step, head]
                        for f in range(frames)
                    ],
                    axis=0,
                )

            mixed = attend(gathered(0), gathered(1), gathered(2), same)
            if step == count:
                out_ref[:, head] = mixed
                continue
            for f in range(frames):
                start = f * count + low
                out_ref[start : start + step, head] = mixed[f * step : (f + 1) * step]


def swap(value, axis, size, k):
    return lax.ppermute(value, axis, [(i, i ^ k) for i in range(size)])


def smem(count):
    return [pl.BlockSpec(memory_space=pltpu.SMEM)] * count


def on_device(
    residual, spatial_qkv, spatial_out, temporal_qkv, shift, scale, gate, *, n_seq, n_mlp
):
    frames, patches, share = residual.shape
    width = spatial_qkv.shape[-1]
    features = share * n_mlp
    tokens = frames * patches
    chunks = CHUNKS if tokens % (n_seq * CHUNKS * GROUP) == 0 else 1
    rows = tokens // chunks
    count = rows // n_seq
    mlp = lax.axis_index("mlp")
    mlp_place = mlp.reshape(1)
    flat_residual = residual.reshape(tokens, share)
    qkv = spatial_qkv.transpose(2, 0, 1, 3).reshape(3, tokens, width)
    weights = temporal_qkv.transpose(1, 0, 2)
    vm = pl.BlockSpec(memory_space=pltpu.VMEM)
    bf16, f32 = jnp.bfloat16, jnp.float32

    def columns(array, block):
        return lax.dynamic_slice_in_dim(array, block * share, share, 1)

    gate_row = gate.reshape(1, features)
    own_send, own_keep = columns(spatial_out, mlp ^ 2), columns(spatial_out, mlp)
    other_send = swap(columns(spatial_out, mlp ^ 3), "mlp", n_mlp, 1)
    other_keep = swap(columns(spatial_out, mlp ^ 1), "mlp", n_mlp, 1)
    gate_send, gate_keep = columns(gate_row, mlp ^ 2), columns(gate_row, mlp)

    rates = 10000.0 ** (-2.0 * jnp.arange(HEAD_DIM // 2, dtype=f32) / HEAD_DIM)
    angles = jnp.arange(n_seq, dtype=f32)[:, None] * rates
    cosine = jnp.concatenate([jnp.cos(angles)] * 2, axis=1)
    sine = jnp.concatenate([-jnp.sin(angles), jnp.sin(angles)], axis=1)

    matmul_bytes = 4 * share * width + 4 * rows * width + 6 * rows * share
    updates, results = [], []
    for c in range(chunks):
        heads = call(
            functools.partial(spatial_kernel, first=c * rows),
            jax.ShapeDtypeStruct((rows, width), bf16),
            4 * rows * tokens * width,
            2 * (3 * tokens * width),
            rows * tokens * width // HEAD_DIM,
        )(qkv)
        others = swap(heads, "mlp", n_mlp, 1)
        sent = call(
            send_kernel,
            jax.ShapeDtypeStruct((rows, share), bf16),
            4 * rows * width * share,
            matmul_bytes,
        )(heads, others, own_send, other_send, gate_send)
        arrived = swap(sent, "mlp", n_mlp, 2)
        base = call(
            keep_kernel,
            jax.ShapeDtypeStruct((rows, share), f32),
            4 * rows * width * share,
            matmul_bytes,
        )(heads, others, own_keep, other_keep, gate_keep, flat_residual[c * rows : (c + 1) * rows])
        updated = (base + arrived.astype(f32)).astype(bf16)
        mine = lax.all_to_all(
            updated.reshape(n_seq, count, share), "seq", 0, 0, tiled=True
        ).reshape(rows, share)
        updates.append(updated)
        across = swap(mine, "mlp", n_mlp, 2)
        beside = swap(mine, "mlp", n_mlp, 1)
        diagonal = swap(across, "mlp", n_mlp, 1)
        mixed = pl.pallas_call(
            functools.partial(temporal_kernel, frames=n_seq),
            out_shape=jax.ShapeDtypeStruct((rows, width), bf16),
            in_specs=smem(1) + [vm] * 9,
            out_specs=vm,
            scratch_shapes=[
                pltpu.VMEM((n_mlp, rows, share), bf16),
                pltpu.VMEM((3, rows, width), bf16),
            ],
            compiler_params=pltpu.CompilerParams(vmem_limit_bytes=VMEM_LIMIT),
            cost_estimate=pl.CostEstimate(
                flops=6 * rows * features * width,
                bytes_accessed=6 * features * width + 2 * rows * features,
                transcendentals=rows * 128 * width // HEAD_DIM,
            ),
        )(
            mlp_place, mine, beside, across, diagonal, weights,
            scale.reshape(1, features), shift.reshape(1, features), cosine, sine,
        )
        results.append(
            lax.all_to_all(
                mixed.reshape(n_seq, count, width), "seq", 0, 0, tiled=True
            ).reshape(rows, width)
        )
    result = jnp.concatenate(results, axis=0)
    return (
        jnp.concatenate(updates, axis=0).reshape(frames, patches, share),
        result.reshape(frames, patches, width),
    )


def solution(mesh):
    return jax.shard_map(
        functools.partial(on_device, n_seq=mesh.shape["seq"], n_mlp=mesh.shape["mlp"]),
        mesh=mesh,
        in_specs=(
            P("seq", None, "mlp"),
            P("seq", None, None, "mlp"),
            P("mlp", None),
            P(None, None, "mlp"),
            P(),
            P(),
            P(),
        ),
        out_specs=(P("seq", None, "mlp"), P("seq", None, "mlp")),
        check_vma=False,
    )
```

```python
import functools
import math

import jax
import jax.numpy as jnp
import numpy as np
from jax import lax
from jax.experimental import pallas as pl
from jax.experimental.pallas import tpu as pltpu
from jax.sharding import PartitionSpec as P

HEAD_DIM = 128
EPSILON = 1e-06
GROUP = 16
MASKED = -1e30
VMEM_LIMIT = 16 * 1024 * 1024
EXP2_SCALE = math.log2(math.e) / math.sqrt(HEAD_DIM)
CHUNK_ROWS = (256, 256)
PARTNERS = ((7, 4, 2, 0), (5, 3, 6, 1))
SHARES = len(PARTNERS[0])


def call(body, outs, flops=0, moved=0, exps=0, inputs=0, scratch=(), far=0):
    return pl.pallas_call(
        body,
        out_shape=outs,
        in_specs=[pl.BlockSpec(memory_space=pltpu.VMEM)] * (inputs - far)
        + [pl.BlockSpec(memory_space=pltpu.HBM)] * far,
        scratch_shapes=list(scratch),
        compiler_params=pltpu.CompilerParams(vmem_limit_bytes=VMEM_LIMIT),
        cost_estimate=pl.CostEstimate(
            flops=int(flops), bytes_accessed=int(moved), transcendentals=int(exps)
        ),
    )


def dot(a, b):
    return jnp.dot(a, b, preferred_element_type=jnp.float32)


def dot_nt(a, b):
    return lax.dot_general(a, b, (((1,), (1,)), ((), ())), preferred_element_type=jnp.float32)


def attend(query, key, value, same=None):
    logits = dot_nt(query, key)
    if same is not None:
        logits = jnp.where(same, logits, MASKED)
    top = jnp.max(logits, axis=-1, keepdims=True)
    weights = jnp.exp2((logits - top) * EXP2_SCALE)
    total = jnp.sum(weights, axis=-1, keepdims=True)
    return (dot(weights.astype(jnp.bfloat16), value) / total).astype(jnp.bfloat16)


def project_and_mix(parts, frame_of, write, w_ref, gain_ref, shift_ref, cos_ref, sin_ref, normed_ref, proj_ref):
    features, width = w_ref.shape[1:]
    frames = cos_ref.shape[0]
    rows = normed_ref.shape[0]
    count = rows // frames
    first = 0
    for part in parts:
        size = part[0][0].shape[0]
        total = jnp.zeros((size, 1), jnp.float32)
        square = jnp.zeros((size, 1), jnp.float32)
        for ref, _ in part:
            values = ref[...].astype(jnp.float32)
            total += jnp.sum(values, axis=-1, keepdims=True)
            square += jnp.sum(values * values, axis=-1, keepdims=True)
        mean = total / features
        rate = lax.rsqrt(square / features - mean * mean + EPSILON)
        for ref, start in part:
            lanes = pl.ds(start, ref.shape[-1])
            gain = 1.0 + gain_ref[:, lanes]
            normed_ref[first : first + size, lanes] = (
                (ref[...].astype(jnp.float32) - mean) * rate * gain + shift_ref[:, lanes]
            ).astype(normed_ref.dtype)
        first += size
    for part in range(3):
        acc = dot(normed_ref[...], w_ref[part])
        if part == 2:
            proj_ref[part] = acc.astype(proj_ref.dtype)
            continue
        for f in range(frames):
            row = pl.ds(frame_of(f), 1)
            cosine, sine = cos_ref[row, :], sin_ref[row, :]
            span = slice(f * count, (f + 1) * count)
            for lane in range(0, width, HEAD_DIM):
                head = acc[span, lane : lane + HEAD_DIM]
                turned = pltpu.roll(head, HEAD_DIM // 2, 1)
                proj_ref[part, span, lane : lane + HEAD_DIM] = (
                    head * cosine + turned * sine
                ).astype(proj_ref.dtype)
    step = GROUP if count % GROUP == 0 else count
    size = step * frames
    patch_of = lambda axis: lax.rem(lax.broadcasted_iota(jnp.int32, (size, size), axis), step)
    same = patch_of(0) == patch_of(1)
    for low in range(0, count, step):
        for lane in range(0, width, HEAD_DIM):
            head = slice(lane, lane + HEAD_DIM)

            def gathered(part):
                if step == count:
                    return proj_ref[part, :, head]
                return jnp.concatenate(
                    [
                        proj_ref[part, f * count + low : f * count + low + step, head]
                        for f in range(frames)
                    ],
                    axis=0,
                )

            mixed = attend(gathered(0), gathered(1), gathered(2), same)
            for f in range(frames):
                write(f, low, head, mixed[f * step : (f + 1) * step])


def core_of():
    return lax.rem(lax.axis_index("mlp"), 2)


def chip_of():
    return lax.div(lax.axis_index("mlp"), 2)


def frame_of(i):
    low, high = (PARTNERS[core][i % SHARES] for core in range(2))
    which = core_of() if i < SHARES else 1 - core_of()
    return lax.axis_index("seq") ^ (low + which * (high - low))


def piece_span(first, count, i):
    return pl.ds(pl.multiple_of(first + frame_of(i) * count, count), count)


def piece_rows(ref, first, count, lanes):
    return jnp.concatenate(
        [ref[piece_span(first, count, i), lanes] for i in range(2 * SHARES)], axis=0
    )


def chip_columns(features, flip):
    half = features // 2
    return pl.ds(pl.multiple_of((chip_of() ^ flip) * half, half), half)


def spatial_body(qkv_ref, far_w_ref, far_gate, heads_ref, message_ref, first, before_message):
    rows, width = heads_ref.shape
    for lane in range(0, width, HEAD_DIM):
        head = slice(lane, lane + HEAD_DIM)
        query = piece_rows(qkv_ref.at[0], first, rows // (2 * SHARES), head)
        heads_ref[:, head] = attend(query, qkv_ref[1, :, head], qkv_ref[2, :, head])
    before_message()
    message_ref[...] = (dot(heads_ref[rows // 2 :, :], far_w_ref[...]) * far_gate).astype(
        message_ref.dtype
    )


def first_spatial_kernel(
    gate_ref, qkv_far, w_far, heads_ref, message_ref, qkv_ref, w_ref, semaphores, *, first
):
    columns = chip_columns(w_far.shape[-1], 1)
    copies = [
        pltpu.make_async_copy(qkv_far, qkv_ref, semaphores.at[0]),
        pltpu.make_async_copy(w_far.at[:, columns], w_ref, semaphores.at[1]),
    ]
    for copy in copies:
        copy.start()
    copies[0].wait()
    spatial_body(
        qkv_ref, w_ref, gate_ref[:, columns], heads_ref, message_ref, first, copies[1].wait
    )


def spatial_kernel(gate_ref, qkv_ref, w_ref, heads_ref, message_ref, *, first):
    columns = chip_columns(w_ref.shape[-1], 1)
    spatial_body(
        qkv_ref,
        w_ref.at[:, columns],
        gate_ref[:, columns],
        heads_ref,
        message_ref,
        first,
        lambda: None,
    )


def terms_kernel(
    heads_ref, w_ref, gate_ref, residual_ref, far_ref, base_ref, message_ref, *, first
):
    half, both = base_ref.shape
    share = both // 2
    features = w_ref.shape[-1]
    far = chip_columns(features, 1)
    far_ref[...] = dot(heads_ref[:half, :], w_ref[:, far]) * gate_ref[:, far]
    for flip in range(2):
        place = pl.multiple_of((core_of() ^ flip) * share, share)
        lanes = pl.ds(pl.multiple_of(chip_of() * both + place, share), share)
        term = dot(heads_ref[...], w_ref[:, lanes]) * gate_ref[:, lanes]
        if flip == 0:
            term += piece_rows(residual_ref, first, half // SHARES, slice(None)).astype(
                jnp.float32
            )
        base_ref[:, pl.ds(place, share)] = term[:half]
        message_ref[:, pl.ds(place, share)] = term[half:].astype(message_ref.dtype)


def add_kernel(a_ref, b_ref, out_ref):
    out_ref[...] = (a_ref[...] + b_ref[...].astype(jnp.float32)).astype(out_ref.dtype)


def update_kernel(base_ref, message_ref, arrived_ref, own_ref, other_ref, *piece_refs):
    updated = (
        base_ref[...] + message_ref[...].astype(jnp.float32) + arrived_ref[...].astype(jnp.float32)
    ).astype(jnp.bfloat16)
    count = piece_refs[0].shape[0]
    for i, piece_ref in enumerate(piece_refs):
        piece_ref[...] = updated[i * count : (i + 1) * count]
    share = own_ref.shape[-1]
    left, right = updated[:, :share], updated[:, share:]
    core = core_of()
    own_ref[...] = jnp.where(core == 0, left, right)
    other_ref[...] = jnp.where(core == 0, right, left)


def split_temporal_kernel(own_near, own_far, other_near, other_far, w_ref, gain_ref, shift_ref, cos_ref, sin_ref, own_ref, other_ref, *scratch):
    half = own_near.shape[-1]
    near, far = (pl.multiple_of((chip_of() ^ flip) * half, half) for flip in range(2))
    count = own_ref.shape[0] // SHARES

    def write(i, low, head, value):
        ref = own_ref if i < SHARES else other_ref
        start = (i % SHARES) * count + low
        ref[start : start + value.shape[0], head] = value

    project_and_mix(
        [[(own_near, near), (own_far, far)], [(other_near, near), (other_far, far)]],
        frame_of,
        write,
        w_ref,
        gain_ref,
        shift_ref,
        cos_ref,
        sin_ref,
        *scratch,
    )


def pack_kernel(*refs):
    block_refs, out_refs = refs[:-SHARES], refs[-SHARES:]
    for i, out_ref in enumerate(out_refs):
        start = 0
        for ref in block_refs:
            count = ref.shape[0] // SHARES
            out_ref[start : start + count] = ref[i * count : (i + 1) * count]
            start += count


def unpack_kernel(*refs):
    *piece_refs, out_ref = refs
    count = piece_refs[0].shape[0] // 2
    for i, ref in enumerate(piece_refs):
        out_ref[i * count : (i + 1) * count] = ref[count:]


def place_updated_kernel(*refs, chunks):
    *block_refs, out_ref = refs
    for (first, rows), own_ref, other_ref in zip(chunks, block_refs[::2], block_refs[1::2]):
        count = rows // (2 * SHARES)
        for i in range(2 * SHARES):
            ref = own_ref if i < SHARES else other_ref
            start = (i % SHARES) * count
            out_ref[piece_span(first, count, i), :] = ref[start : start + count, :]


def place_mixed_kernel(*refs, chunks):
    *own_refs, other_ref, out_ref = refs
    size = own_refs[0].shape[0] // 2
    start = 0
    for first, rows in chunks:
        count = rows // (2 * SHARES)
        for i in range(SHARES):
            out_ref[piece_span(first, count, i), :] = own_refs[i][start : start + count, :]
            low = i * size + start
            out_ref[piece_span(first, count, SHARES + i), :] = other_ref[low : low + count, :]
        start += count


def swap(value, axis, size, k):
    return lax.ppermute(value, axis, [(i, i ^ k) for i in range(size)])


def rotation_tables(frames):
    rates = 10000.0 ** (-2.0 * np.arange(HEAD_DIM // 2, dtype=np.float32) / HEAD_DIM)
    angles = np.arange(frames, dtype=np.float32)[:, None] * rates.astype(np.float32)
    cosine, sine = np.cos(angles), np.sin(angles)
    return (
        jnp.asarray(np.concatenate([cosine, cosine], axis=1), jnp.float32),
        jnp.asarray(np.concatenate([-sine, sine], axis=1), jnp.float32),
    )


def piece_pairs(n_seq, n_mlp, index):
    return [
        (s * n_mlp + m, (s ^ PARTNERS[m % 2][index]) * n_mlp + m)
        for s in range(n_seq)
        for m in range(n_mlp)
    ]


def after(value, *others):
    return lax.optimization_barrier((value,) + others)[0]


def split_on_device(
    residual, spatial_qkv, spatial_out, temporal_qkv, shift, scale, gate, *, n_seq, n_mlp
):
    frames, patches, share = residual.shape
    width = spatial_qkv.shape[-1]
    features = share * n_mlp
    both = 2 * share
    tokens = frames * patches
    bf16, f32 = jnp.bfloat16, jnp.float32
    flat_residual = residual.reshape(tokens, share)
    qkv = spatial_qkv.transpose(2, 0, 1, 3).reshape(3, tokens, width)
    weights = temporal_qkv.transpose(1, 0, 2)
    gate_row = gate.reshape(1, features)
    gain_row, shift_row = scale.reshape(1, features), shift.reshape(1, features)
    cosine, sine = rotation_tables(n_seq)

    def shape(rows, columns, kind=bf16):
        return jax.ShapeDtypeStruct((rows, columns), kind)

    def send_pieces(pieces):
        return [
            lax.ppermute(piece, ("seq", "mlp"), piece_pairs(n_seq, n_mlp, i))
            for i, piece in enumerate(pieces)
        ]

    chunks = []
    first = 0
    for rows in CHUNK_ROWS:
        chunks.append((first, rows))
        first += rows

    reduced = []
    previous = None
    for first, rows in chunks:
        half = rows // 2
        if previous is None:
            heads, message = call(
                functools.partial(first_spatial_kernel, first=first),
                [shape(rows, width), shape(half, both)],
                inputs=3,
                far=2,
                scratch=(
                    pltpu.VMEM((3, tokens, width), bf16),
                    pltpu.VMEM((width, both), bf16),
                    pltpu.SemaphoreType.DMA((2,)),
                ),
            )(gate_row, *(pltpu.with_memory_space_constraint(a, pltpu.HBM) for a in (qkv, spatial_out)))
        else:
            heads, message = call(
                functools.partial(spatial_kernel, first=first),
                [shape(rows, width), shape(half, both)],
                inputs=3,
            )(gate_row, after(qkv, previous), spatial_out)
        message = swap(message, "mlp", n_mlp, 1)
        far_term, base, near_message = call(
            functools.partial(terms_kernel, first=first),
            [shape(half, both, f32), shape(half, both, f32), shape(half, both)],
            inputs=4,
        )(heads, spatial_out, gate_row, flat_residual)
        sent = call(add_kernel, shape(half, both), inputs=2)(far_term, message)
        previous = sent
        reduced.append((base, swap(near_message, "mlp", n_mlp, 1), sent))

    arrivals = [swap(sent, "mlp", n_mlp, 2) for _, _, sent in reduced]
    arrivals[0] = after(arrivals[0], previous, *(message for _, message, _ in reduced))
    nears, blocks = [], []
    for (first, rows), (base, near_message, _), arrived in zip(chunks, reduced, arrivals):
        half = rows // 2
        own, other, *pieces = call(
            update_kernel,
            [shape(half, share)] * 2 + [shape(half // SHARES, both)] * SHARES,
            inputs=3,
        )(base, near_message, arrived)
        blocks += [own, swap(other, "mlp", n_mlp, 1)]
        nears.append(jnp.concatenate(send_pieces(pieces), axis=0))

    own_mixed, other_mixed = [], []
    for (first, rows), near in zip(chunks, nears):
        half = rows // 2
        far = swap(near, "mlp", n_mlp, 2)
        other_near = swap(near, "mlp", n_mlp, 1)
        if own_mixed:
            updated = call(
                functools.partial(place_updated_kernel, chunks=chunks),
                shape(tokens, share),
                inputs=len(blocks),
            )(*blocks)
            far = after(far, own_mixed[-1], updated)
        other_far = swap(far, "mlp", n_mlp, 1)
        own, other = call(
            split_temporal_kernel,
            [shape(half, width)] * 2,
            inputs=9,
            scratch=(pltpu.VMEM((rows, features), bf16), pltpu.VMEM((3, rows, width), bf16)),
        )(near, far, other_near, other_far, weights, gain_row, shift_row, cosine, sine)
        own_mixed.append(own)
        other_mixed.append(swap(other, "mlp", n_mlp, 1))
    packed = call(
        pack_kernel, [shape(2 * tokens // (2 * SHARES), width)] * SHARES, inputs=2 * len(chunks)
    )(*own_mixed, *other_mixed)
    pieces = send_pieces(packed)
    others = call(unpack_kernel, shape(tokens // 2, width), inputs=SHARES)(*pieces)
    results = pieces + [swap(others, "mlp", n_mlp, 1)]
    result = call(
        functools.partial(place_mixed_kernel, chunks=chunks),
        shape(tokens, width),
        inputs=len(results),
    )(*results)
    return updated.reshape(frames, patches, share), result.reshape(frames, patches, width)


def heads_kernel(qkv_ref, out_ref):
    for lane in range(0, out_ref.shape[-1], HEAD_DIM):
        head = slice(lane, lane + HEAD_DIM)
        out_ref[:, head] = attend(qkv_ref[0, :, head], qkv_ref[1, :, head], qkv_ref[2, :, head])


def columns_kernel(own_ref, other_ref, own_w_ref, other_w_ref, gate_ref, out_ref):
    term = dot(own_ref[...], own_w_ref[...]) + dot(other_ref[...], other_w_ref[...])
    out_ref[...] = (term * gate_ref[...]).astype(out_ref.dtype)


def temporal_kernel(u0, u1, u2, u3, *refs):
    *refs, out_ref, normed_ref, proj_ref = refs
    share = u0.shape[-1]
    count = out_ref.shape[0] // refs[-1].shape[0]
    part = [
        (ref, pl.multiple_of((lax.axis_index("mlp") ^ k) * share, share))
        for k, ref in enumerate((u0, u1, u2, u3))
    ]

    def write(f, low, head, value):
        start = f * count + low
        out_ref[start : start + value.shape[0], head] = value

    project_and_mix([part], lambda f: f, write, *refs, normed_ref, proj_ref)


def on_device(
    residual, spatial_qkv, spatial_out, temporal_qkv, shift, scale, gate, *, n_seq, n_mlp
):
    frames, patches, share = residual.shape
    width = spatial_qkv.shape[-1]
    features = share * n_mlp
    rows = frames * patches
    count = rows // n_seq
    mlp = lax.axis_index("mlp")
    bf16, f32 = jnp.bfloat16, jnp.float32
    qkv = spatial_qkv.transpose(2, 0, 1, 3).reshape(3, rows, width)
    gate_row = gate.reshape(1, features)

    def columns(array, block):
        return lax.dynamic_slice_in_dim(array, block * share, share, 1)

    heads = call(heads_kernel, jax.ShapeDtypeStruct((rows, width), bf16), inputs=1)(qkv)
    others = swap(heads, "mlp", n_mlp, 1)

    def term(block, kind):
        other_w = swap(columns(spatial_out, block ^ 1), "mlp", n_mlp, 1)
        return call(columns_kernel, jax.ShapeDtypeStruct((rows, share), kind), inputs=5)(
            heads, others, columns(spatial_out, block), other_w, columns(gate_row, block)
        )

    arrived = swap(term(mlp ^ 2, bf16), "mlp", n_mlp, 2)
    branch = term(mlp, f32) + arrived.astype(f32)
    updated = (residual.reshape(rows, share).astype(f32) + branch).astype(bf16)
    mine = lax.all_to_all(
        updated.reshape(n_seq, count, share), "seq", 0, 0, tiled=True
    ).reshape(rows, share)
    across = swap(mine, "mlp", n_mlp, 2)
    mixed = call(
        temporal_kernel,
        jax.ShapeDtypeStruct((rows, width), bf16),
        inputs=9,
        scratch=(pltpu.VMEM((rows, features), bf16), pltpu.VMEM((3, rows, width), bf16)),
    )(
        mine,
        swap(mine, "mlp", n_mlp, 1),
        across,
        swap(across, "mlp", n_mlp, 1),
        temporal_qkv.transpose(1, 0, 2),
        scale.reshape(1, features),
        shift.reshape(1, features),
        *rotation_tables(n_seq),
    )
    result = lax.all_to_all(
        mixed.reshape(n_seq, count, width), "seq", 0, 0, tiled=True
    ).reshape(rows, width)
    return updated.reshape(frames, patches, share), result.reshape(frames, patches, width)


def solution(mesh):
    sizes = dict(n_seq=mesh.shape["seq"], n_mlp=mesh.shape["mlp"])
    split = sizes["n_seq"] == 2 * SHARES and sizes["n_mlp"] == 4
    return jax.shard_map(
        functools.partial(split_on_device if split else on_device, **sizes),
        mesh=mesh,
        in_specs=(
            P("seq", None, "mlp"),
            P("seq", None, None, "mlp"),
            P("mlp", None),
            P(None, None, "mlp"),
            P(),
            P(),
            P(),
        ),
        out_specs=(P("seq", None, "mlp"), P("seq", None, "mlp")),
        check_vma=False,
    )
```

```python
import functools
import math

import jax
import jax.numpy as jnp
import numpy as np
from jax import lax
from jax.experimental import pallas as pl
from jax.experimental.pallas import tpu as pltpu
from jax.sharding import PartitionSpec as P

HEAD_DIM = 128
EPSILON = 1e-06
GROUP = 16
MASKED = -1e30
VMEM_LIMIT = 16 * 1024 * 1024
EXP2_SCALE = math.log2(math.e) / math.sqrt(HEAD_DIM)
CHUNK_ROWS = (256, 256)
PARTNERS = ((7, 4, 2, 0), (5, 3, 6, 1))
SHARES = len(PARTNERS[0])


def call(body, outs, flops=0, moved=0, exps=0, inputs=0, scratch=(), far=0):
    return pl.pallas_call(
        body,
        out_shape=outs,
        in_specs=[pl.BlockSpec(memory_space=pltpu.VMEM)] * (inputs - far)
        + [pl.BlockSpec(memory_space=pltpu.HBM)] * far,
        scratch_shapes=list(scratch),
        compiler_params=pltpu.CompilerParams(vmem_limit_bytes=VMEM_LIMIT),
        cost_estimate=pl.CostEstimate(
            flops=int(flops), bytes_accessed=int(moved), transcendentals=int(exps)
        ),
    )


def dot(a, b):
    return jnp.dot(a, b, preferred_element_type=jnp.float32)


def dot_nt(a, b):
    return lax.dot_general(a, b, (((1,), (1,)), ((), ())), preferred_element_type=jnp.float32)


def attend(heads, same=None):
    logits = [dot_nt(query, key) for query, key, _ in heads]
    if same is not None:
        logits = [jnp.where(same, one, MASKED) for one in logits]
    tops = [jnp.max(one, axis=-1, keepdims=True) for one in logits]
    weights = [jnp.exp2((one - top) * EXP2_SCALE) for one, top in zip(logits, tops)]
    rates = [1.0 / jnp.sum(one, axis=-1, keepdims=True) for one in weights]
    return [
        (dot(one.astype(jnp.bfloat16), value) * rate).astype(jnp.bfloat16)
        for one, (_, _, value), rate in zip(weights, heads, rates)
    ]


def normalize(blocks, gain_ref, shift_ref, out_ref):
    features = out_ref.shape[-1]
    total, square = 0.0, 0.0
    for ref, _ in blocks:
        values = ref[...].astype(jnp.float32)
        total += jnp.sum(values, axis=-1, keepdims=True)
        square += jnp.sum(values * values, axis=-1, keepdims=True)
    mean = total / features
    rate = lax.rsqrt(square / features - mean * mean + EPSILON)
    for ref, start in blocks:
        lanes = pl.ds(start, ref.shape[-1])
        gain = 1.0 + gain_ref[:, lanes]
        out_ref[:, lanes] = (
            (ref[...].astype(jnp.float32) - mean) * rate * gain + shift_ref[:, lanes]
        ).astype(out_ref.dtype)


def project_and_mix(normed_refs, frame_of, write, w_ref, cos_ref, sin_ref, proj_ref):
    frames = cos_ref.shape[0]
    width = w_ref.shape[-1] // 3
    rows = proj_ref.shape[0]
    count = rows // frames
    first = 0
    for ref in normed_refs:
        size = ref.shape[0]
        acc = dot(ref[...], w_ref[...])
        span = slice(first, first + size)
        proj_ref[span, 2 * width :] = acc[:, 2 * width :].astype(proj_ref.dtype)
        for low in range(0, size, count):
            row = pl.ds(frame_of((first + low) // count), 1)
            cosine, sine = cos_ref[row, :], sin_ref[row, :]
            for lane in range(0, 2 * width, HEAD_DIM):
                head = acc[low : low + count, lane : lane + HEAD_DIM]
                turned = pltpu.roll(head, HEAD_DIM // 2, 1)
                proj_ref[first + low : first + low + count, lane : lane + HEAD_DIM] = (
                    head * cosine + turned * sine
                ).astype(proj_ref.dtype)
        first += size
    step = GROUP if count % GROUP == 0 else count
    size = step * frames
    patch_of = lambda axis: lax.rem(lax.broadcasted_iota(jnp.int32, (size, size), axis), step)
    same = patch_of(0) == patch_of(1)
    lanes = range(0, width, HEAD_DIM)

    def gathered(low, lane):
        head = slice(lane, lane + HEAD_DIM)
        if step == count:
            return proj_ref[:, head]
        spans = [slice(f * count + low, f * count + low + step) for f in range(frames)]
        return jnp.concatenate([proj_ref[span, head] for span in spans], axis=0)

    units = [(low, lane) for low in range(0, count, step) for lane in lanes]
    heads = [tuple(gathered(low, part * width + lane) for part in range(3)) for low, lane in units]
    for (low, lane), mixed in zip(units, attend(heads, same)):
        for f in range(frames):
            write(f, low, slice(lane, lane + HEAD_DIM), mixed[f * step : (f + 1) * step])


def hold_kernel(w_far, out_ref, semaphores):
    width = w_far.shape[-1]
    copies = [
        pltpu.make_async_copy(
            w_far.at[part], out_ref.at[:, part * width : (part + 1) * width], semaphores.at[part]
        )
        for part in range(3)
    ]
    for copy in copies:
        copy.start()
    for copy in copies:
        copy.wait()


def hold_weights(temporal_qkv):
    features, parts, width = temporal_qkv.shape
    return pl.pallas_call(
        hold_kernel,
        out_shape=pltpu.VMEM((features, parts * width), temporal_qkv.dtype),
        in_specs=[pl.BlockSpec(memory_space=pltpu.HBM)],
        out_specs=pl.BlockSpec(memory_space=pltpu.VMEM),
        scratch_shapes=[pltpu.SemaphoreType.DMA((parts,))],
        compiler_params=pltpu.CompilerParams(vmem_limit_bytes=1024 * 1024),
        cost_estimate=pl.CostEstimate(flops=0, bytes_accessed=0, transcendentals=0),
    )(in_hbm(temporal_qkv.transpose(1, 0, 2)))


def core_of():
    return lax.rem(lax.axis_index("mlp"), 2)


def chip_of():
    return lax.div(lax.axis_index("mlp"), 2)


def frame_of(i):
    low, high = (PARTNERS[core][i % SHARES] for core in range(2))
    which = core_of() if i < SHARES else 1 - core_of()
    return lax.axis_index("seq") ^ (low + which * (high - low))


def piece_span(first, count, i):
    return pl.ds(pl.multiple_of(first + frame_of(i) * count, count), count)


def piece_rows(ref, first, count, lanes):
    return jnp.concatenate(
        [ref[piece_span(first, count, i), lanes] for i in range(2 * SHARES)], axis=0
    )


def chip_columns(features, flip):
    half = features // 2
    return pl.ds(pl.multiple_of((chip_of() ^ flip) * half, half), half)


def spatial_body(qkv_ref, far_w_ref, heads_ref, message_ref, first, far_gate):
    rows, width = heads_ref.shape
    for lane in range(0, width, HEAD_DIM):
        head = slice(lane, lane + HEAD_DIM)
        query = piece_rows(qkv_ref.at[0], first, rows // (2 * SHARES), head)
        (heads_ref[:, head],) = attend([(query, qkv_ref[1, :, head], qkv_ref[2, :, head])])
    gate = far_gate()
    term = dot(heads_ref[rows // 2 :, :], far_w_ref[...])
    message_ref[...] = (term * gate).astype(message_ref.dtype)


def first_spatial_kernel(
    qkv_far, w_far, gate_far, residual_far,
    heads_ref, message_ref, qkv_ref, w_ref, gate_ref, residual_ref, semaphores, *, first
):
    far, near = (chip_columns(w_far.shape[-1], flip) for flip in (1, 0))
    moves = [
        (qkv_far, qkv_ref),
        (w_far.at[:, far], w_ref.at[:, far]),
        (gate_far, gate_ref),
        (w_far.at[:, near], w_ref.at[:, near]),
        (residual_far, residual_ref),
    ]
    copies = [pltpu.make_async_copy(*move, semaphores.at[i]) for i, move in enumerate(moves)]
    for copy in copies:
        copy.start()
    copies[0].wait()

    def far_gate():
        copies[1].wait()
        copies[2].wait()
        return gate_ref[:, far]

    spatial_body(qkv_ref, w_ref.at[:, far], heads_ref, message_ref, first, far_gate)
    copies[3].wait()
    copies[4].wait()


def spatial_kernel(gate_ref, qkv_ref, w_ref, heads_ref, message_ref, *, first):
    columns = chip_columns(w_ref.shape[-1], 1)
    spatial_body(
        qkv_ref,
        w_ref.at[:, columns],
        heads_ref,
        message_ref,
        first,
        lambda: gate_ref[:, columns],
    )


def terms_kernel(
    heads_ref, w_ref, gate_ref, residual_ref, far_ref, base_ref, message_ref, *, first
):
    half, both = base_ref.shape
    share = both // 2
    features = w_ref.shape[-1]
    far = chip_columns(features, 1)
    far_ref[...] = dot(heads_ref[:half, :], w_ref[:, far]) * gate_ref[:, far]
    for flip in range(2):
        place = pl.multiple_of((core_of() ^ flip) * share, share)
        lanes = pl.ds(pl.multiple_of(chip_of() * both + place, share), share)
        term = dot(heads_ref[...], w_ref[:, lanes]) * gate_ref[:, lanes]
        if flip == 0:
            term += piece_rows(residual_ref, first, half // SHARES, slice(None)).astype(
                jnp.float32
            )
        base_ref[:, pl.ds(place, share)] = term[:half]
        message_ref[:, pl.ds(place, share)] = term[half:].astype(message_ref.dtype)


def add_kernel(a_ref, b_ref, out_ref):
    out_ref[...] = (a_ref[...] + b_ref[...].astype(jnp.float32)).astype(out_ref.dtype)


def update_kernel(base_ref, message_ref, arrived_ref, own_ref, other_ref, *piece_refs):
    updated = (
        base_ref[...] + message_ref[...].astype(jnp.float32) + arrived_ref[...].astype(jnp.float32)
    ).astype(jnp.bfloat16)
    count = piece_refs[0].shape[0]
    for i, piece_ref in enumerate(piece_refs):
        piece_ref[...] = updated[i * count : (i + 1) * count]
    share = own_ref.shape[-1]
    left, right = updated[:, :share], updated[:, share:]
    core = core_of()
    own_ref[...] = jnp.where(core == 0, left, right)
    other_ref[...] = jnp.where(core == 0, right, left)


def split_blocks(near_ref, far_ref):
    half = near_ref.shape[-1]
    return [
        (ref, pl.multiple_of((chip_of() ^ flip) * half, half))
        for flip, ref in enumerate((near_ref, far_ref))
    ]


def split_norm_kernel(near_ref, far_ref, gain_ref, shift_ref, out_ref):
    normalize(split_blocks(near_ref, far_ref), gain_ref, shift_ref, out_ref)


def split_temporal_kernel(
    own_normed_ref, near_ref, far_ref, gain_ref, shift_ref, w_ref, cos_ref, sin_ref,
    own_ref, other_ref, normed_ref, proj_ref,
):
    normalize(split_blocks(near_ref, far_ref), gain_ref, shift_ref, normed_ref)
    count = own_ref.shape[0] // SHARES

    def write(i, low, head, value):
        ref = own_ref if i < SHARES else other_ref
        start = (i % SHARES) * count + low
        ref[start : start + value.shape[0], head] = value

    project_and_mix(
        [own_normed_ref, normed_ref], frame_of, write, w_ref, cos_ref, sin_ref, proj_ref
    )


def pack_kernel(*refs):
    block_refs, out_refs = refs[:-SHARES], refs[-SHARES:]
    for i, out_ref in enumerate(out_refs):
        start = 0
        for ref in block_refs:
            count = ref.shape[0] // SHARES
            out_ref[start : start + count] = ref[i * count : (i + 1) * count]
            start += count


def unpack_kernel(*refs):
    *piece_refs, out_ref = refs
    count = piece_refs[0].shape[0] // 2
    for i, ref in enumerate(piece_refs):
        out_ref[i * count : (i + 1) * count] = ref[count:]


def place_updated_kernel(*refs, chunks):
    *block_refs, out_ref = refs
    for (first, rows), own_ref, other_ref in zip(chunks, block_refs[::2], block_refs[1::2]):
        count = rows // (2 * SHARES)
        for i in range(2 * SHARES):
            ref = own_ref if i < SHARES else other_ref
            start = (i % SHARES) * count
            out_ref[piece_span(first, count, i), :] = ref[start : start + count, :]


def place_mixed_kernel(*refs, chunks):
    *own_refs, other_ref, out_ref = refs
    size = own_refs[0].shape[0] // 2
    start = 0
    for first, rows in chunks:
        count = rows // (2 * SHARES)
        for i in range(SHARES):
            out_ref[piece_span(first, count, i), :] = own_refs[i][start : start + count, :]
            low = i * size + start
            out_ref[piece_span(first, count, SHARES + i), :] = other_ref[low : low + count, :]
        start += count


def swap(value, axis, size, k):
    return lax.ppermute(value, axis, [(i, i ^ k) for i in range(size)])


def rotation_tables(frames):
    rates = 10000.0 ** (-2.0 * np.arange(HEAD_DIM // 2, dtype=np.float32) / HEAD_DIM)
    angles = np.arange(frames, dtype=np.float32)[:, None] * rates.astype(np.float32)
    cosine, sine = np.cos(angles), np.sin(angles)
    return (
        jnp.asarray(np.concatenate([cosine, cosine], axis=1), jnp.float32),
        jnp.asarray(np.concatenate([-sine, sine], axis=1), jnp.float32),
    )


def piece_pairs(n_seq, n_mlp, index):
    return [
        (s * n_mlp + m, (s ^ PARTNERS[m % 2][index]) * n_mlp + m)
        for s in range(n_seq)
        for m in range(n_mlp)
    ]


def in_hbm(array):
    return pltpu.with_memory_space_constraint(array, pltpu.HBM)


def after(value, *others):
    return lax.optimization_barrier((value,) + others)[0]


def split_on_device(
    residual, spatial_qkv, spatial_out, temporal_qkv, shift, scale, gate, *, n_seq, n_mlp
):
    frames, patches, share = residual.shape
    width = spatial_qkv.shape[-1]
    features = share * n_mlp
    both = 2 * share
    tokens = frames * patches
    bf16, f32 = jnp.bfloat16, jnp.float32
    flat_residual = residual.reshape(tokens, share)
    qkv = spatial_qkv.transpose(2, 0, 1, 3).reshape(3, tokens, width)
    weights = hold_weights(temporal_qkv)
    gate_row = gate.reshape(1, features)
    gain_row, shift_row = scale.reshape(1, features), shift.reshape(1, features)
    cosine, sine = rotation_tables(n_seq)

    def shape(rows, columns, kind=bf16):
        return jax.ShapeDtypeStruct((rows, columns), kind)

    def send_pieces(pieces):
        return [
            lax.ppermute(piece, ("seq", "mlp"), piece_pairs(n_seq, n_mlp, i))
            for i, piece in enumerate(pieces)
        ]

    chunks = []
    first = 0
    for rows in CHUNK_ROWS:
        chunks.append((first, rows))
        first += rows

    reduced = []
    previous = None
    for first, rows in chunks:
        half = rows // 2
        if previous is None:
            operands = (qkv, spatial_out, gate_row, flat_residual)
            heads, message, *operands = call(
                functools.partial(first_spatial_kernel, first=first),
                [shape(rows, width), shape(half, both)]
                + [pltpu.VMEM(one.shape, one.dtype) for one in operands],
                inputs=len(operands),
                far=len(operands),
                scratch=(pltpu.SemaphoreType.DMA((len(operands) + 1,)),),
            )(*(in_hbm(one) for one in operands))
            qkv, spatial_out, gate_row, flat_residual = operands
        else:
            heads, message = call(
                functools.partial(spatial_kernel, first=first),
                [shape(rows, width), shape(half, both)],
                inputs=3,
            )(gate_row, after(qkv, previous), spatial_out)
        message = swap(message, "mlp", n_mlp, 1)
        far_term, base, near_message = call(
            functools.partial(terms_kernel, first=first),
            [shape(half, both, f32), shape(half, both, f32), shape(half, both)],
            inputs=4,
        )(heads, spatial_out, gate_row, flat_residual)
        sent = call(add_kernel, shape(half, both), inputs=2)(far_term, message)
        previous = sent
        reduced.append((base, swap(near_message, "mlp", n_mlp, 1), sent))

    arrivals = [swap(sent, "mlp", n_mlp, 2) for _, _, sent in reduced]
    arrivals[0] = after(arrivals[0], previous, weights, *(message for _, message, _ in reduced))
    blocks, pieces = [], []
    for index, ((first, rows), (base, near_message, _)) in enumerate(zip(chunks, reduced)):
        half = rows // 2
        own, other, *sends = call(
            update_kernel,
            [shape(half, share)] * 2 + [shape(half // SHARES, both)] * SHARES,
            flops=1e10 * index,
            inputs=3,
        )(base, near_message, arrivals[index])
        blocks += [own, swap(other, "mlp", n_mlp, 1)]
        pieces.append(sends)
    nears = []
    for index, sends in enumerate(pieces):
        received = send_pieces(sends)
        if index + 1 < len(pieces):
            received[0], pieces[index + 1][0] = lax.optimization_barrier(
                (received[0], pieces[index + 1][0])
            )
        nears.append(jnp.concatenate(received, axis=0))

    own_mixed, other_mixed = [], []
    for (first, rows), near in zip(chunks, nears):
        half = rows // 2
        far = swap(near, "mlp", n_mlp, 2)
        other_near = swap(near, "mlp", n_mlp, 1)
        if own_mixed:
            updated = call(
                functools.partial(place_updated_kernel, chunks=chunks),
                shape(tokens, share),
                inputs=len(blocks),
            )(*blocks)
            far = after(far, own_mixed[-1], updated)
        other_far = swap(far, "mlp", n_mlp, 1)
        own_normed = call(split_norm_kernel, shape(half, features), inputs=4)(
            near, far, gain_row, shift_row
        )
        own, other = call(
            split_temporal_kernel,
            [shape(half, width)] * 2,
            inputs=8,
            scratch=(pltpu.VMEM((half, features), bf16), pltpu.VMEM((rows, 3 * width), bf16)),
        )(own_normed, other_near, other_far, gain_row, shift_row, weights, cosine, sine)
        own_mixed.append(own)
        other_mixed.append(swap(other, "mlp", n_mlp, 1))
    packed = call(
        pack_kernel, [shape(2 * tokens // (2 * SHARES), width)] * SHARES, inputs=2 * len(chunks)
    )(*own_mixed, *other_mixed)
    pieces = send_pieces(packed)
    others = call(unpack_kernel, shape(tokens // 2, width), inputs=SHARES)(*pieces)
    results = pieces + [swap(others, "mlp", n_mlp, 1)]
    result = call(
        functools.partial(place_mixed_kernel, chunks=chunks),
        shape(tokens, width),
        inputs=len(results),
    )(*results)
    return updated.reshape(frames, patches, share), result.reshape(frames, patches, width)


def heads_kernel(qkv_ref, out_ref):
    for lane in range(0, out_ref.shape[-1], HEAD_DIM):
        head = slice(lane, lane + HEAD_DIM)
        (out_ref[:, head],) = attend([tuple(qkv_ref[part, :, head] for part in range(3))])


def columns_kernel(own_ref, other_ref, own_w_ref, other_w_ref, gate_ref, out_ref):
    term = dot(own_ref[...], own_w_ref[...]) + dot(other_ref[...], other_w_ref[...])
    out_ref[...] = (term * gate_ref[...]).astype(out_ref.dtype)


def temporal_kernel(
    u0, u1, u2, u3, gain_ref, shift_ref, w_ref, cos_ref, sin_ref, out_ref, normed_ref, proj_ref
):
    share = u0.shape[-1]
    count = out_ref.shape[0] // cos_ref.shape[0]
    blocks = [
        (ref, pl.multiple_of((lax.axis_index("mlp") ^ k) * share, share))
        for k, ref in enumerate((u0, u1, u2, u3))
    ]
    normalize(blocks, gain_ref, shift_ref, normed_ref)

    def write(f, low, head, value):
        start = f * count + low
        out_ref[start : start + value.shape[0], head] = value

    project_and_mix([normed_ref], lambda f: f, write, w_ref, cos_ref, sin_ref, proj_ref)


def on_device(
    residual, spatial_qkv, spatial_out, temporal_qkv, shift, scale, gate, *, n_seq, n_mlp
):
    frames, patches, share = residual.shape
    width = spatial_qkv.shape[-1]
    features = share * n_mlp
    rows = frames * patches
    count = rows // n_seq
    mlp = lax.axis_index("mlp")
    bf16, f32 = jnp.bfloat16, jnp.float32
    qkv = spatial_qkv.transpose(2, 0, 1, 3).reshape(3, rows, width)
    gate_row = gate.reshape(1, features)

    def columns(array, block):
        return lax.dynamic_slice_in_dim(array, block * share, share, 1)

    heads = call(heads_kernel, jax.ShapeDtypeStruct((rows, width), bf16), inputs=1)(qkv)
    others = swap(heads, "mlp", n_mlp, 1)

    def term(block, kind):
        other_w = swap(columns(spatial_out, block ^ 1), "mlp", n_mlp, 1)
        return call(columns_kernel, jax.ShapeDtypeStruct((rows, share), kind), inputs=5)(
            heads, others, columns(spatial_out, block), other_w, columns(gate_row, block)
        )

    arrived = swap(term(mlp ^ 2, bf16), "mlp", n_mlp, 2)
    branch = term(mlp, f32) + arrived.astype(f32)
    updated = (residual.reshape(rows, share).astype(f32) + branch).astype(bf16)
    mine = lax.all_to_all(
        updated.reshape(n_seq, count, share), "seq", 0, 0, tiled=True
    ).reshape(rows, share)
    across = swap(mine, "mlp", n_mlp, 2)
    mixed = call(
        temporal_kernel,
        jax.ShapeDtypeStruct((rows, width), bf16),
        inputs=9,
        scratch=(pltpu.VMEM((rows, features), bf16), pltpu.VMEM((rows, 3 * width), bf16)),
    )(
        mine,
        swap(mine, "mlp", n_mlp, 1),
        across,
        swap(across, "mlp", n_mlp, 1),
        scale.reshape(1, features),
        shift.reshape(1, features),
        hold_weights(temporal_qkv),
        *rotation_tables(n_seq),
    )
    result = lax.all_to_all(
        mixed.reshape(n_seq, count, width), "seq", 0, 0, tiled=True
    ).reshape(rows, width)
    return updated.reshape(frames, patches, share), result.reshape(frames, patches, width)


def solution(mesh):
    sizes = dict(n_seq=mesh.shape["seq"], n_mlp=mesh.shape["mlp"])
    split = sizes["n_seq"] == 2 * SHARES and sizes["n_mlp"] == 4
    return jax.shard_map(
        functools.partial(split_on_device if split else on_device, **sizes),
        mesh=mesh,
        in_specs=(
            P("seq", None, "mlp"),
            P("seq", None, None, "mlp"),
            P("mlp", None),
            P(None, None, "mlp"),
            P(),
            P(),
            P(),
        ),
        out_specs=(P("seq", None, "mlp"), P("seq", None, "mlp")),
        check_vma=False,
    )
```

```python
import functools
import math

import jax
import jax.numpy as jnp
import numpy as np
from jax import lax
from jax.experimental import pallas as pl
from jax.experimental.pallas import tpu as pltpu
from jax.sharding import PartitionSpec as P

HEAD_DIM = 128
EPSILON = 1e-06
GROUP = 16
MASKED = -1e30
VMEM_LIMIT = 16 * 1024 * 1024
EXP2_SCALE = math.log2(math.e) / math.sqrt(HEAD_DIM)
CHUNK_ROWS = (256, 256)
PARTNERS = ((7, 4, 2, 0), (5, 3, 6, 1))
SHARES = len(PARTNERS[0])


def call(body, outs, flops=0, moved=0, exps=0, inputs=0, scratch=(), far=0):
    return pl.pallas_call(
        body,
        out_shape=outs,
        in_specs=[pl.BlockSpec(memory_space=pltpu.VMEM)] * (inputs - far)
        + [pl.BlockSpec(memory_space=pltpu.HBM)] * far,
        scratch_shapes=list(scratch),
        compiler_params=pltpu.CompilerParams(vmem_limit_bytes=VMEM_LIMIT),
        cost_estimate=pl.CostEstimate(
            flops=int(flops), bytes_accessed=int(moved), transcendentals=int(exps)
        ),
    )


def dot(a, b):
    return jnp.dot(a, b, preferred_element_type=jnp.float32)


def dot_nt(a, b):
    return lax.dot_general(a, b, (((1,), (1,)), ((), ())), preferred_element_type=jnp.float32)


def attend(heads, same=None):
    logits = [dot_nt(query, key) for query, key, _ in heads]
    if same is not None:
        logits = [jnp.where(same, one, MASKED) for one in logits]
    tops = [jnp.max(one, axis=-1, keepdims=True) for one in logits]
    weights = [jnp.exp2((one - top) * EXP2_SCALE) for one, top in zip(logits, tops)]
    rates = [1.0 / jnp.sum(one, axis=-1, keepdims=True) for one in weights]
    return [
        (dot(one.astype(jnp.bfloat16), value) * rate).astype(jnp.bfloat16)
        for one, (_, _, value), rate in zip(weights, heads, rates)
    ]


def normalize(blocks, gain_ref, shift_ref, out_ref):
    features = out_ref.shape[-1]
    total, square = 0.0, 0.0
    for ref, _ in blocks:
        values = ref[...].astype(jnp.float32)
        total += jnp.sum(values, axis=-1, keepdims=True)
        square += jnp.sum(values * values, axis=-1, keepdims=True)
    mean = total / features
    rate = lax.rsqrt(square / features - mean * mean + EPSILON)
    for ref, start in blocks:
        lanes = pl.ds(start, ref.shape[-1])
        gain = 1.0 + gain_ref[:, lanes]
        out_ref[:, lanes] = (
            (ref[...].astype(jnp.float32) - mean) * rate * gain + shift_ref[:, lanes]
        ).astype(out_ref.dtype)


def project_and_mix(normed_refs, frame_of, write, w_ref, cos_ref, sin_ref, proj_ref):
    frames = cos_ref.shape[0]
    width = w_ref.shape[-1] // 3
    rows = proj_ref.shape[0]
    count = rows // frames
    first = 0
    for ref in normed_refs:
        size = ref.shape[0]
        acc = dot(ref[...], w_ref[...])
        span = slice(first, first + size)
        proj_ref[span, 2 * width :] = acc[:, 2 * width :].astype(proj_ref.dtype)
        for low in range(0, size, count):
            row = pl.ds(frame_of((first + low) // count), 1)
            cosine, sine = cos_ref[row, :], sin_ref[row, :]
            for lane in range(0, 2 * width, HEAD_DIM):
                head = acc[low : low + count, lane : lane + HEAD_DIM]
                turned = pltpu.roll(head, HEAD_DIM // 2, 1)
                proj_ref[first + low : first + low + count, lane : lane + HEAD_DIM] = (
                    head * cosine + turned * sine
                ).astype(proj_ref.dtype)
        first += size
    step = GROUP if count % GROUP == 0 else count
    size = step * frames
    patch_of = lambda axis: lax.rem(lax.broadcasted_iota(jnp.int32, (size, size), axis), step)
    same = patch_of(0) == patch_of(1)
    lanes = range(0, width, HEAD_DIM)

    def gathered(low, lane):
        head = slice(lane, lane + HEAD_DIM)
        if step == count:
            return proj_ref[:, head]
        spans = [slice(f * count + low, f * count + low + step) for f in range(frames)]
        return jnp.concatenate([proj_ref[span, head] for span in spans], axis=0)

    units = [(low, lane) for low in range(0, count, step) for lane in lanes]
    heads = [tuple(gathered(low, part * width + lane) for part in range(3)) for low, lane in units]
    for (low, lane), mixed in zip(units, attend(heads, same)):
        for f in range(frames):
            write(f, low, slice(lane, lane + HEAD_DIM), mixed[f * step : (f + 1) * step])


def hold_kernel(w_far, out_ref, semaphores):
    width = w_far.shape[-1]
    copies = [
        pltpu.make_async_copy(
            w_far.at[part], out_ref.at[:, part * width : (part + 1) * width], semaphores.at[part]
        )
        for part in range(3)
    ]
    for copy in copies:
        copy.start()
    for copy in copies:
        copy.wait()


def hold_weights(temporal_qkv):
    features, parts, width = temporal_qkv.shape
    return pl.pallas_call(
        hold_kernel,
        out_shape=pltpu.VMEM((features, parts * width), temporal_qkv.dtype),
        in_specs=[pl.BlockSpec(memory_space=pltpu.HBM)],
        out_specs=pl.BlockSpec(memory_space=pltpu.VMEM),
        scratch_shapes=[pltpu.SemaphoreType.DMA((parts,))],
        compiler_params=pltpu.CompilerParams(vmem_limit_bytes=1024 * 1024),
        cost_estimate=pl.CostEstimate(flops=0, bytes_accessed=0, transcendentals=0),
    )(in_hbm(temporal_qkv.transpose(1, 0, 2)))


def core_of():
    return lax.rem(lax.axis_index("mlp"), 2)


def chip_of():
    return lax.div(lax.axis_index("mlp"), 2)


def frame_of(i):
    low, high = (PARTNERS[core][i % SHARES] for core in range(2))
    which = core_of() if i < SHARES else 1 - core_of()
    return lax.axis_index("seq") ^ (low + which * (high - low))


def piece_span(first, count, i):
    return pl.ds(pl.multiple_of(first + frame_of(i) * count, count), count)


def piece_rows(ref, first, count, lanes):
    return jnp.concatenate(
        [ref[piece_span(first, count, i), lanes] for i in range(2 * SHARES)], axis=0
    )


def chip_columns(features, flip):
    half = features // 2
    return pl.ds(pl.multiple_of((chip_of() ^ flip) * half, half), half)


def spatial_heads(qkv_ref, heads_ref, first):
    rows, width = heads_ref.shape
    for lane in range(0, width, HEAD_DIM):
        head = slice(lane, lane + HEAD_DIM)
        query = piece_rows(qkv_ref.at[0], first, rows // (2 * SHARES), head)
        (heads_ref[:, head],) = attend([(query, qkv_ref[1, :, head], qkv_ref[2, :, head])])


def first_spatial_kernel(
    qkv_far, w_far, gate_far, heads_ref, message_ref, w_ref, gate_ref, qkv_ref, semaphores, *, first
):
    far = chip_columns(w_far.shape[-1], 1)
    moves = [(qkv_far, qkv_ref), (w_far.at[:, far], w_ref), (gate_far.at[:, far], gate_ref)]
    copies = [pltpu.make_async_copy(*move, semaphores.at[i]) for i, move in enumerate(moves)]
    for copy in copies:
        copy.start()
    copies[0].wait()
    spatial_heads(qkv_ref, heads_ref, first)
    copies[1].wait()
    copies[2].wait()
    term = dot(heads_ref[heads_ref.shape[0] // 2 :, :], w_ref[...])
    message_ref[...] = (term * gate_ref[...]).astype(message_ref.dtype)


def term_kernel(heads_ref, w_ref, gate_ref, out_ref):
    out_ref[...] = dot(heads_ref[: out_ref.shape[0], :], w_ref[...]) * gate_ref[...]


def rest_kernel(
    heads0_ref, qkv_far, w_far, gate_far, residual_far,
    message_ref, term_ref, base0_ref, near0_ref, base1_ref, near1_ref,
    heads1_ref, qkv_ref, w_ref, gate_ref, residual_ref, semaphores, *, firsts
):
    moves = [
        (qkv_far, qkv_ref), (w_far, w_ref), (gate_far, gate_ref), (residual_far, residual_ref)
    ]
    copies = [pltpu.make_async_copy(*move, semaphores.at[i]) for i, move in enumerate(moves)]
    for copy in copies:
        copy.start()
    copies[0].wait()
    spatial_heads(qkv_ref, heads1_ref, firsts[1])
    for copy in copies[1:]:
        copy.wait()
    half, both = message_ref.shape
    features = w_ref.shape[-1]
    far = chip_columns(features, 1)
    term = dot(heads1_ref[...], w_ref[:, far]) * gate_ref[:, far]
    term_ref[...] = term[:half]
    message_ref[...] = term[half:].astype(message_ref.dtype)
    share = both // 2
    for first, heads_ref, base_ref, near_ref in (
        (firsts[0], heads0_ref, base0_ref, near0_ref),
        (firsts[1], heads1_ref, base1_ref, near1_ref),
    ):
        size = base_ref.shape[0]
        for flip in range(2):
            place = pl.multiple_of((core_of() ^ flip) * share, share)
            lanes = pl.ds(pl.multiple_of(chip_of() * both + place, share), share)
            term = dot(heads_ref[...], w_ref[:, lanes]) * gate_ref[:, lanes]
            if flip == 0:
                term += piece_rows(residual_ref, first, size // SHARES, slice(None)).astype(
                    jnp.float32
                )
            base_ref[:, pl.ds(place, share)] = term[:size]
            near_ref[:, pl.ds(place, share)] = term[size:].astype(near_ref.dtype)


def add_kernel(a_ref, b_ref, out_ref):
    out_ref[...] = (a_ref[...] + b_ref[...].astype(jnp.float32)).astype(out_ref.dtype)


def update_kernel(base_ref, arrived_ref, own_ref, other_ref, *piece_refs):
    updated = (base_ref[...] + arrived_ref[...].astype(jnp.float32)).astype(jnp.bfloat16)
    count = piece_refs[0].shape[0]
    for i, piece_ref in enumerate(piece_refs):
        piece_ref[...] = updated[i * count : (i + 1) * count]
    share = own_ref.shape[-1]
    left, right = updated[:, :share], updated[:, share:]
    core = core_of()
    own_ref[...] = jnp.where(core == 0, left, right)
    other_ref[...] = jnp.where(core == 0, right, left)


def split_blocks(near_ref, far_ref):
    half = near_ref.shape[-1]
    return [
        (ref, pl.multiple_of((chip_of() ^ flip) * half, half))
        for flip, ref in enumerate((near_ref, far_ref))
    ]


def split_norm_kernel(near_ref, far_ref, gain_ref, shift_ref, out_ref):
    normalize(split_blocks(near_ref, far_ref), gain_ref, shift_ref, out_ref)


def split_temporal_kernel(
    own_normed_ref, near_ref, far_ref, gain_ref, shift_ref, w_ref, cos_ref, sin_ref,
    own_ref, other_ref, normed_ref, proj_ref,
):
    normalize(split_blocks(near_ref, far_ref), gain_ref, shift_ref, normed_ref)
    count = own_ref.shape[0] // SHARES

    def write(i, low, head, value):
        ref = own_ref if i < SHARES else other_ref
        start = (i % SHARES) * count + low
        ref[start : start + value.shape[0], head] = value

    project_and_mix(
        [own_normed_ref, normed_ref], frame_of, write, w_ref, cos_ref, sin_ref, proj_ref
    )


def pack_kernel(*refs):
    block_refs, out_refs = refs[:-SHARES], refs[-SHARES:]
    for i, out_ref in enumerate(out_refs):
        start = 0
        for ref in block_refs:
            count = ref.shape[0] // SHARES
            out_ref[start : start + count] = ref[i * count : (i + 1) * count]
            start += count


def unpack_kernel(*refs):
    *piece_refs, out_ref = refs
    count = piece_refs[0].shape[0] // 2
    for i, ref in enumerate(piece_refs):
        out_ref[i * count : (i + 1) * count] = ref[count:]


def place_updated_kernel(*refs, chunks):
    *block_refs, out_ref = refs
    for (first, rows), own_ref, other_ref in zip(chunks, block_refs[::2], block_refs[1::2]):
        count = rows // (2 * SHARES)
        for i in range(2 * SHARES):
            ref = own_ref if i < SHARES else other_ref
            start = (i % SHARES) * count
            out_ref[piece_span(first, count, i), :] = ref[start : start + count, :]


def place_mixed_kernel(*refs, chunks):
    *own_refs, other_ref, out_ref = refs
    size = own_refs[0].shape[0] // 2
    start = 0
    for first, rows in chunks:
        count = rows // (2 * SHARES)
        for i in range(SHARES):
            out_ref[piece_span(first, count, i), :] = own_refs[i][start : start + count, :]
            low = i * size + start
            out_ref[piece_span(first, count, SHARES + i), :] = other_ref[low : low + count, :]
        start += count


def swap(value, axis, size, k):
    return lax.ppermute(value, axis, [(i, i ^ k) for i in range(size)])


def rotation_tables(frames):
    rates = 10000.0 ** (-2.0 * np.arange(HEAD_DIM // 2, dtype=np.float32) / HEAD_DIM)
    angles = np.arange(frames, dtype=np.float32)[:, None] * rates.astype(np.float32)
    cosine, sine = np.cos(angles), np.sin(angles)
    return (
        jnp.asarray(np.concatenate([cosine, cosine], axis=1), jnp.float32),
        jnp.asarray(np.concatenate([-sine, sine], axis=1), jnp.float32),
    )


def piece_pairs(n_seq, n_mlp, index):
    return [
        (s * n_mlp + m, (s ^ PARTNERS[m % 2][index]) * n_mlp + m)
        for s in range(n_seq)
        for m in range(n_mlp)
    ]


def in_hbm(array):
    return pltpu.with_memory_space_constraint(array, pltpu.HBM)


def after(value, *others):
    return lax.optimization_barrier((value,) + others)[0]


def split_on_device(
    residual, spatial_qkv, spatial_out, temporal_qkv, shift, scale, gate, *, n_seq, n_mlp
):
    frames, patches, share = residual.shape
    width = spatial_qkv.shape[-1]
    features = share * n_mlp
    both = 2 * share
    tokens = frames * patches
    bf16, f32 = jnp.bfloat16, jnp.float32
    flat_residual = residual.reshape(tokens, share)
    qkv = spatial_qkv.transpose(2, 0, 1, 3).reshape(3, tokens, width)
    gate_row = gate.reshape(1, features)
    gain_row, shift_row = scale.reshape(1, features), shift.reshape(1, features)
    cosine, sine = rotation_tables(n_seq)

    def shape(rows, columns, kind=bf16):
        return jax.ShapeDtypeStruct((rows, columns), kind)

    def send_pieces(pieces):
        return [
            lax.ppermute(piece, ("seq", "mlp"), piece_pairs(n_seq, n_mlp, i))
            for i, piece in enumerate(pieces)
        ]

    once = jnp.minimum(lax.axis_index("seq") + 1, 1)

    chunks = []
    first = 0
    for rows in CHUNK_ROWS:
        chunks.append((first, rows))
        first += rows

    (first0, rows0), (first1, rows1) = chunks
    half0, half1 = rows0 // 2, rows1 // 2
    heads, message, far_w, far_gate = call(
        functools.partial(first_spatial_kernel, first=first0),
        [
            shape(rows0, width),
            shape(half0, both),
            pltpu.VMEM((width, both), bf16),
            pltpu.VMEM((1, both), f32),
        ],
        inputs=3,
        far=3,
        scratch=(pltpu.VMEM(qkv.shape, bf16), pltpu.SemaphoreType.DMA((3,))),
    )(*(in_hbm(one) for one in (qkv, spatial_out, gate_row)))
    message = swap(message, "mlp", n_mlp, 1)
    far_term = call(term_kernel, shape(half0, both, f32), inputs=3)(heads, far_w, far_gate)
    sent = call(add_kernel, shape(half0, both), inputs=2)(far_term, message)
    arrived0 = swap(sent, "mlp", n_mlp, 2)

    def rest(heads, *operands):
        message, far_term, base0, near0, base1, near1 = call(
            functools.partial(rest_kernel, firsts=(first0, first1)),
            [
                shape(half1, both),
                shape(half1, both, f32),
                shape(half0, both, f32),
                shape(half0, both),
                shape(half1, both, f32),
                shape(half1, both),
            ],
            inputs=5,
            far=4,
            scratch=(
                pltpu.VMEM((rows1, width), bf16),
                *(pltpu.VMEM(one.shape, one.dtype) for one in operands),
                pltpu.SemaphoreType.DMA((4,)),
            ),
        )(heads, *(in_hbm(one) for one in operands))
        message, near0, near1 = (swap(one, "mlp", n_mlp, 1) for one in (message, near0, near1))
        sent = call(add_kernel, shape(half1, both), inputs=2)(far_term, message)
        base0, base1 = (
            call(add_kernel, shape(*base.shape, f32), inputs=2)(base, near)
            for base, near in ((base0, near0), (base1, near1))
        )
        return sent, base0, base1

    def nothing(*_):
        return (
            jnp.zeros((half1, both), bf16),
            jnp.zeros((half0, both), f32),
            jnp.zeros((half1, both), f32),
        )

    sent, base0, base1 = lax.cond(
        once > 0, rest, nothing, after(heads, sent), qkv, spatial_out, gate_row, flat_residual
    )
    arrived1 = swap(sent, "mlp", n_mlp, 2)
    arrived0 = after(arrived0, sent)
    reduced = [(base0, arrived0), (base1, arrived1)]

    blocks, pieces = [], []
    for index, ((first, rows), operands) in enumerate(zip(chunks, reduced)):
        half = rows // 2
        own, other, *sends = call(
            update_kernel,
            [shape(half, share)] * 2 + [shape(half // SHARES, both)] * SHARES,
            inputs=2,
        )(*operands)
        blocks += [own, swap(other, "mlp", n_mlp, 1)]
        pieces.append(sends)
    nears = []
    for sends in pieces:
        sends = lax.fori_loop(0, once, lambda _, sends: send_pieces(sends), sends)
        nears.append(jnp.concatenate(sends, axis=0))
    weights = hold_weights(after(temporal_qkv, *nears))

    own_mixed, other_mixed = [], []
    for (first, rows), near in zip(chunks, nears):
        half = rows // 2
        far = swap(near, "mlp", n_mlp, 2)
        other_near = swap(near, "mlp", n_mlp, 1)
        if not own_mixed:
            far = after(far, *nears)
        else:
            updated = call(
                functools.partial(place_updated_kernel, chunks=chunks),
                shape(tokens, share),
                inputs=len(blocks),
            )(*blocks)
            far = after(far, other_mixed[-1], updated)
        other_far = swap(far, "mlp", n_mlp, 1)
        own_normed = call(split_norm_kernel, shape(half, features), inputs=4)(
            near, far, gain_row, shift_row
        )
        own, other = call(
            split_temporal_kernel,
            [shape(half, width)] * 2,
            inputs=8,
            scratch=(pltpu.VMEM((half, features), bf16), pltpu.VMEM((rows, 3 * width), bf16)),
        )(own_normed, other_near, other_far, gain_row, shift_row, weights, cosine, sine)
        own_mixed.append(own)
        other_mixed.append(swap(other, "mlp", n_mlp, 1))
    packed = call(
        pack_kernel, [shape(2 * tokens // (2 * SHARES), width)] * SHARES, inputs=2 * len(chunks)
    )(*own_mixed, *other_mixed)
    pieces = send_pieces(packed)
    others = call(unpack_kernel, shape(tokens // 2, width), inputs=SHARES)(*pieces)
    results = pieces + [swap(others, "mlp", n_mlp, 1)]
    result = call(
        functools.partial(place_mixed_kernel, chunks=chunks),
        shape(tokens, width),
        inputs=len(results),
    )(*results)
    return updated.reshape(frames, patches, share), result.reshape(frames, patches, width)


def heads_kernel(qkv_ref, out_ref):
    for lane in range(0, out_ref.shape[-1], HEAD_DIM):
        head = slice(lane, lane + HEAD_DIM)
        (out_ref[:, head],) = attend([tuple(qkv_ref[part, :, head] for part in range(3))])


def columns_kernel(own_ref, other_ref, own_w_ref, other_w_ref, gate_ref, out_ref):
    term = dot(own_ref[...], own_w_ref[...]) + dot(other_ref[...], other_w_ref[...])
    out_ref[...] = (term * gate_ref[...]).astype(out_ref.dtype)


def temporal_kernel(
    u0, u1, u2, u3, gain_ref, shift_ref, w_ref, cos_ref, sin_ref, out_ref, normed_ref, proj_ref
):
    share = u0.shape[-1]
    count = out_ref.shape[0] // cos_ref.shape[0]
    blocks = [
        (ref, pl.multiple_of((lax.axis_index("mlp") ^ k) * share, share))
        for k, ref in enumerate((u0, u1, u2, u3))
    ]
    normalize(blocks, gain_ref, shift_ref, normed_ref)

    def write(f, low, head, value):
        start = f * count + low
        out_ref[start : start + value.shape[0], head] = value

    project_and_mix([normed_ref], lambda f: f, write, w_ref, cos_ref, sin_ref, proj_ref)


def on_device(
    residual, spatial_qkv, spatial_out, temporal_qkv, shift, scale, gate, *, n_seq, n_mlp
):
    frames, patches, share = residual.shape
    width = spatial_qkv.shape[-1]
    features = share * n_mlp
    rows = frames * patches
    count = rows // n_seq
    mlp = lax.axis_index("mlp")
    bf16, f32 = jnp.bfloat16, jnp.float32
    qkv = spatial_qkv.transpose(2, 0, 1, 3).reshape(3, rows, width)
    gate_row = gate.reshape(1, features)

    def columns(array, block):
        return lax.dynamic_slice_in_dim(array, block * share, share, 1)

    heads = call(heads_kernel, jax.ShapeDtypeStruct((rows, width), bf16), inputs=1)(qkv)
    others = swap(heads, "mlp", n_mlp, 1)

    def term(block, kind):
        other_w = swap(columns(spatial_out, block ^ 1), "mlp", n_mlp, 1)
        return call(columns_kernel, jax.ShapeDtypeStruct((rows, share), kind), inputs=5)(
            heads, others, columns(spatial_out, block), other_w, columns(gate_row, block)
        )

    arrived = swap(term(mlp ^ 2, bf16), "mlp", n_mlp, 2)
    branch = term(mlp, f32) + arrived.astype(f32)
    updated = (residual.reshape(rows, share).astype(f32) + branch).astype(bf16)
    mine = lax.all_to_all(
        updated.reshape(n_seq, count, share), "seq", 0, 0, tiled=True
    ).reshape(rows, share)
    across = swap(mine, "mlp", n_mlp, 2)
    mixed = call(
        temporal_kernel,
        jax.ShapeDtypeStruct((rows, width), bf16),
        inputs=9,
        scratch=(pltpu.VMEM((rows, features), bf16), pltpu.VMEM((rows, 3 * width), bf16)),
    )(
        mine,
        swap(mine, "mlp", n_mlp, 1),
        across,
        swap(across, "mlp", n_mlp, 1),
        scale.reshape(1, features),
        shift.reshape(1, features),
        hold_weights(temporal_qkv),
        *rotation_tables(n_seq),
    )
    result = lax.all_to_all(
        mixed.reshape(n_seq, count, width), "seq", 0, 0, tiled=True
    ).reshape(rows, width)
    return updated.reshape(frames, patches, share), result.reshape(frames, patches, width)


def solution(mesh):
    sizes = dict(n_seq=mesh.shape["seq"], n_mlp=mesh.shape["mlp"])
    split = sizes["n_seq"] == 2 * SHARES and sizes["n_mlp"] == 4
    return jax.shard_map(
        functools.partial(split_on_device if split else on_device, **sizes),
        mesh=mesh,
        in_specs=(
            P("seq", None, "mlp"),
            P("seq", None, None, "mlp"),
            P("mlp", None),
            P(None, None, "mlp"),
            P(),
            P(),
            P(),
        ),
        out_specs=(P("seq", None, "mlp"), P("seq", None, "mlp")),
        check_vma=False,
    )
```

```python
import functools
import math

import jax
import jax.numpy as jnp
import numpy as np
from jax import lax
from jax.experimental import pallas as pl
from jax.experimental.pallas import tpu as pltpu
from jax.sharding import PartitionSpec as P

HEAD_DIM = 128
EPSILON = 1e-06
GROUP = 16
MASKED = -1e30
VMEM_LIMIT = 16 * 1024 * 1024
EXP2_SCALE = math.log2(math.e) / math.sqrt(HEAD_DIM)
CHUNK_ROWS = (256, 256)
PARTNERS = ((7, 4, 2, 0), (5, 3, 6, 1))
SHARES = len(PARTNERS[0])


def call(body, outs, flops=0, moved=0, exps=0, inputs=0, scratch=(), far=0):
    return pl.pallas_call(
        body,
        out_shape=outs,
        in_specs=[pl.BlockSpec(memory_space=pltpu.VMEM)] * (inputs - far)
        + [pl.BlockSpec(memory_space=pltpu.HBM)] * far,
        scratch_shapes=list(scratch),
        compiler_params=pltpu.CompilerParams(vmem_limit_bytes=VMEM_LIMIT),
        cost_estimate=pl.CostEstimate(
            flops=int(flops), bytes_accessed=int(moved), transcendentals=int(exps)
        ),
    )


def dot(a, b):
    return jnp.dot(a, b, preferred_element_type=jnp.float32)


def dot_nt(a, b):
    return lax.dot_general(a, b, (((1,), (1,)), ((), ())), preferred_element_type=jnp.float32)


def attend(heads, same=None):
    logits = [dot_nt(query, key) for query, key, _ in heads]
    if same is not None:
        logits = [jnp.where(same, one, MASKED) for one in logits]
    tops = [jnp.max(one, axis=-1, keepdims=True) for one in logits]
    weights = [jnp.exp2((one - top) * EXP2_SCALE) for one, top in zip(logits, tops)]
    rates = [1.0 / jnp.sum(one, axis=-1, keepdims=True) for one in weights]
    return [
        (dot(one.astype(jnp.bfloat16), value) * rate).astype(jnp.bfloat16)
        for one, (_, _, value), rate in zip(weights, heads, rates)
    ]


def normalize(blocks, gain_ref, shift_ref, out_ref):
    features = out_ref.shape[-1]
    total, square = 0.0, 0.0
    for ref, _ in blocks:
        values = ref[...].astype(jnp.float32)
        total += jnp.sum(values, axis=-1, keepdims=True)
        square += jnp.sum(values * values, axis=-1, keepdims=True)
    mean = total / features
    rate = lax.rsqrt(square / features - mean * mean + EPSILON)
    for ref, start in blocks:
        lanes = pl.ds(start, ref.shape[-1])
        gain = 1.0 + gain_ref[:, lanes]
        out_ref[:, lanes] = (
            (ref[...].astype(jnp.float32) - mean) * rate * gain + shift_ref[:, lanes]
        ).astype(out_ref.dtype)


def project(normed_ref, places, w_ref, cos_ref, sin_ref, proj_ref):
    turned_width = w_ref.shape[-1] // 3 * 2
    acc = dot(normed_ref[...], w_ref[...])
    proj_ref[:, turned_width:] = acc[:, turned_width:].astype(proj_ref.dtype)
    count = acc.shape[0] // len(places)
    for i, place in enumerate(places):
        span = slice(i * count, (i + 1) * count)
        row = pl.ds(place, 1)
        cosine, sine = cos_ref[row, :], sin_ref[row, :]
        for lane in range(0, turned_width, HEAD_DIM):
            head = acc[span, lane : lane + HEAD_DIM]
            turned = pltpu.roll(head, HEAD_DIM // 2, 1)
            proj_ref[span, lane : lane + HEAD_DIM] = (head * cosine + turned * sine).astype(
                proj_ref.dtype
            )


def mix(spans, count, write):
    frames = len(spans)
    width = spans[0][0].shape[-1] // 3
    step = GROUP if count % GROUP == 0 else count
    size = step * frames
    patch_of = lambda axis: lax.rem(lax.broadcasted_iota(jnp.int32, (size, size), axis), step)
    same = patch_of(0) == patch_of(1)

    def gathered(low, lane):
        head = slice(lane, lane + HEAD_DIM)
        ref = spans[0][0]
        if step == count and all(span == (ref, i * count) for i, span in enumerate(spans)):
            return ref[:, head]
        return jnp.concatenate(
            [ref[first + low : first + low + step, head] for ref, first in spans], axis=0
        )

    lanes = range(0, width, HEAD_DIM)
    units = [(low, lane) for low in range(0, count, step) for lane in lanes]
    heads = [tuple(gathered(low, part * width + lane) for part in range(3)) for low, lane in units]
    for (low, lane), mixed in zip(units, attend(heads, same)):
        for f in range(frames):
            write(f, low, slice(lane, lane + HEAD_DIM), mixed[f * step : (f + 1) * step])


def hold_kernel(w_far, out_ref, semaphores):
    width = w_far.shape[-1]
    copies = [
        pltpu.make_async_copy(
            w_far.at[part], out_ref.at[:, part * width : (part + 1) * width], semaphores.at[part]
        )
        for part in range(3)
    ]
    for copy in copies:
        copy.start()
    for copy in copies:
        copy.wait()


def hold_weights(temporal_qkv):
    features, parts, width = temporal_qkv.shape
    return pl.pallas_call(
        hold_kernel,
        out_shape=pltpu.VMEM((features, parts * width), temporal_qkv.dtype),
        in_specs=[pl.BlockSpec(memory_space=pltpu.HBM)],
        out_specs=pl.BlockSpec(memory_space=pltpu.VMEM),
        scratch_shapes=[pltpu.SemaphoreType.DMA((parts,))],
        compiler_params=pltpu.CompilerParams(vmem_limit_bytes=1024 * 1024),
        cost_estimate=pl.CostEstimate(flops=0, bytes_accessed=0, transcendentals=0),
    )(in_hbm(temporal_qkv.transpose(1, 0, 2)))


def core_of():
    return lax.rem(lax.axis_index("mlp"), 2)


def chip_of():
    return lax.div(lax.axis_index("mlp"), 2)


def frame_of(i):
    low, high = (PARTNERS[core][i % SHARES] for core in range(2))
    which = core_of() if i < SHARES else 1 - core_of()
    return lax.axis_index("seq") ^ (low + which * (high - low))


def piece_span(first, count, i):
    return pl.ds(pl.multiple_of(first + frame_of(i) * count, count), count)


def piece_rows(ref, first, count, lanes):
    return jnp.concatenate(
        [ref[piece_span(first, count, i), lanes] for i in range(2 * SHARES)], axis=0
    )


def chip_columns(features, flip):
    half = features // 2
    return pl.ds(pl.multiple_of((chip_of() ^ flip) * half, half), half)


def spatial_heads(qkv_ref, heads_ref, first):
    rows, width = heads_ref.shape
    for lane in range(0, width, HEAD_DIM):
        head = slice(lane, lane + HEAD_DIM)
        query = piece_rows(qkv_ref.at[0], first, rows // (2 * SHARES), head)
        (heads_ref[:, head],) = attend([(query, qkv_ref[1, :, head], qkv_ref[2, :, head])])


def first_spatial_kernel(
    qkv_far, w_far, gate_far, heads_ref, message_ref, w_ref, gate_ref, qkv_ref, semaphores, *, first
):
    far = chip_columns(w_far.shape[-1], 1)
    query = pl.ds(first, heads_ref.shape[0])
    moves = [
        (qkv_far.at[0, query], qkv_ref.at[0, query]),
        (qkv_far.at[1:], qkv_ref.at[1:]),
        (w_far.at[:, far], w_ref),
        (gate_far.at[:, far], gate_ref),
    ]
    copies = [pltpu.make_async_copy(*move, semaphores.at[i]) for i, move in enumerate(moves)]
    for copy in copies:
        copy.start()
    for copy in copies[:2]:
        copy.wait()
    spatial_heads(qkv_ref, heads_ref, first)
    for copy in copies[2:]:
        copy.wait()
    term = dot(heads_ref[heads_ref.shape[0] // 2 :, :], w_ref[...])
    message_ref[...] = (term * gate_ref[...]).astype(message_ref.dtype)


def term_kernel(heads_ref, w_ref, gate_ref, out_ref):
    out_ref[...] = dot(heads_ref[: out_ref.shape[0], :], w_ref[...]) * gate_ref[...]


def rest_kernel(
    heads0_ref, qkv_far, w_far, gate_far, residual_far,
    message_ref, term_ref, base0_ref, near0_ref, base1_ref, near1_ref,
    heads1_ref, qkv_ref, w_ref, gate_ref, residual_ref, semaphores, *, firsts
):
    moves = [
        (qkv_far, qkv_ref), (w_far, w_ref), (gate_far, gate_ref), (residual_far, residual_ref)
    ]
    copies = [pltpu.make_async_copy(*move, semaphores.at[i]) for i, move in enumerate(moves)]
    for copy in copies:
        copy.start()
    copies[0].wait()
    spatial_heads(qkv_ref, heads1_ref, firsts[1])
    for copy in copies[1:]:
        copy.wait()
    half, both = message_ref.shape
    features = w_ref.shape[-1]
    far = chip_columns(features, 1)
    term = dot(heads1_ref[...], w_ref[:, far]) * gate_ref[:, far]
    term_ref[...] = term[:half]
    message_ref[...] = term[half:].astype(message_ref.dtype)
    share = both // 2
    for first, heads_ref, base_ref, near_ref in (
        (firsts[0], heads0_ref, base0_ref, near0_ref),
        (firsts[1], heads1_ref, base1_ref, near1_ref),
    ):
        size = base_ref.shape[0]
        for flip in range(2):
            place = pl.multiple_of((core_of() ^ flip) * share, share)
            lanes = pl.ds(pl.multiple_of(chip_of() * both + place, share), share)
            term = dot(heads_ref[...], w_ref[:, lanes]) * gate_ref[:, lanes]
            if flip == 0:
                term += piece_rows(residual_ref, first, size // SHARES, slice(None)).astype(
                    jnp.float32
                )
            base_ref[:, pl.ds(place, share)] = term[:size]
            near_ref[:, pl.ds(place, share)] = term[size:].astype(near_ref.dtype)


def add_kernel(a_ref, b_ref, out_ref):
    out_ref[...] = (a_ref[...] + b_ref[...].astype(jnp.float32)).astype(out_ref.dtype)


def update_kernel(base_ref, arrived_ref, own_ref, other_ref, *piece_refs):
    updated = (base_ref[...] + arrived_ref[...].astype(jnp.float32)).astype(jnp.bfloat16)
    count = piece_refs[0].shape[0]
    for i, piece_ref in enumerate(piece_refs):
        piece_ref[...] = updated[i * count : (i + 1) * count]
    share = own_ref.shape[-1]
    left, right = updated[:, :share], updated[:, share:]
    core = core_of()
    own_ref[...] = jnp.where(core == 0, left, right)
    other_ref[...] = jnp.where(core == 0, right, left)


def split_normalize(near, far, gain_ref, shift_ref, out_ref):
    half = near.shape[-1]
    blocks = [
        (ref, pl.multiple_of((chip_of() ^ flip) * half, half)) for flip, ref in enumerate((near, far))
    ]
    normalize(blocks, gain_ref, shift_ref, out_ref)


def half_kernel(
    near, far, gain_ref, shift_ref, w_ref, cos_ref, sin_ref, proj_ref, normed_ref
):
    split_normalize(near, far, gain_ref, shift_ref, normed_ref)
    places = [frame_of(i) for i in range(SHARES)]
    project(normed_ref, places, w_ref, cos_ref, sin_ref, proj_ref)


def split_temporal_kernel(
    own_proj_ref, near, far, gain_ref, shift_ref, w_ref, cos_ref, sin_ref,
    own_ref, other_ref, normed_ref, proj_ref,
):
    split_normalize(near, far, gain_ref, shift_ref, normed_ref)
    places = [frame_of(SHARES + i) for i in range(SHARES)]
    project(normed_ref, places, w_ref, cos_ref, sin_ref, proj_ref)
    count = own_ref.shape[0] // SHARES

    def write(i, low, head, value):
        ref = own_ref if i < SHARES else other_ref
        start = (i % SHARES) * count + low
        ref[start : start + value.shape[0], head] = value

    spans = [(ref, i * count) for ref in (own_proj_ref, proj_ref) for i in range(SHARES)]
    mix(spans, count, write)


def pack_kernel(*refs):
    block_refs, out_refs = refs[:-SHARES], refs[-SHARES:]
    for i, out_ref in enumerate(out_refs):
        start = 0
        for ref in block_refs:
            count = ref.shape[0] // SHARES
            out_ref[start : start + count] = ref[i * count : (i + 1) * count]
            start += count


def unpack_kernel(*refs):
    *piece_refs, out_ref = refs
    count = piece_refs[0].shape[0] // 2
    for i, ref in enumerate(piece_refs):
        out_ref[i * count : (i + 1) * count] = ref[count:]


def place_updated_kernel(*refs, chunks):
    *block_refs, out_ref = refs
    for (first, rows), own_ref, other_ref in zip(chunks, block_refs[::2], block_refs[1::2]):
        count = rows // (2 * SHARES)
        for i in range(2 * SHARES):
            ref = own_ref if i < SHARES else other_ref
            start = (i % SHARES) * count
            out_ref[piece_span(first, count, i), :] = ref[start : start + count, :]


def place_mixed_kernel(*refs, chunks):
    *own_refs, other_ref, out_ref = refs
    size = own_refs[0].shape[0] // 2
    start = 0
    for first, rows in chunks:
        count = rows // (2 * SHARES)
        for i in range(SHARES):
            out_ref[piece_span(first, count, i), :] = own_refs[i][start : start + count, :]
            low = i * size + start
            out_ref[piece_span(first, count, SHARES + i), :] = other_ref[low : low + count, :]
        start += count


def swap(value, axis, size, k):
    return lax.ppermute(value, axis, [(i, i ^ k) for i in range(size)])


def rotation_tables(frames):
    rates = 10000.0 ** (-2.0 * np.arange(HEAD_DIM // 2, dtype=np.float32) / HEAD_DIM)
    angles = np.arange(frames, dtype=np.float32)[:, None] * rates.astype(np.float32)
    cosine, sine = np.cos(angles), np.sin(angles)
    return (
        jnp.asarray(np.concatenate([cosine, cosine], axis=1), jnp.float32),
        jnp.asarray(np.concatenate([-sine, sine], axis=1), jnp.float32),
    )


def piece_pairs(n_seq, n_mlp, index):
    return [
        (s * n_mlp + m, (s ^ PARTNERS[m % 2][index]) * n_mlp + m)
        for s in range(n_seq)
        for m in range(n_mlp)
    ]


def in_hbm(array):
    return pltpu.with_memory_space_constraint(array, pltpu.HBM)


def after(value, *others):
    return lax.optimization_barrier((value,) + others)[0]


def split_on_device(
    residual, spatial_qkv, spatial_out, temporal_qkv, shift, scale, gate, *, n_seq, n_mlp
):
    frames, patches, share = residual.shape
    width = spatial_qkv.shape[-1]
    features = share * n_mlp
    both = 2 * share
    tokens = frames * patches
    bf16, f32 = jnp.bfloat16, jnp.float32
    flat_residual = residual.reshape(tokens, share)
    qkv = spatial_qkv.transpose(2, 0, 1, 3).reshape(3, tokens, width)
    gate_row = gate.reshape(1, features)
    gain_row, shift_row = scale.reshape(1, features), shift.reshape(1, features)
    cosine, sine = rotation_tables(n_seq)

    def shape(rows, columns, kind=bf16):
        return jax.ShapeDtypeStruct((rows, columns), kind)

    def send_pieces(pieces):
        return [
            lax.ppermute(piece, ("seq", "mlp"), piece_pairs(n_seq, n_mlp, i))
            for i, piece in enumerate(pieces)
        ]

    once = jnp.minimum(lax.axis_index("seq") + 1, 1)

    chunks = []
    first = 0
    for rows in CHUNK_ROWS:
        chunks.append((first, rows))
        first += rows

    (first0, rows0), (first1, rows1) = chunks
    half0, half1 = rows0 // 2, rows1 // 2
    heads, message, far_w, far_gate = call(
        functools.partial(first_spatial_kernel, first=first0),
        [
            shape(rows0, width),
            shape(half0, both),
            pltpu.VMEM((width, both), bf16),
            pltpu.VMEM((1, both), f32),
        ],
        inputs=3,
        far=3,
        scratch=(pltpu.VMEM(qkv.shape, bf16), pltpu.SemaphoreType.DMA((4,))),
    )(*(in_hbm(one) for one in (qkv, spatial_out, gate_row)))
    message = swap(message, "mlp", n_mlp, 1)
    far_term = call(term_kernel, shape(half0, both, f32), inputs=3)(heads, far_w, far_gate)
    sent = call(add_kernel, shape(half0, both), inputs=2)(far_term, message)
    arrived0 = swap(sent, "mlp", n_mlp, 2)

    def rest(heads, *operands):
        message, far_term, base0, near0, base1, near1 = call(
            functools.partial(rest_kernel, firsts=(first0, first1)),
            [
                shape(half1, both),
                shape(half1, both, f32),
                shape(half0, both, f32),
                shape(half0, both),
                shape(half1, both, f32),
                shape(half1, both),
            ],
            inputs=5,
            far=4,
            scratch=(
                pltpu.VMEM((rows1, width), bf16),
                *(pltpu.VMEM(one.shape, one.dtype) for one in operands),
                pltpu.SemaphoreType.DMA((4,)),
            ),
        )(heads, *(in_hbm(one) for one in operands))
        message, near0, near1 = (swap(one, "mlp", n_mlp, 1) for one in (message, near0, near1))
        sent = call(add_kernel, shape(half1, both), inputs=2)(far_term, message)
        base0, base1 = (
            call(add_kernel, shape(*base.shape, f32), inputs=2)(base, near)
            for base, near in ((base0, near0), (base1, near1))
        )
        return sent, base0, base1

    def nothing(*_):
        return (
            jnp.zeros((half1, both), bf16),
            jnp.zeros((half0, both), f32),
            jnp.zeros((half1, both), f32),
        )

    sent, base0, base1 = lax.cond(
        once > 0, rest, nothing, after(heads, sent), qkv, spatial_out, gate_row, flat_residual
    )
    arrived1 = swap(sent, "mlp", n_mlp, 2)
    arrived0 = after(arrived0, sent)

    def update(rows, base, arrived):
        half = rows // 2
        own, other, *pieces = call(
            update_kernel,
            [shape(half, share)] * 2 + [shape(half // SHARES, both)] * SHARES,
            inputs=2,
        )(base, arrived)
        return [own, swap(other, "mlp", n_mlp, 1)], pieces

    blocks0, pieces = update(rows0, base0, arrived0)
    pieces = lax.fori_loop(0, once, lambda _, pieces: send_pieces(pieces), pieces)
    near0 = jnp.concatenate(pieces, axis=0)
    blocks1, pieces = update(rows1, base1, after(arrived1, near0))

    def last_exchange(temporal_qkv, *pieces):
        return (*send_pieces(pieces), hold_weights(temporal_qkv))

    def no_exchange(temporal_qkv, *pieces):
        return (*pieces, jnp.zeros((features, 3 * width), bf16))

    *pieces, weights = lax.cond(once > 0, last_exchange, no_exchange, temporal_qkv, *pieces)
    nears = [near0, jnp.concatenate(pieces, axis=0)]
    blocks = blocks0 + blocks1

    own_mixed, other_mixed = [], []
    for (first, rows), near in zip(chunks, nears):
        half = rows // 2
        far = swap(near, "mlp", n_mlp, 2)
        other_near = swap(near, "mlp", n_mlp, 1)
        if not own_mixed:
            far = after(far, *nears)
        else:
            updated = call(
                functools.partial(place_updated_kernel, chunks=chunks),
                shape(tokens, share),
                inputs=len(blocks),
            )(*blocks)
            far = after(far, other_mixed[-1], updated)
        rest_in = (gain_row, shift_row, weights, cosine, sine)
        other_far = swap(far, "mlp", n_mlp, 1)
        own_proj = call(
            half_kernel,
            shape(half, 3 * width),
            inputs=7,
            scratch=(pltpu.VMEM((half, features), bf16),),
        )(near, far, *rest_in)
        own, other = call(
            split_temporal_kernel,
            [shape(half, width)] * 2,
            inputs=8,
            scratch=(pltpu.VMEM((half, features), bf16), pltpu.VMEM((half, 3 * width), bf16)),
        )(own_proj, other_near, other_far, *rest_in)
        own_mixed.append(own)
        other_mixed.append(swap(other, "mlp", n_mlp, 1))
    packed = call(
        pack_kernel, [shape(2 * tokens // (2 * SHARES), width)] * SHARES, inputs=2 * len(chunks)
    )(*own_mixed, *other_mixed)
    pieces = send_pieces(packed)
    others = call(unpack_kernel, shape(tokens // 2, width), inputs=SHARES)(*pieces)
    results = pieces + [swap(others, "mlp", n_mlp, 1)]
    result = call(
        functools.partial(place_mixed_kernel, chunks=chunks),
        shape(tokens, width),
        inputs=len(results),
    )(*results)
    return updated.reshape(frames, patches, share), result.reshape(frames, patches, width)


def heads_kernel(qkv_ref, out_ref):
    for lane in range(0, out_ref.shape[-1], HEAD_DIM):
        head = slice(lane, lane + HEAD_DIM)
        (out_ref[:, head],) = attend([tuple(qkv_ref[part, :, head] for part in range(3))])


def columns_kernel(own_ref, other_ref, own_w_ref, other_w_ref, gate_ref, out_ref):
    term = dot(own_ref[...], own_w_ref[...]) + dot(other_ref[...], other_w_ref[...])
    out_ref[...] = (term * gate_ref[...]).astype(out_ref.dtype)


def temporal_kernel(
    u0, u1, u2, u3, gain_ref, shift_ref, w_ref, cos_ref, sin_ref, out_ref, normed_ref, proj_ref
):
    share = u0.shape[-1]
    frames = cos_ref.shape[0]
    count = out_ref.shape[0] // frames
    blocks = [
        (ref, pl.multiple_of((lax.axis_index("mlp") ^ k) * share, share))
        for k, ref in enumerate((u0, u1, u2, u3))
    ]
    normalize(blocks, gain_ref, shift_ref, normed_ref)
    project(normed_ref, range(frames), w_ref, cos_ref, sin_ref, proj_ref)

    def write(f, low, head, value):
        start = f * count + low
        out_ref[start : start + value.shape[0], head] = value

    mix([(proj_ref, f * count) for f in range(frames)], count, write)


def on_device(
    residual, spatial_qkv, spatial_out, temporal_qkv, shift, scale, gate, *, n_seq, n_mlp
):
    frames, patches, share = residual.shape
    width = spatial_qkv.shape[-1]
    features = share * n_mlp
    rows = frames * patches
    count = rows // n_seq
    mlp = lax.axis_index("mlp")
    bf16, f32 = jnp.bfloat16, jnp.float32
    qkv = spatial_qkv.transpose(2, 0, 1, 3).reshape(3, rows, width)
    gate_row = gate.reshape(1, features)

    def columns(array, block):
        return lax.dynamic_slice_in_dim(array, block * share, share, 1)

    heads = call(heads_kernel, jax.ShapeDtypeStruct((rows, width), bf16), inputs=1)(qkv)
    others = swap(heads, "mlp", n_mlp, 1)

    def term(block, kind):
        other_w = swap(columns(spatial_out, block ^ 1), "mlp", n_mlp, 1)
        return call(columns_kernel, jax.ShapeDtypeStruct((rows, share), kind), inputs=5)(
            heads, others, columns(spatial_out, block), other_w, columns(gate_row, block)
        )

    arrived = swap(term(mlp ^ 2, bf16), "mlp", n_mlp, 2)
    branch = term(mlp, f32) + arrived.astype(f32)
    updated = (residual.reshape(rows, share).astype(f32) + branch).astype(bf16)
    mine = lax.all_to_all(
        updated.reshape(n_seq, count, share), "seq", 0, 0, tiled=True
    ).reshape(rows, share)
    across = swap(mine, "mlp", n_mlp, 2)
    mixed = call(
        temporal_kernel,
        jax.ShapeDtypeStruct((rows, width), bf16),
        inputs=9,
        scratch=(pltpu.VMEM((rows, features), bf16), pltpu.VMEM((rows, 3 * width), bf16)),
    )(
        mine,
        swap(mine, "mlp", n_mlp, 1),
        across,
        swap(across, "mlp", n_mlp, 1),
        scale.reshape(1, features),
        shift.reshape(1, features),
        hold_weights(temporal_qkv),
        *rotation_tables(n_seq),
    )
    result = lax.all_to_all(
        mixed.reshape(n_seq, count, width), "seq", 0, 0, tiled=True
    ).reshape(rows, width)
    return updated.reshape(frames, patches, share), result.reshape(frames, patches, width)


def solution(mesh):
    sizes = dict(n_seq=mesh.shape["seq"], n_mlp=mesh.shape["mlp"])
    split = sizes["n_seq"] == 2 * SHARES and sizes["n_mlp"] == 4
    return jax.shard_map(
        functools.partial(split_on_device if split else on_device, **sizes),
        mesh=mesh,
        in_specs=(
            P("seq", None, "mlp"),
            P("seq", None, None, "mlp"),
            P("mlp", None),
            P(None, None, "mlp"),
            P(),
            P(),
            P(),
        ),
        out_specs=(P("seq", None, "mlp"), P("seq", None, "mlp")),
        check_vma=False,
    )
```

```python
import functools
import math

import jax
import jax.numpy as jnp
import numpy as np
from jax import lax
from jax.experimental import pallas as pl
from jax.experimental.pallas import tpu as pltpu
from jax.sharding import PartitionSpec as P

HEAD_DIM = 128
EPSILON = 1e-06
GROUP = 16
MASKED = -1e30
VMEM_LIMIT = 16 * 1024 * 1024
EXP2_SCALE = math.log2(math.e) / math.sqrt(HEAD_DIM)
CHUNK_ROWS = (256, 256)
PARTNERS = ((4, 7, 2, 0), (5, 3, 6, 1))
SHARES = len(PARTNERS[0])


def call(body, outs, flops=0, moved=0, exps=0, inputs=0, scratch=(), far=0):
    return pl.pallas_call(
        body,
        out_shape=outs,
        in_specs=[pl.BlockSpec(memory_space=pltpu.VMEM)] * (inputs - far)
        + [pl.BlockSpec(memory_space=pltpu.HBM)] * far,
        scratch_shapes=list(scratch),
        compiler_params=pltpu.CompilerParams(vmem_limit_bytes=VMEM_LIMIT),
        cost_estimate=pl.CostEstimate(
            flops=int(flops), bytes_accessed=int(moved), transcendentals=int(exps)
        ),
    )


def dot(a, b):
    return jnp.dot(a, b, preferred_element_type=jnp.float32)


def dot_nt(a, b):
    return lax.dot_general(a, b, (((1,), (1,)), ((), ())), preferred_element_type=jnp.float32)


def attend(heads, same=None):
    logits = [dot_nt(query, key) for query, key, _ in heads]
    if same is not None:
        logits = [jnp.where(same, one, MASKED) for one in logits]
    tops = [jnp.max(one, axis=-1, keepdims=True) for one in logits]
    weights = [jnp.exp2((one - top) * EXP2_SCALE) for one, top in zip(logits, tops)]
    rates = [1.0 / jnp.sum(one, axis=-1, keepdims=True) for one in weights]
    return [
        (dot(one.astype(jnp.bfloat16), value) * rate).astype(jnp.bfloat16)
        for one, (_, _, value), rate in zip(weights, heads, rates)
    ]


def normalize(blocks, gain_ref, shift_ref, out_ref):
    features = out_ref.shape[-1]
    total, square = 0.0, 0.0
    for ref, _ in blocks:
        values = ref[...].astype(jnp.float32)
        total += jnp.sum(values, axis=-1, keepdims=True)
        square += jnp.sum(values * values, axis=-1, keepdims=True)
    mean = total / features
    rate = lax.rsqrt(square / features - mean * mean + EPSILON)
    for ref, start in blocks:
        lanes = pl.ds(start, ref.shape[-1])
        gain = 1.0 + gain_ref[:, lanes]
        out_ref[:, lanes] = (
            (ref[...].astype(jnp.float32) - mean) * rate * gain + shift_ref[:, lanes]
        ).astype(out_ref.dtype)


def project(normed_ref, places, w_ref, cos_ref, sin_ref, proj_ref):
    turned_width = w_ref.shape[-1] // 3 * 2
    acc = dot(normed_ref[...], w_ref[...])
    proj_ref[:, turned_width:] = acc[:, turned_width:].astype(proj_ref.dtype)
    count = acc.shape[0] // len(places)
    for i, place in enumerate(places):
        span = slice(i * count, (i + 1) * count)
        row = pl.ds(place, 1)
        cosine, sine = cos_ref[row, :], sin_ref[row, :]
        for lane in range(0, turned_width, HEAD_DIM):
            head = acc[span, lane : lane + HEAD_DIM]
            turned = pltpu.roll(head, HEAD_DIM // 2, 1)
            proj_ref[span, lane : lane + HEAD_DIM] = (head * cosine + turned * sine).astype(
                proj_ref.dtype
            )


def mix(spans, count, write):
    frames = len(spans)
    width = spans[0][0].shape[-1] // 3
    step = GROUP if count % GROUP == 0 else count
    size = step * frames
    patch_of = lambda axis: lax.rem(lax.broadcasted_iota(jnp.int32, (size, size), axis), step)
    same = patch_of(0) == patch_of(1)

    def gathered(low, lane):
        head = slice(lane, lane + HEAD_DIM)
        ref = spans[0][0]
        if step == count and all(span == (ref, i * count) for i, span in enumerate(spans)):
            return ref[:, head]
        return jnp.concatenate(
            [ref[first + low : first + low + step, head] for ref, first in spans], axis=0
        )

    lanes = range(0, width, HEAD_DIM)
    units = [(low, lane) for low in range(0, count, step) for lane in lanes]
    heads = [tuple(gathered(low, part * width + lane) for part in range(3)) for low, lane in units]
    for (low, lane), mixed in zip(units, attend(heads, same)):
        for f in range(frames):
            write(f, low, slice(lane, lane + HEAD_DIM), mixed[f * step : (f + 1) * step])


def hold_kernel(w_far, out_ref, semaphores):
    width = w_far.shape[-1]
    copies = [
        pltpu.make_async_copy(
            w_far.at[part], out_ref.at[:, part * width : (part + 1) * width], semaphores.at[part]
        )
        for part in range(3)
    ]
    for copy in copies:
        copy.start()
    for copy in copies:
        copy.wait()


def hold_weights(temporal_qkv):
    features, parts, width = temporal_qkv.shape
    return pl.pallas_call(
        hold_kernel,
        out_shape=pltpu.VMEM((features, parts * width), temporal_qkv.dtype),
        in_specs=[pl.BlockSpec(memory_space=pltpu.HBM)],
        out_specs=pl.BlockSpec(memory_space=pltpu.VMEM),
        scratch_shapes=[pltpu.SemaphoreType.DMA((parts,))],
        compiler_params=pltpu.CompilerParams(vmem_limit_bytes=1024 * 1024),
        cost_estimate=pl.CostEstimate(flops=0, bytes_accessed=0, transcendentals=0),
    )(in_hbm(temporal_qkv.transpose(1, 0, 2)))


def core_of():
    return lax.rem(lax.axis_index("mlp"), 2)


def chip_of():
    return lax.div(lax.axis_index("mlp"), 2)


def frame_of(i):
    low, high = (PARTNERS[core][i % SHARES] for core in range(2))
    which = core_of() if i < SHARES else 1 - core_of()
    return lax.axis_index("seq") ^ (low + which * (high - low))


def piece_span(first, count, i):
    return pl.ds(pl.multiple_of(first + frame_of(i) * count, count), count)


OWN, OTHER, ALL = range(SHARES), range(SHARES, 2 * SHARES), range(2 * SHARES)


def piece_rows(ref, first, count, lanes, pieces=ALL):
    return jnp.concatenate([ref[piece_span(first, count, i), lanes] for i in pieces], axis=0)


def chip_columns(features, flip):
    half = features // 2
    return pl.ds(pl.multiple_of((chip_of() ^ flip) * half, half), half)


def spatial_heads(qkv_ref, heads_ref, first, pieces=ALL):
    rows, width = heads_ref.shape
    for lane in range(0, width, HEAD_DIM):
        head = slice(lane, lane + HEAD_DIM)
        query = piece_rows(qkv_ref.at[0], first, rows // len(pieces), head, pieces)
        (heads_ref[:, head],) = attend([(query, qkv_ref[1, :, head], qkv_ref[2, :, head])])


def first_spatial_kernel(
    qkv_far, w_far, gate_far, heads_ref, message_ref, w_ref, gate_ref, qkv_ref, semaphores, *, first
):
    far = chip_columns(w_far.shape[-1], 1)
    query = pl.ds(first, 2 * heads_ref.shape[0])
    moves = [
        (qkv_far.at[0, query], qkv_ref.at[0, query]),
        (qkv_far.at[1:], qkv_ref.at[1:]),
        (w_far.at[:, far], w_ref),
        (gate_far.at[:, far], gate_ref),
    ]
    copies = [pltpu.make_async_copy(*move, semaphores.at[i]) for i, move in enumerate(moves)]
    for copy in copies:
        copy.start()
    for copy in copies[:2]:
        copy.wait()
    spatial_heads(qkv_ref, heads_ref, first, OTHER)
    for copy in copies[2:]:
        copy.wait()
    term = dot(heads_ref[...], w_ref[...])
    message_ref[...] = (term * gate_ref[...]).astype(message_ref.dtype)


def term_kernel(w_ref, gate_ref, qkv_ref, heads_ref, out_ref, *, first):
    spatial_heads(qkv_ref, heads_ref, first, OWN)
    out_ref[...] = dot(heads_ref[...], w_ref[...]) * gate_ref[...]


def rest_kernel(
    own0_ref, other0_ref, qkv_far, w_far, gate_far, residual_far,
    message_ref, term_ref, base0_ref, near0_ref, base1_ref, near1_ref,
    heads1_ref, qkv_ref, w_ref, gate_ref, residual_ref, semaphores, *, firsts
):
    moves = [
        (qkv_far, qkv_ref), (w_far, w_ref), (gate_far, gate_ref), (residual_far, residual_ref)
    ]
    copies = [pltpu.make_async_copy(*move, semaphores.at[i]) for i, move in enumerate(moves)]
    for copy in copies:
        copy.start()
    copies[0].wait()
    spatial_heads(qkv_ref, heads1_ref, firsts[1])
    for copy in copies[1:]:
        copy.wait()
    half, both = message_ref.shape
    features = w_ref.shape[-1]
    far = chip_columns(features, 1)
    term = dot(heads1_ref[...], w_ref[:, far]) * gate_ref[:, far]
    term_ref[...] = term[:half]
    message_ref[...] = term[half:].astype(message_ref.dtype)
    share = both // 2
    heads0 = jnp.concatenate([own0_ref[...], other0_ref[...]], axis=0)
    for first, heads, base_ref, near_ref in (
        (firsts[0], heads0, base0_ref, near0_ref),
        (firsts[1], heads1_ref[...], base1_ref, near1_ref),
    ):
        size = base_ref.shape[0]
        for flip in range(2):
            place = pl.multiple_of((core_of() ^ flip) * share, share)
            lanes = pl.ds(pl.multiple_of(chip_of() * both + place, share), share)
            term = dot(heads, w_ref[:, lanes]) * gate_ref[:, lanes]
            if flip == 0:
                term += piece_rows(residual_ref, first, size // SHARES, slice(None)).astype(
                    jnp.float32
                )
            base_ref[:, pl.ds(place, share)] = term[:size]
            near_ref[:, pl.ds(place, share)] = term[size:].astype(near_ref.dtype)


def add_kernel(a_ref, b_ref, out_ref):
    out_ref[...] = (a_ref[...] + b_ref[...].astype(jnp.float32)).astype(out_ref.dtype)


def update_kernel(base_ref, arrived_ref, own_ref, other_ref, *piece_refs):
    updated = (base_ref[...] + arrived_ref[...].astype(jnp.float32)).astype(jnp.bfloat16)
    count = piece_refs[0].shape[0]
    for i, piece_ref in enumerate(piece_refs):
        piece_ref[...] = updated[i * count : (i + 1) * count]
    share = own_ref.shape[-1]
    left, right = updated[:, :share], updated[:, share:]
    core = core_of()
    own_ref[...] = jnp.where(core == 0, left, right)
    other_ref[...] = jnp.where(core == 0, right, left)


def split_normalize(near, far, gain_ref, shift_ref, out_ref):
    half = near.shape[-1]
    blocks = [
        (ref, pl.multiple_of((chip_of() ^ flip) * half, half)) for flip, ref in enumerate((near, far))
    ]
    normalize(blocks, gain_ref, shift_ref, out_ref)


def half_kernel(
    near, far, gain_ref, shift_ref, w_ref, cos_ref, sin_ref, proj_ref, normed_ref
):
    split_normalize(near, far, gain_ref, shift_ref, normed_ref)
    places = [frame_of(i) for i in range(SHARES)]
    project(normed_ref, places, w_ref, cos_ref, sin_ref, proj_ref)


def split_temporal_kernel(
    own_proj_ref, near, far, gain_ref, shift_ref, w_ref, cos_ref, sin_ref,
    own_ref, other_ref, normed_ref, proj_ref,
):
    split_normalize(near, far, gain_ref, shift_ref, normed_ref)
    places = [frame_of(SHARES + i) for i in range(SHARES)]
    project(normed_ref, places, w_ref, cos_ref, sin_ref, proj_ref)
    count = own_ref.shape[0] // SHARES

    def write(i, low, head, value):
        ref = own_ref if i < SHARES else other_ref
        start = (i % SHARES) * count + low
        ref[start : start + value.shape[0], head] = value

    spans = [(ref, i * count) for ref in (own_proj_ref, proj_ref) for i in range(SHARES)]
    mix(spans, count, write)


def pack_kernel(*refs):
    block_refs, out_refs = refs[:-SHARES], refs[-SHARES:]
    for i, out_ref in enumerate(out_refs):
        start = 0
        for ref in block_refs:
            count = ref.shape[0] // SHARES
            out_ref[start : start + count] = ref[i * count : (i + 1) * count]
            start += count


def unpack_kernel(*refs):
    *piece_refs, out_ref = refs
    count = piece_refs[0].shape[0] // 2
    for i, ref in enumerate(piece_refs):
        out_ref[i * count : (i + 1) * count] = ref[count:]


def place_updated_kernel(*refs, chunks):
    *block_refs, out_ref = refs
    for (first, rows), own_ref, other_ref in zip(chunks, block_refs[::2], block_refs[1::2]):
        count = rows // (2 * SHARES)
        for i in range(2 * SHARES):
            ref = own_ref if i < SHARES else other_ref
            start = (i % SHARES) * count
            out_ref[piece_span(first, count, i), :] = ref[start : start + count, :]


def place_mixed_kernel(*refs, chunks):
    *own_refs, other_ref, out_ref = refs
    size = own_refs[0].shape[0] // 2
    start = 0
    for first, rows in chunks:
        count = rows // (2 * SHARES)
        for i in range(SHARES):
            out_ref[piece_span(first, count, i), :] = own_refs[i][start : start + count, :]
            low = i * size + start
            out_ref[piece_span(first, count, SHARES + i), :] = other_ref[low : low + count, :]
        start += count


def swap(value, axis, size, k):
    return lax.ppermute(value, axis, [(i, i ^ k) for i in range(size)])


def rotation_tables(frames):
    rates = 10000.0 ** (-2.0 * np.arange(HEAD_DIM // 2, dtype=np.float32) / HEAD_DIM)
    angles = np.arange(frames, dtype=np.float32)[:, None] * rates.astype(np.float32)
    cosine, sine = np.cos(angles), np.sin(angles)
    return (
        jnp.asarray(np.concatenate([cosine, cosine], axis=1), jnp.float32),
        jnp.asarray(np.concatenate([-sine, sine], axis=1), jnp.float32),
    )


def piece_pairs(n_seq, n_mlp, index):
    return [
        (s * n_mlp + m, (s ^ PARTNERS[m % 2][index]) * n_mlp + m)
        for s in range(n_seq)
        for m in range(n_mlp)
    ]


def in_hbm(array):
    return pltpu.with_memory_space_constraint(array, pltpu.HBM)


def after(value, *others):
    return lax.optimization_barrier((value,) + others)[0]


def split_on_device(
    residual, spatial_qkv, spatial_out, temporal_qkv, shift, scale, gate, *, n_seq, n_mlp
):
    frames, patches, share = residual.shape
    width = spatial_qkv.shape[-1]
    features = share * n_mlp
    both = 2 * share
    tokens = frames * patches
    bf16, f32 = jnp.bfloat16, jnp.float32
    flat_residual = residual.reshape(tokens, share)
    qkv = spatial_qkv.transpose(2, 0, 1, 3).reshape(3, tokens, width)
    gate_row = gate.reshape(1, features)
    gain_row, shift_row = scale.reshape(1, features), shift.reshape(1, features)
    cosine, sine = rotation_tables(n_seq)

    def shape(rows, columns, kind=bf16):
        return jax.ShapeDtypeStruct((rows, columns), kind)

    def send_pieces(pieces):
        return [
            lax.ppermute(piece, ("seq", "mlp"), piece_pairs(n_seq, n_mlp, i))
            for i, piece in enumerate(pieces)
        ]

    once = jnp.minimum(lax.axis_index("seq") + 1, 1)

    chunks = []
    first = 0
    for rows in CHUNK_ROWS:
        chunks.append((first, rows))
        first += rows

    (first0, rows0), (first1, rows1) = chunks
    half0, half1 = rows0 // 2, rows1 // 2
    other_heads, message, *held = call(
        functools.partial(first_spatial_kernel, first=first0),
        [
            shape(half0, width),
            shape(half0, both),
            pltpu.VMEM((width, both), bf16),
            pltpu.VMEM((1, both), f32),
            pltpu.VMEM(qkv.shape, bf16),
        ],
        inputs=3,
        far=3,
        scratch=(pltpu.SemaphoreType.DMA((4,)),),
    )(*(in_hbm(one) for one in (qkv, spatial_out, gate_row)))
    message = swap(message, "mlp", n_mlp, 1)
    own_heads, far_term = call(
        functools.partial(term_kernel, first=first0),
        [shape(half0, width), shape(half0, both, f32)],
        inputs=3,
    )(*held)
    sent = call(add_kernel, shape(half0, both), inputs=2)(far_term, message)
    arrived0 = swap(sent, "mlp", n_mlp, 2)

    def rest(own_heads, other_heads, *operands):
        message, far_term, base0, near0, base1, near1 = call(
            functools.partial(rest_kernel, firsts=(first0, first1)),
            [
                shape(half1, both),
                shape(half1, both, f32),
                shape(half0, both, f32),
                shape(half0, both),
                shape(half1, both, f32),
                shape(half1, both),
            ],
            inputs=6,
            far=4,
            scratch=(
                pltpu.VMEM((rows1, width), bf16),
                *(pltpu.VMEM(one.shape, one.dtype) for one in operands),
                pltpu.SemaphoreType.DMA((4,)),
            ),
        )(own_heads, other_heads, *(in_hbm(one) for one in operands))
        message, near0, near1 = (swap(one, "mlp", n_mlp, 1) for one in (message, near0, near1))
        sent = call(add_kernel, shape(half1, both), inputs=2)(far_term, message)
        base0, base1 = (
            call(add_kernel, shape(*base.shape, f32), inputs=2)(base, near)
            for base, near in ((base0, near0), (base1, near1))
        )
        return sent, base0, base1

    def nothing(*_):
        return (
            jnp.zeros((half1, both), bf16),
            jnp.zeros((half0, both), f32),
            jnp.zeros((half1, both), f32),
        )

    sent, base0, base1 = lax.cond(
        once > 0,
        rest,
        nothing,
        after(own_heads, sent),
        other_heads,
        qkv,
        spatial_out,
        gate_row,
        flat_residual,
    )
    arrived1 = swap(sent, "mlp", n_mlp, 2)
    arrived0 = after(arrived0, sent)

    def update(rows, base, arrived):
        half = rows // 2
        own, other, *pieces = call(
            update_kernel,
            [shape(half, share)] * 2 + [shape(half // SHARES, both)] * SHARES,
            inputs=2,
        )(base, arrived)
        return [own, swap(other, "mlp", n_mlp, 1)], pieces

    blocks0, pieces = update(rows0, base0, arrived0)
    pieces = lax.fori_loop(0, once, lambda _, pieces: send_pieces(pieces), pieces)
    near0 = jnp.concatenate(pieces, axis=0)
    blocks1, pieces = update(rows1, base1, after(arrived1, near0))

    def last_exchange(temporal_qkv, *pieces):
        return (*send_pieces(pieces), hold_weights(temporal_qkv))

    def no_exchange(temporal_qkv, *pieces):
        return (*pieces, jnp.zeros((features, 3 * width), bf16))

    *pieces, weights = lax.cond(once > 0, last_exchange, no_exchange, temporal_qkv, *pieces)
    nears = [near0, jnp.concatenate(pieces, axis=0)]
    blocks = blocks0 + blocks1

    own_mixed, other_mixed = [], []
    for (first, rows), near in zip(chunks, nears):
        half = rows // 2
        far = swap(near, "mlp", n_mlp, 2)
        other_near = swap(near, "mlp", n_mlp, 1)
        if not own_mixed:
            far = after(far, *nears)
        else:
            updated = call(
                functools.partial(place_updated_kernel, chunks=chunks),
                shape(tokens, share),
                inputs=len(blocks),
            )(*blocks)
            far = after(far, other_mixed[-1], updated)
        rest_in = (gain_row, shift_row, weights, cosine, sine)
        other_far = swap(far, "mlp", n_mlp, 1)
        own_proj = call(
            half_kernel,
            shape(half, 3 * width),
            inputs=7,
            scratch=(pltpu.VMEM((half, features), bf16),),
        )(near, far, *rest_in)
        own, other = call(
            split_temporal_kernel,
            [shape(half, width)] * 2,
            inputs=8,
            scratch=(pltpu.VMEM((half, features), bf16), pltpu.VMEM((half, 3 * width), bf16)),
        )(own_proj, other_near, other_far, *rest_in)
        own_mixed.append(own)
        other_mixed.append(swap(other, "mlp", n_mlp, 1))
    packed = call(
        pack_kernel, [shape(2 * tokens // (2 * SHARES), width)] * SHARES, inputs=2 * len(chunks)
    )(*own_mixed, *other_mixed)
    pieces = send_pieces(packed)
    others = call(unpack_kernel, shape(tokens // 2, width), inputs=SHARES)(*pieces)
    results = pieces + [swap(others, "mlp", n_mlp, 1)]
    result = call(
        functools.partial(place_mixed_kernel, chunks=chunks),
        shape(tokens, width),
        inputs=len(results),
    )(*results)
    return updated.reshape(frames, patches, share), result.reshape(frames, patches, width)


def heads_kernel(qkv_ref, out_ref):
    for lane in range(0, out_ref.shape[-1], HEAD_DIM):
        head = slice(lane, lane + HEAD_DIM)
        (out_ref[:, head],) = attend([tuple(qkv_ref[part, :, head] for part in range(3))])


def columns_kernel(own_ref, other_ref, own_w_ref, other_w_ref, gate_ref, out_ref):
    term = dot(own_ref[...], own_w_ref[...]) + dot(other_ref[...], other_w_ref[...])
    out_ref[...] = (term * gate_ref[...]).astype(out_ref.dtype)


def temporal_kernel(
    u0, u1, u2, u3, gain_ref, shift_ref, w_ref, cos_ref, sin_ref, out_ref, normed_ref, proj_ref
):
    share = u0.shape[-1]
    frames = cos_ref.shape[0]
    count = out_ref.shape[0] // frames
    blocks = [
        (ref, pl.multiple_of((lax.axis_index("mlp") ^ k) * share, share))
        for k, ref in enumerate((u0, u1, u2, u3))
    ]
    normalize(blocks, gain_ref, shift_ref, normed_ref)
    project(normed_ref, range(frames), w_ref, cos_ref, sin_ref, proj_ref)

    def write(f, low, head, value):
        start = f * count + low
        out_ref[start : start + value.shape[0], head] = value

    mix([(proj_ref, f * count) for f in range(frames)], count, write)


def on_device(
    residual, spatial_qkv, spatial_out, temporal_qkv, shift, scale, gate, *, n_seq, n_mlp
):
    frames, patches, share = residual.shape
    width = spatial_qkv.shape[-1]
    features = share * n_mlp
    rows = frames * patches
    count = rows // n_seq
    mlp = lax.axis_index("mlp")
    bf16, f32 = jnp.bfloat16, jnp.float32
    qkv = spatial_qkv.transpose(2, 0, 1, 3).reshape(3, rows, width)
    gate_row = gate.reshape(1, features)

    def columns(array, block):
        return lax.dynamic_slice_in_dim(array, block * share, share, 1)

    heads = call(heads_kernel, jax.ShapeDtypeStruct((rows, width), bf16), inputs=1)(qkv)
    others = swap(heads, "mlp", n_mlp, 1)

    def term(block, kind):
        other_w = swap(columns(spatial_out, block ^ 1), "mlp", n_mlp, 1)
        return call(columns_kernel, jax.ShapeDtypeStruct((rows, share), kind), inputs=5)(
            heads, others, columns(spatial_out, block), other_w, columns(gate_row, block)
        )

    arrived = swap(term(mlp ^ 2, bf16), "mlp", n_mlp, 2)
    branch = term(mlp, f32) + arrived.astype(f32)
    updated = (residual.reshape(rows, share).astype(f32) + branch).astype(bf16)
    mine = lax.all_to_all(
        updated.reshape(n_seq, count, share), "seq", 0, 0, tiled=True
    ).reshape(rows, share)
    across = swap(mine, "mlp", n_mlp, 2)
    mixed = call(
        temporal_kernel,
        jax.ShapeDtypeStruct((rows, width), bf16),
        inputs=9,
        scratch=(pltpu.VMEM((rows, features), bf16), pltpu.VMEM((rows, 3 * width), bf16)),
    )(
        mine,
        swap(mine, "mlp", n_mlp, 1),
        across,
        swap(across, "mlp", n_mlp, 1),
        scale.reshape(1, features),
        shift.reshape(1, features),
        hold_weights(temporal_qkv),
        *rotation_tables(n_seq),
    )
    result = lax.all_to_all(
        mixed.reshape(n_seq, count, width), "seq", 0, 0, tiled=True
    ).reshape(rows, width)
    return updated.reshape(frames, patches, share), result.reshape(frames, patches, width)


def solution(mesh):
    sizes = dict(n_seq=mesh.shape["seq"], n_mlp=mesh.shape["mlp"])
    split = sizes["n_seq"] == 2 * SHARES and sizes["n_mlp"] == 4
    return jax.shard_map(
        functools.partial(split_on_device if split else on_device, **sizes),
        mesh=mesh,
        in_specs=(
            P("seq", None, "mlp"),
            P("seq", None, None, "mlp"),
            P("mlp", None),
            P(None, None, "mlp"),
            P(),
            P(),
            P(),
        ),
        out_specs=(P("seq", None, "mlp"), P("seq", None, "mlp")),
        check_vma=False,
    )
```

```python
import functools
import math

import jax
import jax.numpy as jnp
import numpy as np
from jax import lax
from jax.experimental import pallas as pl
from jax.experimental.pallas import tpu as pltpu
from jax.sharding import PartitionSpec as P

HEAD_DIM = 128
EPSILON = 1e-06
GROUP = 16
MASKED = -1e30
VMEM_LIMIT = 16 * 1024 * 1024
EXP2_SCALE = math.log2(math.e) / math.sqrt(HEAD_DIM)
CHUNK_ROWS = (256, 256)
PARTNERS = ((4, 7, 2, 0), (5, 3, 6, 1))
SHARES = len(PARTNERS[0])


def call(body, outs, flops=0, moved=0, exps=0, inputs=0, scratch=(), far=0):
    return pl.pallas_call(
        body,
        out_shape=outs,
        in_specs=[pl.BlockSpec(memory_space=pltpu.VMEM)] * (inputs - far)
        + [pl.BlockSpec(memory_space=pltpu.HBM)] * far,
        scratch_shapes=list(scratch),
        compiler_params=pltpu.CompilerParams(vmem_limit_bytes=VMEM_LIMIT),
        cost_estimate=pl.CostEstimate(
            flops=int(flops), bytes_accessed=int(moved), transcendentals=int(exps)
        ),
    )


def dot(a, b):
    return jnp.dot(a, b, preferred_element_type=jnp.float32)


def dot_nt(a, b):
    return lax.dot_general(a, b, (((1,), (1,)), ((), ())), preferred_element_type=jnp.float32)


def attend(heads, same=None):
    logits = [dot_nt(query, key) for query, key, _ in heads]
    if same is not None:
        logits = [jnp.where(same, one, MASKED) for one in logits]
    tops = [jnp.max(one, axis=-1, keepdims=True) for one in logits]
    weights = [jnp.exp2((one - top) * EXP2_SCALE) for one, top in zip(logits, tops)]
    rates = [1.0 / jnp.sum(one, axis=-1, keepdims=True) for one in weights]
    return [
        (dot(one.astype(jnp.bfloat16), value) * rate).astype(jnp.bfloat16)
        for one, (_, _, value), rate in zip(weights, heads, rates)
    ]


def normalize(blocks, gain_ref, shift_ref, out_ref):
    features = out_ref.shape[-1]
    total, square = 0.0, 0.0
    for ref, _ in blocks:
        values = ref[...].astype(jnp.float32)
        total += jnp.sum(values, axis=-1, keepdims=True)
        square += jnp.sum(values * values, axis=-1, keepdims=True)
    mean = total / features
    rate = lax.rsqrt(square / features - mean * mean + EPSILON)
    for ref, start in blocks:
        lanes = pl.ds(start, ref.shape[-1])
        gain = 1.0 + gain_ref[:, lanes]
        out_ref[:, lanes] = (
            (ref[...].astype(jnp.float32) - mean) * rate * gain + shift_ref[:, lanes]
        ).astype(out_ref.dtype)


def turn(acc, places, cos_ref, sin_ref, proj_ref):
    turned_width = acc.shape[-1] // 3 * 2
    proj_ref[:, turned_width:] = acc[:, turned_width:].astype(proj_ref.dtype)
    count = acc.shape[0] // len(places)
    for i, place in enumerate(places):
        span = slice(i * count, (i + 1) * count)
        row = pl.ds(place, 1)
        cosine, sine = cos_ref[row, :], sin_ref[row, :]
        for lane in range(0, turned_width, HEAD_DIM):
            head = acc[span, lane : lane + HEAD_DIM]
            turned = pltpu.roll(head, HEAD_DIM // 2, 1)
            proj_ref[span, lane : lane + HEAD_DIM] = (head * cosine + turned * sine).astype(
                proj_ref.dtype
            )


def project(normed_ref, places, w_ref, cos_ref, sin_ref, proj_ref):
    turn(dot(normed_ref[...], w_ref[...]), places, cos_ref, sin_ref, proj_ref)


def mix(spans, count, write):
    frames = len(spans)
    width = spans[0][0].shape[-1] // 3
    step = GROUP if count % GROUP == 0 else count
    size = step * frames
    patch_of = lambda axis: lax.rem(lax.broadcasted_iota(jnp.int32, (size, size), axis), step)
    same = patch_of(0) == patch_of(1)

    def gathered(low, lane):
        head = slice(lane, lane + HEAD_DIM)
        ref = spans[0][0]
        if step == count and all(span == (ref, i * count) for i, span in enumerate(spans)):
            return ref[:, head]
        return jnp.concatenate(
            [ref[first + low : first + low + step, head] for ref, first in spans], axis=0
        )

    lanes = range(0, width, HEAD_DIM)
    units = [(low, lane) for low in range(0, count, step) for lane in lanes]
    heads = [tuple(gathered(low, part * width + lane) for part in range(3)) for low, lane in units]
    for (low, lane), mixed in zip(units, attend(heads, same)):
        for f in range(frames):
            write(f, low, slice(lane, lane + HEAD_DIM), mixed[f * step : (f + 1) * step])


def hold_kernel(w_far, out_ref, semaphores):
    width = w_far.shape[-1]
    copies = [
        pltpu.make_async_copy(
            w_far.at[part], out_ref.at[:, part * width : (part + 1) * width], semaphores.at[part]
        )
        for part in range(3)
    ]
    for copy in copies:
        copy.start()
    for copy in copies:
        copy.wait()


def hold_weights(temporal_qkv):
    features, parts, width = temporal_qkv.shape
    return pl.pallas_call(
        hold_kernel,
        out_shape=pltpu.VMEM((features, parts * width), temporal_qkv.dtype),
        in_specs=[pl.BlockSpec(memory_space=pltpu.HBM)],
        out_specs=pl.BlockSpec(memory_space=pltpu.VMEM),
        scratch_shapes=[pltpu.SemaphoreType.DMA((parts,))],
        compiler_params=pltpu.CompilerParams(vmem_limit_bytes=1024 * 1024),
        cost_estimate=pl.CostEstimate(flops=0, bytes_accessed=0, transcendentals=0),
    )(in_hbm(temporal_qkv.transpose(1, 0, 2)))


def core_of():
    return lax.rem(lax.axis_index("mlp"), 2)


def chip_of():
    return lax.div(lax.axis_index("mlp"), 2)


def frame_of(i):
    low, high = (PARTNERS[core][i % SHARES] for core in range(2))
    which = core_of() if i < SHARES else 1 - core_of()
    return lax.axis_index("seq") ^ (low + which * (high - low))


def piece_span(first, count, i):
    return pl.ds(pl.multiple_of(first + frame_of(i) * count, count), count)


OWN, OTHER, ALL = range(SHARES), range(SHARES, 2 * SHARES), range(2 * SHARES)


def piece_rows(ref, first, count, lanes, pieces=ALL):
    return jnp.concatenate([ref[piece_span(first, count, i), lanes] for i in pieces], axis=0)


def chip_columns(features, flip):
    half = features // 2
    return pl.ds(pl.multiple_of((chip_of() ^ flip) * half, half), half)


def spatial_heads(qkv_ref, heads_ref, first, pieces=ALL):
    rows, width = heads_ref.shape
    for lane in range(0, width, HEAD_DIM):
        head = slice(lane, lane + HEAD_DIM)
        query = piece_rows(qkv_ref.at[0], first, rows // len(pieces), head, pieces)
        (heads_ref[:, head],) = attend([(query, qkv_ref[1, :, head], qkv_ref[2, :, head])])


def first_spatial_kernel(
    qkv_far, w_far, gate_far, heads_ref, message_ref, w_ref, gate_ref, qkv_ref, semaphores, *, first
):
    far = chip_columns(w_far.shape[-1], 1)
    query = pl.ds(first, 2 * heads_ref.shape[0])
    moves = [
        (qkv_far.at[0, query], qkv_ref.at[0, query]),
        (qkv_far.at[1:], qkv_ref.at[1:]),
        (w_far.at[:, far], w_ref),
        (gate_far.at[:, far], gate_ref),
    ]
    copies = [pltpu.make_async_copy(*move, semaphores.at[i]) for i, move in enumerate(moves)]
    for copy in copies:
        copy.start()
    for copy in copies[:2]:
        copy.wait()
    spatial_heads(qkv_ref, heads_ref, first, OTHER)
    for copy in copies[2:]:
        copy.wait()
    term = dot(heads_ref[...], w_ref[...])
    message_ref[...] = (term * gate_ref[...]).astype(message_ref.dtype)


def term_kernel(w_ref, gate_ref, qkv_ref, heads_ref, out_ref, *, first):
    spatial_heads(qkv_ref, heads_ref, first, OWN)
    out_ref[...] = dot(heads_ref[...], w_ref[...]) * gate_ref[...]


def rest_kernel(
    own0_ref, other0_ref, qkv_far, w_far, gate_far, residual_far,
    message_ref, term_ref, base0_ref, near0_ref, base1_ref, near1_ref,
    heads1_ref, qkv_ref, w_ref, gate_ref, residual_ref, semaphores, *, firsts
):
    moves = [
        (qkv_far, qkv_ref), (w_far, w_ref), (gate_far, gate_ref), (residual_far, residual_ref)
    ]
    copies = [pltpu.make_async_copy(*move, semaphores.at[i]) for i, move in enumerate(moves)]
    for copy in copies:
        copy.start()
    copies[0].wait()
    spatial_heads(qkv_ref, heads1_ref, firsts[1])
    for copy in copies[1:]:
        copy.wait()
    half, both = message_ref.shape
    features = w_ref.shape[-1]
    far = chip_columns(features, 1)
    term = dot(heads1_ref[...], w_ref[:, far]) * gate_ref[:, far]
    term_ref[...] = term[:half]
    message_ref[...] = term[half:].astype(message_ref.dtype)
    share = both // 2
    heads0 = jnp.concatenate([own0_ref[...], other0_ref[...]], axis=0)
    for first, heads, base_ref, near_ref in (
        (firsts[0], heads0, base0_ref, near0_ref),
        (firsts[1], heads1_ref[...], base1_ref, near1_ref),
    ):
        size = base_ref.shape[0]
        for flip in range(2):
            place = pl.multiple_of((core_of() ^ flip) * share, share)
            lanes = pl.ds(pl.multiple_of(chip_of() * both + place, share), share)
            term = dot(heads, w_ref[:, lanes]) * gate_ref[:, lanes]
            if flip == 0:
                term += piece_rows(residual_ref, first, size // SHARES, slice(None)).astype(
                    jnp.float32
                )
            base_ref[:, pl.ds(place, share)] = term[:size]
            near_ref[:, pl.ds(place, share)] = term[size:].astype(near_ref.dtype)


def add_kernel(a_ref, b_ref, out_ref):
    out_ref[...] = (a_ref[...] + b_ref[...].astype(jnp.float32)).astype(out_ref.dtype)


def update_kernel(base_ref, arrived_ref, own_ref, other_ref, *piece_refs):
    updated = (base_ref[...] + arrived_ref[...].astype(jnp.float32)).astype(jnp.bfloat16)
    count = piece_refs[0].shape[0]
    for i, piece_ref in enumerate(piece_refs):
        piece_ref[...] = updated[i * count : (i + 1) * count]
    share = own_ref.shape[-1]
    left, right = updated[:, :share], updated[:, share:]
    core = core_of()
    own_ref[...] = jnp.where(core == 0, left, right)
    other_ref[...] = jnp.where(core == 0, right, left)


def split_normalize(near, far, gain_ref, shift_ref, out_ref):
    half = near.shape[-1]
    blocks = [
        (ref, pl.multiple_of((chip_of() ^ flip) * half, half)) for flip, ref in enumerate((near, far))
    ]
    normalize(blocks, gain_ref, shift_ref, out_ref)


def half_kernel(
    near, far, gain_ref, shift_ref, w_ref, cos_ref, sin_ref, proj_ref, normed_ref
):
    split_normalize(near, far, gain_ref, shift_ref, normed_ref)
    places = [frame_of(i) for i in range(SHARES)]
    project(normed_ref, places, w_ref, cos_ref, sin_ref, proj_ref)


def split_temporal_kernel(
    own_proj_ref, near, far, gain_ref, shift_ref, w_ref, cos_ref, sin_ref,
    own_ref, other_ref, normed_ref, proj_ref,
):
    split_normalize(near, far, gain_ref, shift_ref, normed_ref)
    places = [frame_of(SHARES + i) for i in range(SHARES)]
    project(normed_ref, places, w_ref, cos_ref, sin_ref, proj_ref)
    split_mix(own_proj_ref, proj_ref, own_ref, other_ref)


def split_mix(own_proj_ref, proj_ref, own_ref, other_ref):
    count = own_ref.shape[0] // SHARES

    def write(i, low, head, value):
        ref = own_ref if i < SHARES else other_ref
        start = (i % SHARES) * count + low
        ref[start : start + value.shape[0], head] = value

    spans = [(ref, i * count) for ref in (own_proj_ref, proj_ref) for i in range(SHARES)]
    mix(spans, count, write)


def centred(rows, gain):
    values = rows.astype(jnp.float32)
    total = jnp.sum(values, axis=-1, keepdims=True)
    square = jnp.sum(values * values, axis=-1, keepdims=True)
    return total, square, ((values - total / rows.shape[-1]) * gain).astype(jnp.bfloat16)


def half_lanes(features, flip):
    half = features // 2
    return pl.ds(pl.multiple_of((chip_of() ^ flip) * half, half), half)


def near_kernel(
    own_ref, other_ref, gain_ref, shift_ref, w_ref,
    own_acc_ref, other_acc_ref, own_total_ref, other_total_ref, own_square_ref, other_square_ref,
    fixed_ref,
):
    features = w_ref.shape[0]
    near = half_lanes(features, 0)
    gain = 1.0 + gain_ref[:, near]
    for ref, acc_ref, total_ref, square_ref in (
        (own_ref, own_acc_ref, own_total_ref, own_square_ref),
        (other_ref, other_acc_ref, other_total_ref, other_square_ref),
    ):
        total_ref[...], square_ref[...], scaled = centred(ref[...], gain)
        acc_ref[...] = dot(scaled, w_ref[near, :])
    shifted = 0.0
    for flip in range(2):
        lanes = half_lanes(features, flip)
        rows = []
        for row in (1.0 + gain_ref[:, lanes], shift_ref[:, lanes]):
            high = row.astype(jnp.bfloat16).astype(jnp.float32)
            rows += [high, row - high]
        rows.append(jnp.zeros((GROUP - len(rows), rows[0].shape[-1]), jnp.float32))
        product = dot(jnp.concatenate(rows, axis=0).astype(jnp.bfloat16), w_ref[lanes, :])
        fixed_ref[flip : flip + 1, :] = product[0:1] + product[1:2]
        shifted += product[2:3] + product[3:4]
    fixed_ref[2:3, :] = shifted
    fixed_ref[3:, :] = jnp.zeros((fixed_ref.shape[0] - 3, fixed_ref.shape[1]), jnp.float32)


def join_halves(
    far_ref, acc_ref, total_ref, square_ref, fixed_ref, gain_ref, w_ref, cos_ref, sin_ref,
    proj_ref, pieces,
):
    features = w_ref.shape[0]
    half = features // 2
    far = half_lanes(features, 1)
    total, square, scaled = centred(far_ref[...], 1.0 + gain_ref[:, far])
    near_total = total_ref[...]
    mean = (near_total + total) / features
    rate = lax.rsqrt((square_ref[...] + square) / features - mean * mean + EPSILON)
    acc = acc_ref[...] + dot(scaled, w_ref[far, :])
    acc += (near_total / half - mean) * fixed_ref[0:1, :] + (total / half - mean) * fixed_ref[1:2, :]
    places = [frame_of(i) for i in pieces]
    turn(acc * rate + fixed_ref[2:3, :], places, cos_ref, sin_ref, proj_ref)


def own_far_kernel(*refs):
    join_halves(*refs, OWN)


def other_far_kernel(own_proj_ref, *refs):
    *inputs, own_ref, other_ref, proj_ref = refs
    join_halves(*inputs, proj_ref, OTHER)
    split_mix(own_proj_ref, proj_ref, own_ref, other_ref)


def pack_kernel(*refs):
    block_refs, out_refs = refs[:-SHARES], refs[-SHARES:]
    for i, out_ref in enumerate(out_refs):
        start = 0
        for ref in block_refs:
            count = ref.shape[0] // SHARES
            out_ref[start : start + count] = ref[i * count : (i + 1) * count]
            start += count


def unpack_kernel(*refs):
    *piece_refs, out_ref = refs
    count = piece_refs[0].shape[0] // 2
    for i, ref in enumerate(piece_refs):
        out_ref[i * count : (i + 1) * count] = ref[count:]


def place_updated_kernel(*refs, chunks):
    *block_refs, out_ref = refs
    for (first, rows), own_ref, other_ref in zip(chunks, block_refs[::2], block_refs[1::2]):
        count = rows // (2 * SHARES)
        for i in range(2 * SHARES):
            ref = own_ref if i < SHARES else other_ref
            start = (i % SHARES) * count
            out_ref[piece_span(first, count, i), :] = ref[start : start + count, :]


def place_mixed_kernel(*refs, chunks):
    *own_refs, other_ref, out_ref = refs
    size = own_refs[0].shape[0] // 2
    start = 0
    for first, rows in chunks:
        count = rows // (2 * SHARES)
        for i in range(SHARES):
            out_ref[piece_span(first, count, i), :] = own_refs[i][start : start + count, :]
            low = i * size + start
            out_ref[piece_span(first, count, SHARES + i), :] = other_ref[low : low + count, :]
        start += count


def swap(value, axis, size, k):
    return lax.ppermute(value, axis, [(i, i ^ k) for i in range(size)])


def rotation_tables(frames):
    rates = 10000.0 ** (-2.0 * np.arange(HEAD_DIM // 2, dtype=np.float32) / HEAD_DIM)
    angles = np.arange(frames, dtype=np.float32)[:, None] * rates.astype(np.float32)
    cosine, sine = np.cos(angles), np.sin(angles)
    return (
        jnp.asarray(np.concatenate([cosine, cosine], axis=1), jnp.float32),
        jnp.asarray(np.concatenate([-sine, sine], axis=1), jnp.float32),
    )


def piece_pairs(n_seq, n_mlp, index):
    return [
        (s * n_mlp + m, (s ^ PARTNERS[m % 2][index]) * n_mlp + m)
        for s in range(n_seq)
        for m in range(n_mlp)
    ]


def in_hbm(array):
    return pltpu.with_memory_space_constraint(array, pltpu.HBM)


def after(value, *others):
    return lax.optimization_barrier((value,) + others)[0]


def split_on_device(
    residual, spatial_qkv, spatial_out, temporal_qkv, shift, scale, gate, *, n_seq, n_mlp
):
    frames, patches, share = residual.shape
    width = spatial_qkv.shape[-1]
    features = share * n_mlp
    both = 2 * share
    tokens = frames * patches
    bf16, f32 = jnp.bfloat16, jnp.float32
    flat_residual = residual.reshape(tokens, share)
    qkv = spatial_qkv.transpose(2, 0, 1, 3).reshape(3, tokens, width)
    gate_row = gate.reshape(1, features)
    gain_row, shift_row = scale.reshape(1, features), shift.reshape(1, features)
    cosine, sine = rotation_tables(n_seq)

    def shape(rows, columns, kind=bf16):
        return jax.ShapeDtypeStruct((rows, columns), kind)

    def send_pieces(pieces):
        return [
            lax.ppermute(piece, ("seq", "mlp"), piece_pairs(n_seq, n_mlp, i))
            for i, piece in enumerate(pieces)
        ]

    once = jnp.minimum(lax.axis_index("seq") + 1, 1)

    chunks = []
    first = 0
    for rows in CHUNK_ROWS:
        chunks.append((first, rows))
        first += rows

    (first0, rows0), (first1, rows1) = chunks
    half0, half1 = rows0 // 2, rows1 // 2
    other_heads, message, *held = call(
        functools.partial(first_spatial_kernel, first=first0),
        [
            shape(half0, width),
            shape(half0, both),
            pltpu.VMEM((width, both), bf16),
            pltpu.VMEM((1, both), f32),
            pltpu.VMEM(qkv.shape, bf16),
        ],
        inputs=3,
        far=3,
        scratch=(pltpu.SemaphoreType.DMA((4,)),),
    )(*(in_hbm(one) for one in (qkv, spatial_out, gate_row)))
    message = swap(message, "mlp", n_mlp, 1)
    own_heads, far_term = call(
        functools.partial(term_kernel, first=first0),
        [shape(half0, width), shape(half0, both, f32)],
        inputs=3,
    )(*held)
    sent = call(add_kernel, shape(half0, both), inputs=2)(far_term, message)
    arrived0 = swap(sent, "mlp", n_mlp, 2)

    def rest(own_heads, other_heads, *operands):
        message, far_term, base0, near0, base1, near1 = call(
            functools.partial(rest_kernel, firsts=(first0, first1)),
            [
                shape(half1, both),
                shape(half1, both, f32),
                shape(half0, both, f32),
                shape(half0, both),
                shape(half1, both, f32),
                shape(half1, both),
            ],
            inputs=6,
            far=4,
            scratch=(
                pltpu.VMEM((rows1, width), bf16),
                *(pltpu.VMEM(one.shape, one.dtype) for one in operands),
                pltpu.SemaphoreType.DMA((4,)),
            ),
        )(own_heads, other_heads, *(in_hbm(one) for one in operands))
        message, near0, near1 = (swap(one, "mlp", n_mlp, 1) for one in (message, near0, near1))
        sent = call(add_kernel, shape(half1, both), inputs=2)(far_term, message)
        base0, base1 = (
            call(add_kernel, shape(*base.shape, f32), inputs=2)(base, near)
            for base, near in ((base0, near0), (base1, near1))
        )
        return sent, base0, base1

    def nothing(*_):
        return (
            jnp.zeros((half1, both), bf16),
            jnp.zeros((half0, both), f32),
            jnp.zeros((half1, both), f32),
        )

    sent, base0, base1 = lax.cond(
        once > 0,
        rest,
        nothing,
        after(own_heads, sent),
        other_heads,
        qkv,
        spatial_out,
        gate_row,
        flat_residual,
    )
    arrived1 = swap(sent, "mlp", n_mlp, 2)
    arrived0 = after(arrived0, sent)

    def update(rows, base, arrived):
        half = rows // 2
        own, other, *pieces = call(
            update_kernel,
            [shape(half, share)] * 2 + [shape(half // SHARES, both)] * SHARES,
            inputs=2,
        )(base, arrived)
        return [own, swap(other, "mlp", n_mlp, 1)], pieces

    blocks0, pieces = update(rows0, base0, arrived0)
    pieces = lax.fori_loop(0, once, lambda _, pieces: send_pieces(pieces), pieces)
    near0 = jnp.concatenate(pieces, axis=0)
    blocks1, pieces = update(rows1, base1, after(arrived1, near0))

    def last_exchange(temporal_qkv, *pieces):
        return (*send_pieces(pieces), hold_weights(temporal_qkv))

    def no_exchange(temporal_qkv, *pieces):
        return (*pieces, jnp.zeros((features, 3 * width), bf16))

    *pieces, weights = lax.cond(once > 0, last_exchange, no_exchange, temporal_qkv, *pieces)
    nears = [near0, jnp.concatenate(pieces, axis=0)]
    blocks = blocks0 + blocks1

    own_mixed, other_mixed = [], []
    for (first, rows), near in zip(chunks, nears):
        half = rows // 2
        far = swap(near, "mlp", n_mlp, 2)
        other_near = swap(near, "mlp", n_mlp, 1)
        if not own_mixed:
            far = after(far, *nears)
        else:
            updated = call(
                functools.partial(place_updated_kernel, chunks=chunks),
                shape(tokens, share),
                inputs=len(blocks),
            )(*blocks)
            line = jax.ShapeDtypeStruct((half, 1), f32)
            own_acc, other_acc, own_total, other_total, own_square, other_square, fixed = call(
                near_kernel,
                [shape(half, 3 * width, f32)] * 2 + [line] * 4 + [shape(8, 3 * width, f32)],
                inputs=5,
            )(near, other_near, gain_row, shift_row, weights)
            far = after(far, other_mixed[-1], updated, fixed)
        other_far = swap(far, "mlp", n_mlp, 1)
        if own_mixed:
            rest_in = (fixed, gain_row, weights, cosine, sine)
            own_proj = call(own_far_kernel, shape(half, 3 * width), inputs=9)(
                far, own_acc, own_total, own_square, *rest_in
            )
            own, other = call(
                other_far_kernel,
                [shape(half, width)] * 2,
                inputs=10,
                scratch=(pltpu.VMEM((half, 3 * width), bf16),),
            )(own_proj, other_far, other_acc, other_total, other_square, *rest_in)
        else:
            rest_in = (gain_row, shift_row, weights, cosine, sine)
            own_proj = call(
                half_kernel,
                shape(half, 3 * width),
                inputs=7,
                scratch=(pltpu.VMEM((half, features), bf16),),
            )(near, far, *rest_in)
            own, other = call(
                split_temporal_kernel,
                [shape(half, width)] * 2,
                inputs=8,
                scratch=(
                    pltpu.VMEM((half, features), bf16),
                    pltpu.VMEM((half, 3 * width), bf16),
                ),
            )(own_proj, other_near, other_far, *rest_in)
        own_mixed.append(own)
        other_mixed.append(swap(other, "mlp", n_mlp, 1))
    packed = call(
        pack_kernel, [shape(2 * tokens // (2 * SHARES), width)] * SHARES, inputs=2 * len(chunks)
    )(*own_mixed, *other_mixed)
    pieces = send_pieces(packed)
    others = call(unpack_kernel, shape(tokens // 2, width), inputs=SHARES)(*pieces)
    results = pieces + [swap(others, "mlp", n_mlp, 1)]
    result = call(
        functools.partial(place_mixed_kernel, chunks=chunks),
        shape(tokens, width),
        inputs=len(results),
    )(*results)
    return updated.reshape(frames, patches, share), result.reshape(frames, patches, width)


def heads_kernel(qkv_ref, out_ref):
    for lane in range(0, out_ref.shape[-1], HEAD_DIM):
        head = slice(lane, lane + HEAD_DIM)
        (out_ref[:, head],) = attend([tuple(qkv_ref[part, :, head] for part in range(3))])


def columns_kernel(own_ref, other_ref, own_w_ref, other_w_ref, gate_ref, out_ref):
    term = dot(own_ref[...], own_w_ref[...]) + dot(other_ref[...], other_w_ref[...])
    out_ref[...] = (term * gate_ref[...]).astype(out_ref.dtype)


def temporal_kernel(
    u0, u1, u2, u3, gain_ref, shift_ref, w_ref, cos_ref, sin_ref, out_ref, normed_ref, proj_ref
):
    share = u0.shape[-1]
    frames = cos_ref.shape[0]
    count = out_ref.shape[0] // frames
    blocks = [
        (ref, pl.multiple_of((lax.axis_index("mlp") ^ k) * share, share))
        for k, ref in enumerate((u0, u1, u2, u3))
    ]
    normalize(blocks, gain_ref, shift_ref, normed_ref)
    project(normed_ref, range(frames), w_ref, cos_ref, sin_ref, proj_ref)

    def write(f, low, head, value):
        start = f * count + low
        out_ref[start : start + value.shape[0], head] = value

    mix([(proj_ref, f * count) for f in range(frames)], count, write)


def on_device(
    residual, spatial_qkv, spatial_out, temporal_qkv, shift, scale, gate, *, n_seq, n_mlp
):
    frames, patches, share = residual.shape
    width = spatial_qkv.shape[-1]
    features = share * n_mlp
    rows = frames * patches
    count = rows // n_seq
    mlp = lax.axis_index("mlp")
    bf16, f32 = jnp.bfloat16, jnp.float32
    qkv = spatial_qkv.transpose(2, 0, 1, 3).reshape(3, rows, width)
    gate_row = gate.reshape(1, features)

    def columns(array, block):
        return lax.dynamic_slice_in_dim(array, block * share, share, 1)

    heads = call(heads_kernel, jax.ShapeDtypeStruct((rows, width), bf16), inputs=1)(qkv)
    others = swap(heads, "mlp", n_mlp, 1)

    def term(block, kind):
        other_w = swap(columns(spatial_out, block ^ 1), "mlp", n_mlp, 1)
        return call(columns_kernel, jax.ShapeDtypeStruct((rows, share), kind), inputs=5)(
            heads, others, columns(spatial_out, block), other_w, columns(gate_row, block)
        )

    arrived = swap(term(mlp ^ 2, bf16), "mlp", n_mlp, 2)
    branch = term(mlp, f32) + arrived.astype(f32)
    updated = (residual.reshape(rows, share).astype(f32) + branch).astype(bf16)
    mine = lax.all_to_all(
        updated.reshape(n_seq, count, share), "seq", 0, 0, tiled=True
    ).reshape(rows, share)
    across = swap(mine, "mlp", n_mlp, 2)
    mixed = call(
        temporal_kernel,
        jax.ShapeDtypeStruct((rows, width), bf16),
        inputs=9,
        scratch=(pltpu.VMEM((rows, features), bf16), pltpu.VMEM((rows, 3 * width), bf16)),
    )(
        mine,
        swap(mine, "mlp", n_mlp, 1),
        across,
        swap(across, "mlp", n_mlp, 1),
        scale.reshape(1, features),
        shift.reshape(1, features),
        hold_weights(temporal_qkv),
        *rotation_tables(n_seq),
    )
    result = lax.all_to_all(
        mixed.reshape(n_seq, count, width), "seq", 0, 0, tiled=True
    ).reshape(rows, width)
    return updated.reshape(frames, patches, share), result.reshape(frames, patches, width)


def solution(mesh):
    sizes = dict(n_seq=mesh.shape["seq"], n_mlp=mesh.shape["mlp"])
    split = sizes["n_seq"] == 2 * SHARES and sizes["n_mlp"] == 4
    return jax.shard_map(
        functools.partial(split_on_device if split else on_device, **sizes),
        mesh=mesh,
        in_specs=(
            P("seq", None, "mlp"),
            P("seq", None, None, "mlp"),
            P("mlp", None),
            P(None, None, "mlp"),
            P(),
            P(),
            P(),
        ),
        out_specs=(P("seq", None, "mlp"), P("seq", None, "mlp")),
        check_vma=False,
    )
```

```python
import functools
import math

import jax
import jax.numpy as jnp
import numpy as np
from jax import lax
from jax.experimental import pallas as pl
from jax.experimental.pallas import tpu as pltpu
from jax.sharding import PartitionSpec as P

HEAD_DIM = 128
EPSILON = 1e-06
GROUP = 16
MASKED = -1e30
VMEM_LIMIT = 16 * 1024 * 1024
EXP2_SCALE = math.log2(math.e) / math.sqrt(HEAD_DIM)
CHUNK_ROWS = (256, 256)
PARTNERS = ((4, 7, 2, 0), (5, 3, 6, 1))
SHARES = len(PARTNERS[0])


def call(body, outs, flops=0, moved=0, exps=0, inputs=0, scratch=(), far=0):
    return pl.pallas_call(
        body,
        out_shape=outs,
        in_specs=[pl.BlockSpec(memory_space=pltpu.VMEM)] * (inputs - far)
        + [pl.BlockSpec(memory_space=pltpu.HBM)] * far,
        scratch_shapes=list(scratch),
        compiler_params=pltpu.CompilerParams(vmem_limit_bytes=VMEM_LIMIT),
        cost_estimate=pl.CostEstimate(
            flops=int(flops), bytes_accessed=int(moved), transcendentals=int(exps)
        ),
    )


def dot(a, b):
    return jnp.dot(a, b, preferred_element_type=jnp.float32)


def dot_nt(a, b):
    return lax.dot_general(a, b, (((1,), (1,)), ((), ())), preferred_element_type=jnp.float32)


def attend(heads, same=None):
    logits = [dot_nt(query, key) for query, key, _ in heads]
    if same is not None:
        logits = [jnp.where(same, one, MASKED) for one in logits]
    tops = [jnp.max(one, axis=-1, keepdims=True) for one in logits]
    weights = [jnp.exp2((one - top) * EXP2_SCALE) for one, top in zip(logits, tops)]
    rates = [1.0 / jnp.sum(one, axis=-1, keepdims=True) for one in weights]
    return [
        (dot(one.astype(jnp.bfloat16), value) * rate).astype(jnp.bfloat16)
        for one, (_, _, value), rate in zip(weights, heads, rates)
    ]


def normalize(blocks, gain_ref, shift_ref, out_ref):
    features = out_ref.shape[-1]
    total, square = 0.0, 0.0
    for ref, _ in blocks:
        values = ref[...].astype(jnp.float32)
        total += jnp.sum(values, axis=-1, keepdims=True)
        square += jnp.sum(values * values, axis=-1, keepdims=True)
    mean = total / features
    rate = lax.rsqrt(square / features - mean * mean + EPSILON)
    for ref, start in blocks:
        lanes = pl.ds(start, ref.shape[-1])
        gain = 1.0 + gain_ref[:, lanes]
        out_ref[:, lanes] = (
            (ref[...].astype(jnp.float32) - mean) * rate * gain + shift_ref[:, lanes]
        ).astype(out_ref.dtype)


def turn(acc, places, cos_ref, sin_ref, proj_ref):
    turned_width = acc.shape[-1] // 3 * 2
    proj_ref[:, turned_width:] = acc[:, turned_width:].astype(proj_ref.dtype)
    count = acc.shape[0] // len(places)
    for i, place in enumerate(places):
        span = slice(i * count, (i + 1) * count)
        row = pl.ds(place, 1)
        cosine, sine = cos_ref[row, :], sin_ref[row, :]
        for lane in range(0, turned_width, HEAD_DIM):
            head = acc[span, lane : lane + HEAD_DIM]
            turned = pltpu.roll(head, HEAD_DIM // 2, 1)
            proj_ref[span, lane : lane + HEAD_DIM] = (head * cosine + turned * sine).astype(
                proj_ref.dtype
            )


def project(normed_ref, places, w_ref, cos_ref, sin_ref, proj_ref):
    turn(dot(normed_ref[...], w_ref[...]), places, cos_ref, sin_ref, proj_ref)


def mix(spans, count, write):
    frames = len(spans)
    width = spans[0][0].shape[-1] // 3
    step = GROUP if count % GROUP == 0 else count
    size = step * frames
    patch_of = lambda axis: lax.rem(lax.broadcasted_iota(jnp.int32, (size, size), axis), step)
    same = patch_of(0) == patch_of(1)

    def gathered(low, lane):
        head = slice(lane, lane + HEAD_DIM)
        ref = spans[0][0]
        if step == count and all(span == (ref, i * count) for i, span in enumerate(spans)):
            return ref[:, head]
        return jnp.concatenate(
            [ref[first + low : first + low + step, head] for ref, first in spans], axis=0
        )

    lanes = range(0, width, HEAD_DIM)
    units = [(low, lane) for low in range(0, count, step) for lane in lanes]
    heads = [tuple(gathered(low, part * width + lane) for part in range(3)) for low, lane in units]
    for (low, lane), mixed in zip(units, attend(heads, same)):
        for f in range(frames):
            write(f, low, slice(lane, lane + HEAD_DIM), mixed[f * step : (f + 1) * step])


def hold_kernel(w_far, out_ref, semaphores):
    width = w_far.shape[-1]
    copies = [
        pltpu.make_async_copy(
            w_far.at[part], out_ref.at[:, part * width : (part + 1) * width], semaphores.at[part]
        )
        for part in range(3)
    ]
    for copy in copies:
        copy.start()
    for copy in copies:
        copy.wait()


def hold_weights(temporal_qkv):
    features, parts, width = temporal_qkv.shape
    return pl.pallas_call(
        hold_kernel,
        out_shape=pltpu.VMEM((features, parts * width), temporal_qkv.dtype),
        in_specs=[pl.BlockSpec(memory_space=pltpu.HBM)],
        out_specs=pl.BlockSpec(memory_space=pltpu.VMEM),
        scratch_shapes=[pltpu.SemaphoreType.DMA((parts,))],
        compiler_params=pltpu.CompilerParams(vmem_limit_bytes=1024 * 1024),
        cost_estimate=pl.CostEstimate(flops=0, bytes_accessed=0, transcendentals=0),
    )(in_hbm(temporal_qkv.transpose(1, 0, 2)))


def core_of():
    return lax.rem(lax.axis_index("mlp"), 2)


def chip_of():
    return lax.div(lax.axis_index("mlp"), 2)


def frame_of(i):
    low, high = (PARTNERS[core][i % SHARES] for core in range(2))
    which = core_of() if i < SHARES else 1 - core_of()
    return lax.axis_index("seq") ^ (low + which * (high - low))


def piece_span(first, count, i):
    return pl.ds(pl.multiple_of(first + frame_of(i) * count, count), count)


OWN, OTHER, ALL = range(SHARES), range(SHARES, 2 * SHARES), range(2 * SHARES)


def piece_rows(ref, first, count, lanes, pieces=ALL):
    return jnp.concatenate([ref[piece_span(first, count, i), lanes] for i in pieces], axis=0)


def chip_columns(features, flip):
    half = features // 2
    return pl.ds(pl.multiple_of((chip_of() ^ flip) * half, half), half)


def spatial_heads(qkv_ref, heads_ref, first, pieces=ALL):
    rows, width = heads_ref.shape
    for lane in range(0, width, HEAD_DIM):
        head = slice(lane, lane + HEAD_DIM)
        query = piece_rows(qkv_ref.at[0], first, rows // len(pieces), head, pieces)
        (heads_ref[:, head],) = attend([(query, qkv_ref[1, :, head], qkv_ref[2, :, head])])


def first_spatial_kernel(
    qkv_far, w_far, gate_far, heads_ref, message_ref, w_ref, gate_ref, qkv_ref, semaphores, *, first
):
    far = chip_columns(w_far.shape[-1], 1)
    query = pl.ds(first, 2 * heads_ref.shape[0])
    moves = [
        (qkv_far.at[0, query], qkv_ref.at[0, query]),
        (qkv_far.at[1:], qkv_ref.at[1:]),
        (w_far.at[:, far], w_ref),
        (gate_far.at[:, far], gate_ref),
    ]
    copies = [pltpu.make_async_copy(*move, semaphores.at[i]) for i, move in enumerate(moves)]
    for copy in copies:
        copy.start()
    for copy in copies[:2]:
        copy.wait()
    spatial_heads(qkv_ref, heads_ref, first, OTHER)
    for copy in copies[2:]:
        copy.wait()
    term = dot(heads_ref[...], w_ref[...])
    message_ref[...] = (term * gate_ref[...]).astype(message_ref.dtype)


def term_kernel(w_ref, gate_ref, qkv_ref, heads_ref, out_ref, *, first):
    spatial_heads(qkv_ref, heads_ref, first, OWN)
    out_ref[...] = dot(heads_ref[...], w_ref[...]) * gate_ref[...]


def rest_kernel(
    own0_ref, other0_ref, qkv_far, w_far, gate_far, residual_far,
    message_ref, term_ref, base0_ref, near0_ref, base1_ref, near1_ref,
    heads1_ref, qkv_ref, w_ref, gate_ref, residual_ref, semaphores, *, firsts
):
    moves = [
        (qkv_far, qkv_ref), (w_far, w_ref), (gate_far, gate_ref), (residual_far, residual_ref)
    ]
    copies = [pltpu.make_async_copy(*move, semaphores.at[i]) for i, move in enumerate(moves)]
    for copy in copies:
        copy.start()
    copies[0].wait()
    spatial_heads(qkv_ref, heads1_ref, firsts[1])
    for copy in copies[1:]:
        copy.wait()
    half, both = message_ref.shape
    features = w_ref.shape[-1]
    far = chip_columns(features, 1)
    term = dot(heads1_ref[...], w_ref[:, far]) * gate_ref[:, far]
    term_ref[...] = term[:half]
    message_ref[...] = term[half:].astype(message_ref.dtype)
    share = both // 2
    heads0 = jnp.concatenate([own0_ref[...], other0_ref[...]], axis=0)
    for first, heads, base_ref, near_ref in (
        (firsts[0], heads0, base0_ref, near0_ref),
        (firsts[1], heads1_ref[...], base1_ref, near1_ref),
    ):
        size = base_ref.shape[0]
        for flip in range(2):
            place = pl.multiple_of((core_of() ^ flip) * share, share)
            lanes = pl.ds(pl.multiple_of(chip_of() * both + place, share), share)
            term = dot(heads, w_ref[:, lanes]) * gate_ref[:, lanes]
            if flip == 0:
                term += piece_rows(residual_ref, first, size // SHARES, slice(None)).astype(
                    jnp.float32
                )
            base_ref[:, pl.ds(place, share)] = term[:size]
            near_ref[:, pl.ds(place, share)] = term[size:].astype(near_ref.dtype)


def add_kernel(a_ref, b_ref, out_ref):
    out_ref[...] = (a_ref[...] + b_ref[...].astype(jnp.float32)).astype(out_ref.dtype)


def update_kernel(base_ref, arrived_ref, own_ref, other_ref, *piece_refs):
    updated = (base_ref[...] + arrived_ref[...].astype(jnp.float32)).astype(jnp.bfloat16)
    count = piece_refs[0].shape[0]
    for i, piece_ref in enumerate(piece_refs):
        piece_ref[...] = updated[i * count : (i + 1) * count]
    share = own_ref.shape[-1]
    left, right = updated[:, :share], updated[:, share:]
    core = core_of()
    own_ref[...] = jnp.where(core == 0, left, right)
    other_ref[...] = jnp.where(core == 0, right, left)


def split_normalize(near, far, gain_ref, shift_ref, out_ref):
    half = near.shape[-1]
    blocks = [
        (ref, pl.multiple_of((chip_of() ^ flip) * half, half)) for flip, ref in enumerate((near, far))
    ]
    normalize(blocks, gain_ref, shift_ref, out_ref)


def half_kernel(
    near, far, gain_ref, shift_ref, w_ref, cos_ref, sin_ref, proj_ref, normed_ref
):
    split_normalize(near, far, gain_ref, shift_ref, normed_ref)
    places = [frame_of(i) for i in range(SHARES)]
    project(normed_ref, places, w_ref, cos_ref, sin_ref, proj_ref)


def split_temporal_kernel(
    own_proj_ref, near, far, gain_ref, shift_ref, w_ref, cos_ref, sin_ref,
    own_ref, other_ref, normed_ref, proj_ref,
):
    split_normalize(near, far, gain_ref, shift_ref, normed_ref)
    places = [frame_of(SHARES + i) for i in range(SHARES)]
    project(normed_ref, places, w_ref, cos_ref, sin_ref, proj_ref)
    split_mix(own_proj_ref, proj_ref, own_ref, other_ref)


def split_mix(own_proj_ref, proj_ref, own_ref, other_ref):
    count = own_ref.shape[0] // SHARES

    def write(i, low, head, value):
        ref = own_ref if i < SHARES else other_ref
        start = (i % SHARES) * count + low
        ref[start : start + value.shape[0], head] = value

    spans = [(ref, i * count) for ref in (own_proj_ref, proj_ref) for i in range(SHARES)]
    mix(spans, count, write)


def centred(rows, gain):
    values = rows.astype(jnp.float32)
    total = jnp.sum(values, axis=-1, keepdims=True)
    square = jnp.sum(values * values, axis=-1, keepdims=True)
    return total, square, ((values - total / rows.shape[-1]) * gain).astype(jnp.bfloat16)


def half_lanes(features, flip):
    half = features // 2
    return pl.ds(pl.multiple_of((chip_of() ^ flip) * half, half), half)


def near_kernel(
    own_ref, other_ref, gain_ref, shift_ref, w_ref,
    own_acc_ref, other_acc_ref, own_total_ref, other_total_ref, own_square_ref, other_square_ref,
    fixed_ref,
):
    features = w_ref.shape[0]
    near = half_lanes(features, 0)
    gain = 1.0 + gain_ref[:, near]
    for ref, acc_ref, total_ref, square_ref in (
        (own_ref, own_acc_ref, own_total_ref, own_square_ref),
        (other_ref, other_acc_ref, other_total_ref, other_square_ref),
    ):
        total_ref[...], square_ref[...], scaled = centred(ref[...], gain)
        acc_ref[...] = dot(scaled, w_ref[near, :])
    shifted = 0.0
    for flip in range(2):
        lanes = half_lanes(features, flip)
        rows = []
        for row in (1.0 + gain_ref[:, lanes], shift_ref[:, lanes]):
            high = row.astype(jnp.bfloat16).astype(jnp.float32)
            rows += [high, row - high]
        rows.append(jnp.zeros((GROUP - len(rows), rows[0].shape[-1]), jnp.float32))
        product = dot(jnp.concatenate(rows, axis=0).astype(jnp.bfloat16), w_ref[lanes, :])
        fixed_ref[flip : flip + 1, :] = product[0:1] + product[1:2]
        shifted += product[2:3] + product[3:4]
    fixed_ref[2:3, :] = shifted
    fixed_ref[3:, :] = jnp.zeros((fixed_ref.shape[0] - 3, fixed_ref.shape[1]), jnp.float32)


def join_halves(
    far_ref, acc_ref, total_ref, square_ref, fixed_ref, gain_ref, w_ref, cos_ref, sin_ref,
    proj_ref, pieces,
):
    features = w_ref.shape[0]
    half = features // 2
    far = half_lanes(features, 1)
    total, square, scaled = centred(far_ref[...], 1.0 + gain_ref[:, far])
    near_total = total_ref[...]
    mean = (near_total + total) / features
    rate = lax.rsqrt((square_ref[...] + square) / features - mean * mean + EPSILON)
    acc = acc_ref[...] + dot(scaled, w_ref[far, :])
    acc += (near_total / half - mean) * fixed_ref[0:1, :] + (total / half - mean) * fixed_ref[1:2, :]
    places = [frame_of(i) for i in pieces]
    turn(acc * rate + fixed_ref[2:3, :], places, cos_ref, sin_ref, proj_ref)


def own_far_kernel(*refs):
    join_halves(*refs, OWN)


def other_far_kernel(own_proj_ref, *refs):
    *inputs, own_ref, other_ref, proj_ref = refs
    join_halves(*inputs, proj_ref, OTHER)
    split_mix(own_proj_ref, proj_ref, own_ref, other_ref)


def pack_kernel(*refs):
    block_refs, out_refs = refs[:-SHARES], refs[-SHARES:]
    for i, out_ref in enumerate(out_refs):
        start = 0
        for ref in block_refs:
            count = ref.shape[0] // SHARES
            out_ref[start : start + count] = ref[i * count : (i + 1) * count]
            start += count


def unpack_kernel(*refs):
    *piece_refs, out_ref = refs
    count = piece_refs[0].shape[0] // 2
    for i, ref in enumerate(piece_refs):
        out_ref[i * count : (i + 1) * count] = ref[count:]


def place_updated_kernel(*refs, chunks):
    *block_refs, out_ref = refs
    for (first, rows), own_ref, other_ref in zip(chunks, block_refs[::2], block_refs[1::2]):
        count = rows // (2 * SHARES)
        for i in range(2 * SHARES):
            ref = own_ref if i < SHARES else other_ref
            start = (i % SHARES) * count
            out_ref[piece_span(first, count, i), :] = ref[start : start + count, :]


def place_mixed_kernel(*refs, chunks):
    *own_refs, other_ref, out_ref = refs
    size = own_refs[0].shape[0] // 2
    start = 0
    for first, rows in chunks:
        count = rows // (2 * SHARES)
        for i in range(SHARES):
            out_ref[piece_span(first, count, i), :] = own_refs[i][start : start + count, :]
            low = i * size + start
            out_ref[piece_span(first, count, SHARES + i), :] = other_ref[low : low + count, :]
        start += count


def swap(value, axis, size, k):
    return lax.ppermute(value, axis, [(i, i ^ k) for i in range(size)])


def rotation_tables(frames):
    rates = 10000.0 ** (-2.0 * np.arange(HEAD_DIM // 2, dtype=np.float32) / HEAD_DIM)
    angles = np.arange(frames, dtype=np.float32)[:, None] * rates.astype(np.float32)
    cosine, sine = np.cos(angles), np.sin(angles)
    return (
        jnp.asarray(np.concatenate([cosine, cosine], axis=1), jnp.float32),
        jnp.asarray(np.concatenate([-sine, sine], axis=1), jnp.float32),
    )


def piece_pairs(n_seq, n_mlp, index):
    return [
        (s * n_mlp + m, (s ^ PARTNERS[m % 2][index]) * n_mlp + m)
        for s in range(n_seq)
        for m in range(n_mlp)
    ]


def in_hbm(array):
    return pltpu.with_memory_space_constraint(array, pltpu.HBM)


def after(value, *others):
    return lax.optimization_barrier((value,) + others)[0]


def split_on_device(
    residual, spatial_qkv, spatial_out, temporal_qkv, shift, scale, gate, *, n_seq, n_mlp
):
    frames, patches, share = residual.shape
    width = spatial_qkv.shape[-1]
    features = share * n_mlp
    both = 2 * share
    tokens = frames * patches
    bf16, f32 = jnp.bfloat16, jnp.float32
    flat_residual = residual.reshape(tokens, share)
    qkv = spatial_qkv.transpose(2, 0, 1, 3).reshape(3, tokens, width)
    gate_row = gate.reshape(1, features)
    gain_row, shift_row = scale.reshape(1, features), shift.reshape(1, features)
    cosine, sine = rotation_tables(n_seq)

    def shape(rows, columns, kind=bf16):
        return jax.ShapeDtypeStruct((rows, columns), kind)

    def send_pieces(pieces):
        return [
            lax.ppermute(piece, ("seq", "mlp"), piece_pairs(n_seq, n_mlp, i))
            for i, piece in enumerate(pieces)
        ]

    once = jnp.minimum(lax.axis_index("seq") + 1, 1)

    chunks = []
    first = 0
    for rows in CHUNK_ROWS:
        chunks.append((first, rows))
        first += rows

    (first0, rows0), (first1, rows1) = chunks
    half0, half1 = rows0 // 2, rows1 // 2
    other_heads, message, *held = call(
        functools.partial(first_spatial_kernel, first=first0),
        [
            shape(half0, width),
            shape(half0, both),
            pltpu.VMEM((width, both), bf16),
            pltpu.VMEM((1, both), f32),
            pltpu.VMEM(qkv.shape, bf16),
        ],
        inputs=3,
        far=3,
        scratch=(pltpu.SemaphoreType.DMA((4,)),),
    )(*(in_hbm(one) for one in (qkv, spatial_out, gate_row)))
    message = swap(message, "mlp", n_mlp, 1)
    own_heads, far_term = call(
        functools.partial(term_kernel, first=first0),
        [shape(half0, width), shape(half0, both, f32)],
        inputs=3,
    )(*held)
    sent = call(add_kernel, shape(half0, both), inputs=2)(far_term, message)
    arrived0 = swap(sent, "mlp", n_mlp, 2)

    def rest(own_heads, other_heads, *operands):
        message, far_term, base0, near0, base1, near1 = call(
            functools.partial(rest_kernel, firsts=(first0, first1)),
            [
                shape(half1, both),
                shape(half1, both, f32),
                shape(half0, both, f32),
                shape(half0, both),
                shape(half1, both, f32),
                shape(half1, both),
            ],
            inputs=6,
            far=4,
            scratch=(
                pltpu.VMEM((rows1, width), bf16),
                *(pltpu.VMEM(one.shape, one.dtype) for one in operands),
                pltpu.SemaphoreType.DMA((4,)),
            ),
        )(own_heads, other_heads, *(in_hbm(one) for one in operands))
        message, near0, near1 = (swap(one, "mlp", n_mlp, 1) for one in (message, near0, near1))
        sent = call(add_kernel, shape(half1, both), inputs=2)(far_term, message)
        base0, base1 = (
            call(add_kernel, shape(*base.shape, f32), inputs=2)(base, near)
            for base, near in ((base0, near0), (base1, near1))
        )
        return sent, base0, base1

    def nothing(*_):
        return (
            jnp.zeros((half1, both), bf16),
            jnp.zeros((half0, both), f32),
            jnp.zeros((half1, both), f32),
        )

    sent, base0, base1 = lax.cond(
        once > 0,
        rest,
        nothing,
        after(own_heads, sent),
        other_heads,
        qkv,
        spatial_out,
        gate_row,
        flat_residual,
    )
    arrived1 = swap(sent, "mlp", n_mlp, 2)
    arrived0 = after(arrived0, sent)

    def update(rows, base, arrived):
        half = rows // 2
        own, other, *pieces = call(
            update_kernel,
            [shape(half, share)] * 2 + [shape(half // SHARES, both)] * SHARES,
            inputs=2,
        )(base, arrived)
        return [own, swap(other, "mlp", n_mlp, 1)], pieces

    blocks0, pieces = update(rows0, base0, arrived0)
    pieces = lax.fori_loop(0, once, lambda _, pieces: send_pieces(pieces), pieces)
    near0 = jnp.concatenate(pieces, axis=0)
    blocks1, pieces = update(rows1, base1, after(arrived1, near0))

    def last_exchange(temporal_qkv, near, *pieces):
        far = swap(near, "mlp", n_mlp, 2)
        return (*send_pieces(pieces), far, hold_weights(temporal_qkv))

    def no_exchange(temporal_qkv, near, *pieces):
        return (*pieces, near, jnp.zeros((features, 3 * width), bf16))

    *pieces, far0, weights = lax.cond(
        once > 0, last_exchange, no_exchange, temporal_qkv, near0, *pieces
    )
    nears = [near0, jnp.concatenate(pieces, axis=0)]
    blocks = blocks0 + blocks1

    own_mixed, other_mixed = [], []
    for (first, rows), near in zip(chunks, nears):
        half = rows // 2
        far = swap(near, "mlp", n_mlp, 2) if own_mixed else far0
        other_near = swap(near, "mlp", n_mlp, 1)
        if not own_mixed:
            far = after(far, *nears)
        else:
            updated = call(
                functools.partial(place_updated_kernel, chunks=chunks),
                shape(tokens, share),
                inputs=len(blocks),
            )(*blocks)
            line = jax.ShapeDtypeStruct((half, 1), f32)
            own_acc, other_acc, own_total, other_total, own_square, other_square, fixed = call(
                near_kernel,
                [shape(half, 3 * width, f32)] * 2 + [line] * 4 + [shape(8, 3 * width, f32)],
                inputs=5,
            )(near, other_near, gain_row, shift_row, weights)
            far = after(far, other_mixed[-1], updated, fixed)
        other_far = swap(far, "mlp", n_mlp, 1)
        if own_mixed:
            rest_in = (fixed, gain_row, weights, cosine, sine)
            own_proj = call(own_far_kernel, shape(half, 3 * width), inputs=9)(
                far, own_acc, own_total, own_square, *rest_in
            )
            own, other = call(
                other_far_kernel,
                [shape(half, width)] * 2,
                inputs=10,
                scratch=(pltpu.VMEM((half, 3 * width), bf16),),
            )(own_proj, other_far, other_acc, other_total, other_square, *rest_in)
        else:
            rest_in = (gain_row, shift_row, weights, cosine, sine)
            own_proj = call(
                half_kernel,
                shape(half, 3 * width),
                inputs=7,
                scratch=(pltpu.VMEM((half, features), bf16),),
            )(near, far, *rest_in)
            own, other = call(
                split_temporal_kernel,
                [shape(half, width)] * 2,
                inputs=8,
                scratch=(
                    pltpu.VMEM((half, features), bf16),
                    pltpu.VMEM((half, 3 * width), bf16),
                ),
            )(own_proj, other_near, other_far, *rest_in)
        own_mixed.append(own)
        other_mixed.append(swap(other, "mlp", n_mlp, 1))
    packed = call(
        pack_kernel, [shape(2 * tokens // (2 * SHARES), width)] * SHARES, inputs=2 * len(chunks)
    )(*own_mixed, *other_mixed)
    pieces = send_pieces(packed)
    others = call(unpack_kernel, shape(tokens // 2, width), inputs=SHARES)(*pieces)
    results = pieces + [swap(others, "mlp", n_mlp, 1)]
    result = call(
        functools.partial(place_mixed_kernel, chunks=chunks),
        shape(tokens, width),
        inputs=len(results),
    )(*results)
    return updated.reshape(frames, patches, share), result.reshape(frames, patches, width)


def heads_kernel(qkv_ref, out_ref):
    for lane in range(0, out_ref.shape[-1], HEAD_DIM):
        head = slice(lane, lane + HEAD_DIM)
        (out_ref[:, head],) = attend([tuple(qkv_ref[part, :, head] for part in range(3))])


def columns_kernel(own_ref, other_ref, own_w_ref, other_w_ref, gate_ref, out_ref):
    term = dot(own_ref[...], own_w_ref[...]) + dot(other_ref[...], other_w_ref[...])
    out_ref[...] = (term * gate_ref[...]).astype(out_ref.dtype)


def temporal_kernel(
    u0, u1, u2, u3, gain_ref, shift_ref, w_ref, cos_ref, sin_ref, out_ref, normed_ref, proj_ref
):
    share = u0.shape[-1]
    frames = cos_ref.shape[0]
    count = out_ref.shape[0] // frames
    blocks = [
        (ref, pl.multiple_of((lax.axis_index("mlp") ^ k) * share, share))
        for k, ref in enumerate((u0, u1, u2, u3))
    ]
    normalize(blocks, gain_ref, shift_ref, normed_ref)
    project(normed_ref, range(frames), w_ref, cos_ref, sin_ref, proj_ref)

    def write(f, low, head, value):
        start = f * count + low
        out_ref[start : start + value.shape[0], head] = value

    mix([(proj_ref, f * count) for f in range(frames)], count, write)


def on_device(
    residual, spatial_qkv, spatial_out, temporal_qkv, shift, scale, gate, *, n_seq, n_mlp
):
    frames, patches, share = residual.shape
    width = spatial_qkv.shape[-1]
    features = share * n_mlp
    rows = frames * patches
    count = rows // n_seq
    mlp = lax.axis_index("mlp")
    bf16, f32 = jnp.bfloat16, jnp.float32
    qkv = spatial_qkv.transpose(2, 0, 1, 3).reshape(3, rows, width)
    gate_row = gate.reshape(1, features)

    def columns(array, block):
        return lax.dynamic_slice_in_dim(array, block * share, share, 1)

    heads = call(heads_kernel, jax.ShapeDtypeStruct((rows, width), bf16), inputs=1)(qkv)
    others = swap(heads, "mlp", n_mlp, 1)

    def term(block, kind):
        other_w = swap(columns(spatial_out, block ^ 1), "mlp", n_mlp, 1)
        return call(columns_kernel, jax.ShapeDtypeStruct((rows, share), kind), inputs=5)(
            heads, others, columns(spatial_out, block), other_w, columns(gate_row, block)
        )

    arrived = swap(term(mlp ^ 2, bf16), "mlp", n_mlp, 2)
    branch = term(mlp, f32) + arrived.astype(f32)
    updated = (residual.reshape(rows, share).astype(f32) + branch).astype(bf16)
    mine = lax.all_to_all(
        updated.reshape(n_seq, count, share), "seq", 0, 0, tiled=True
    ).reshape(rows, share)
    across = swap(mine, "mlp", n_mlp, 2)
    mixed = call(
        temporal_kernel,
        jax.ShapeDtypeStruct((rows, width), bf16),
        inputs=9,
        scratch=(pltpu.VMEM((rows, features), bf16), pltpu.VMEM((rows, 3 * width), bf16)),
    )(
        mine,
        swap(mine, "mlp", n_mlp, 1),
        across,
        swap(across, "mlp", n_mlp, 1),
        scale.reshape(1, features),
        shift.reshape(1, features),
        hold_weights(temporal_qkv),
        *rotation_tables(n_seq),
    )
    result = lax.all_to_all(
        mixed.reshape(n_seq, count, width), "seq", 0, 0, tiled=True
    ).reshape(rows, width)
    return updated.reshape(frames, patches, share), result.reshape(frames, patches, width)


def solution(mesh):
    sizes = dict(n_seq=mesh.shape["seq"], n_mlp=mesh.shape["mlp"])
    split = sizes["n_seq"] == 2 * SHARES and sizes["n_mlp"] == 4
    return jax.shard_map(
        functools.partial(split_on_device if split else on_device, **sizes),
        mesh=mesh,
        in_specs=(
            P("seq", None, "mlp"),
            P("seq", None, None, "mlp"),
            P("mlp", None),
            P(None, None, "mlp"),
            P(),
            P(),
            P(),
        ),
        out_specs=(P("seq", None, "mlp"), P("seq", None, "mlp")),
        check_vma=False,
    )
```

```python
import functools
import math

import jax
import jax.numpy as jnp
import numpy as np
from jax import lax
from jax.experimental import pallas as pl
from jax.experimental.pallas import tpu as pltpu
from jax.sharding import PartitionSpec as P

HEAD_DIM = 128
EPSILON = 1e-06
GROUP = 16
MASKED = -1e30
VMEM_LIMIT = 16 * 1024 * 1024
EXP2_SCALE = math.log2(math.e) / math.sqrt(HEAD_DIM)
CHUNK_ROWS = (256, 256)
PARTNERS = ((4, 7, 2, 0), (5, 3, 6, 1))
SHARES = len(PARTNERS[0])


def call(body, outs, flops=0, moved=0, exps=0, inputs=0, scratch=(), far=0):
    return pl.pallas_call(
        body,
        out_shape=outs,
        in_specs=[pl.BlockSpec(memory_space=pltpu.VMEM)] * (inputs - far)
        + [pl.BlockSpec(memory_space=pltpu.HBM)] * far,
        scratch_shapes=list(scratch),
        compiler_params=pltpu.CompilerParams(vmem_limit_bytes=VMEM_LIMIT),
        cost_estimate=pl.CostEstimate(
            flops=int(flops), bytes_accessed=int(moved), transcendentals=int(exps)
        ),
    )


def dot(a, b):
    return jnp.dot(a, b, preferred_element_type=jnp.float32)


def dot_nt(a, b):
    return lax.dot_general(a, b, (((1,), (1,)), ((), ())), preferred_element_type=jnp.float32)


def attend(heads, same=None):
    logits = [dot_nt(query, key) for query, key, _ in heads]
    if same is not None:
        logits = [jnp.where(same, one, MASKED) for one in logits]
    tops = [jnp.max(one, axis=-1, keepdims=True) for one in logits]
    weights = [jnp.exp2((one - top) * EXP2_SCALE) for one, top in zip(logits, tops)]
    rates = [1.0 / jnp.sum(one, axis=-1, keepdims=True) for one in weights]
    return [
        (dot(one.astype(jnp.bfloat16), value) * rate).astype(jnp.bfloat16)
        for one, (_, _, value), rate in zip(weights, heads, rates)
    ]


def normalize(blocks, gain_ref, shift_ref, out_ref):
    features = out_ref.shape[-1]
    total, square = 0.0, 0.0
    for ref, _ in blocks:
        values = ref[...].astype(jnp.float32)
        total += jnp.sum(values, axis=-1, keepdims=True)
        square += jnp.sum(values * values, axis=-1, keepdims=True)
    mean = total / features
    rate = lax.rsqrt(square / features - mean * mean + EPSILON)
    for ref, start in blocks:
        lanes = pl.ds(start, ref.shape[-1])
        gain = 1.0 + gain_ref[:, lanes]
        out_ref[:, lanes] = (
            (ref[...].astype(jnp.float32) - mean) * rate * gain + shift_ref[:, lanes]
        ).astype(out_ref.dtype)


def turn(acc, places, cos_ref, sin_ref, proj_ref):
    turned_width = acc.shape[-1] // 3 * 2
    proj_ref[:, turned_width:] = acc[:, turned_width:].astype(proj_ref.dtype)
    count = acc.shape[0] // len(places)
    for i, place in enumerate(places):
        span = slice(i * count, (i + 1) * count)
        row = pl.ds(place, 1)
        cosine, sine = cos_ref[row, :], sin_ref[row, :]
        for lane in range(0, turned_width, HEAD_DIM):
            head = acc[span, lane : lane + HEAD_DIM]
            turned = pltpu.roll(head, HEAD_DIM // 2, 1)
            proj_ref[span, lane : lane + HEAD_DIM] = (head * cosine + turned * sine).astype(
                proj_ref.dtype
            )


def project(normed_ref, places, w_ref, cos_ref, sin_ref, proj_ref):
    turn(dot(normed_ref[...], w_ref[...]), places, cos_ref, sin_ref, proj_ref)


def mix(spans, count, write):
    frames = len(spans)
    width = spans[0][0].shape[-1] // 3
    step = GROUP if count % GROUP == 0 else count
    size = step * frames
    patch_of = lambda axis: lax.rem(lax.broadcasted_iota(jnp.int32, (size, size), axis), step)
    same = patch_of(0) == patch_of(1)

    def gathered(low, lane):
        head = slice(lane, lane + HEAD_DIM)
        ref = spans[0][0]
        if step == count and all(span == (ref, i * count) for i, span in enumerate(spans)):
            return ref[:, head]
        return jnp.concatenate(
            [ref[first + low : first + low + step, head] for ref, first in spans], axis=0
        )

    lanes = range(0, width, HEAD_DIM)
    units = [(low, lane) for low in range(0, count, step) for lane in lanes]
    heads = [tuple(gathered(low, part * width + lane) for part in range(3)) for low, lane in units]
    for (low, lane), mixed in zip(units, attend(heads, same)):
        for f in range(frames):
            write(f, low, slice(lane, lane + HEAD_DIM), mixed[f * step : (f + 1) * step])


def hold_kernel(w_far, out_ref, semaphores):
    width = w_far.shape[-1]
    copies = [
        pltpu.make_async_copy(
            w_far.at[part], out_ref.at[:, part * width : (part + 1) * width], semaphores.at[part]
        )
        for part in range(3)
    ]
    for copy in copies:
        copy.start()
    for copy in copies:
        copy.wait()


def hold_weights(temporal_qkv):
    features, parts, width = temporal_qkv.shape
    return pl.pallas_call(
        hold_kernel,
        out_shape=pltpu.VMEM((features, parts * width), temporal_qkv.dtype),
        in_specs=[pl.BlockSpec(memory_space=pltpu.HBM)],
        out_specs=pl.BlockSpec(memory_space=pltpu.VMEM),
        scratch_shapes=[pltpu.SemaphoreType.DMA((parts,))],
        compiler_params=pltpu.CompilerParams(vmem_limit_bytes=1024 * 1024),
        cost_estimate=pl.CostEstimate(flops=0, bytes_accessed=0, transcendentals=0),
    )(in_hbm(temporal_qkv.transpose(1, 0, 2)))


def core_of():
    return lax.rem(lax.axis_index("mlp"), 2)


def chip_of():
    return lax.div(lax.axis_index("mlp"), 2)


def frame_of(i):
    low, high = (PARTNERS[core][i % SHARES] for core in range(2))
    which = core_of() if i < SHARES else 1 - core_of()
    return lax.axis_index("seq") ^ (low + which * (high - low))


def piece_span(first, count, i):
    return pl.ds(pl.multiple_of(first + frame_of(i) * count, count), count)


OWN, OTHER, ALL = range(SHARES), range(SHARES, 2 * SHARES), range(2 * SHARES)


def piece_rows(ref, first, count, lanes, pieces=ALL):
    return jnp.concatenate([ref[piece_span(first, count, i), lanes] for i in pieces], axis=0)


def chip_columns(features, flip):
    half = features // 2
    return pl.ds(pl.multiple_of((chip_of() ^ flip) * half, half), half)


def spatial_heads(qkv_ref, heads_ref, first, pieces=ALL):
    rows, width = heads_ref.shape
    for lane in range(0, width, HEAD_DIM):
        head = slice(lane, lane + HEAD_DIM)
        query = piece_rows(qkv_ref.at[0], first, rows // len(pieces), head, pieces)
        (heads_ref[:, head],) = attend([(query, qkv_ref[1, :, head], qkv_ref[2, :, head])])


def first_spatial_kernel(
    qkv_far, w_far, gate_far, heads_ref, message_ref, w_ref, gate_ref, qkv_ref, semaphores, *, first
):
    far = chip_columns(w_far.shape[-1], 1)
    query = pl.ds(first, 2 * heads_ref.shape[0])
    moves = [
        (qkv_far.at[0, query], qkv_ref.at[0, query]),
        (qkv_far.at[1:], qkv_ref.at[1:]),
        (w_far.at[:, far], w_ref),
        (gate_far.at[:, far], gate_ref),
    ]
    copies = [pltpu.make_async_copy(*move, semaphores.at[i]) for i, move in enumerate(moves)]
    for i in (2, 0, 1, 3):
        copies[i].start()
    for copy in copies[:2]:
        copy.wait()
    spatial_heads(qkv_ref, heads_ref, first, OTHER)
    for copy in copies[2:]:
        copy.wait()
    term = dot(heads_ref[...], w_ref[...])
    message_ref[...] = (term * gate_ref[...]).astype(message_ref.dtype)


def term_kernel(w_ref, gate_ref, qkv_ref, heads_ref, out_ref, *, first):
    spatial_heads(qkv_ref, heads_ref, first, OWN)
    out_ref[...] = dot(heads_ref[...], w_ref[...]) * gate_ref[...]


def rest_kernel(
    own0_ref, other0_ref, qkv_far, w_far, gate_far, residual_far,
    message_ref, term_ref, base0_ref, near0_ref, base1_ref, near1_ref,
    heads1_ref, qkv_ref, w_ref, gate_ref, residual_ref, semaphores, *, firsts
):
    moves = [
        (qkv_far, qkv_ref), (w_far, w_ref), (gate_far, gate_ref), (residual_far, residual_ref)
    ]
    copies = [pltpu.make_async_copy(*move, semaphores.at[i]) for i, move in enumerate(moves)]
    for copy in copies:
        copy.start()
    copies[0].wait()
    spatial_heads(qkv_ref, heads1_ref, firsts[1])
    for copy in copies[1:]:
        copy.wait()
    half, both = message_ref.shape
    features = w_ref.shape[-1]
    far = chip_columns(features, 1)
    term = dot(heads1_ref[...], w_ref[:, far]) * gate_ref[:, far]
    term_ref[...] = term[:half]
    message_ref[...] = term[half:].astype(message_ref.dtype)
    share = both // 2
    heads0 = jnp.concatenate([own0_ref[...], other0_ref[...]], axis=0)
    for first, heads, base_ref, near_ref in (
        (firsts[0], heads0, base0_ref, near0_ref),
        (firsts[1], heads1_ref[...], base1_ref, near1_ref),
    ):
        size = base_ref.shape[0]
        for flip in range(2):
            place = pl.multiple_of((core_of() ^ flip) * share, share)
            lanes = pl.ds(pl.multiple_of(chip_of() * both + place, share), share)
            term = dot(heads, w_ref[:, lanes]) * gate_ref[:, lanes]
            if flip == 0:
                term += piece_rows(residual_ref, first, size // SHARES, slice(None)).astype(
                    jnp.float32
                )
            base_ref[:, pl.ds(place, share)] = term[:size]
            near_ref[:, pl.ds(place, share)] = term[size:].astype(near_ref.dtype)


def add_kernel(a_ref, b_ref, out_ref):
    out_ref[...] = (a_ref[...] + b_ref[...].astype(jnp.float32)).astype(out_ref.dtype)


def update_kernel(base_ref, arrived_ref, own_ref, other_ref, *piece_refs):
    updated = (base_ref[...] + arrived_ref[...].astype(jnp.float32)).astype(jnp.bfloat16)
    count = piece_refs[0].shape[0]
    for i, piece_ref in enumerate(piece_refs):
        piece_ref[...] = updated[i * count : (i + 1) * count]
    share = own_ref.shape[-1]
    left, right = updated[:, :share], updated[:, share:]
    core = core_of()
    own_ref[...] = jnp.where(core == 0, left, right)
    other_ref[...] = jnp.where(core == 0, right, left)


def split_normalize(near, far, gain_ref, shift_ref, out_ref):
    half = near.shape[-1]
    blocks = [
        (ref, pl.multiple_of((chip_of() ^ flip) * half, half)) for flip, ref in enumerate((near, far))
    ]
    normalize(blocks, gain_ref, shift_ref, out_ref)


def half_kernel(
    near, far, gain_ref, shift_ref, w_ref, cos_ref, sin_ref, proj_ref, normed_ref
):
    split_normalize(near, far, gain_ref, shift_ref, normed_ref)
    places = [frame_of(i) for i in range(SHARES)]
    project(normed_ref, places, w_ref, cos_ref, sin_ref, proj_ref)


def split_temporal_kernel(
    own_proj_ref, near, far, gain_ref, shift_ref, w_ref, cos_ref, sin_ref,
    own_ref, other_ref, normed_ref, proj_ref,
):
    split_normalize(near, far, gain_ref, shift_ref, normed_ref)
    places = [frame_of(SHARES + i) for i in range(SHARES)]
    project(normed_ref, places, w_ref, cos_ref, sin_ref, proj_ref)
    split_mix(own_proj_ref, proj_ref, own_ref, other_ref)


def split_mix(own_proj_ref, proj_ref, own_ref, other_ref):
    count = own_ref.shape[0] // SHARES

    def write(i, low, head, value):
        ref = own_ref if i < SHARES else other_ref
        start = (i % SHARES) * count + low
        ref[start : start + value.shape[0], head] = value

    spans = [(ref, i * count) for ref in (own_proj_ref, proj_ref) for i in range(SHARES)]
    mix(spans, count, write)


def centred(rows, gain):
    values = rows.astype(jnp.float32)
    total = jnp.sum(values, axis=-1, keepdims=True)
    square = jnp.sum(values * values, axis=-1, keepdims=True)
    return total, square, ((values - total / rows.shape[-1]) * gain).astype(jnp.bfloat16)


def half_lanes(features, flip):
    half = features // 2
    return pl.ds(pl.multiple_of((chip_of() ^ flip) * half, half), half)


def near_kernel(
    own_ref, other_ref, gain_ref, shift_ref, w_ref,
    own_acc_ref, other_acc_ref, own_total_ref, other_total_ref, own_square_ref, other_square_ref,
    fixed_ref,
):
    features = w_ref.shape[0]
    near = half_lanes(features, 0)
    gain = 1.0 + gain_ref[:, near]
    for ref, acc_ref, total_ref, square_ref in (
        (own_ref, own_acc_ref, own_total_ref, own_square_ref),
        (other_ref, other_acc_ref, other_total_ref, other_square_ref),
    ):
        total_ref[...], square_ref[...], scaled = centred(ref[...], gain)
        acc_ref[...] = dot(scaled, w_ref[near, :])
    shifted = 0.0
    for flip in range(2):
        lanes = half_lanes(features, flip)
        rows = []
        for row in (1.0 + gain_ref[:, lanes], shift_ref[:, lanes]):
            high = row.astype(jnp.bfloat16).astype(jnp.float32)
            rows += [high, row - high]
        rows.append(jnp.zeros((GROUP - len(rows), rows[0].shape[-1]), jnp.float32))
        product = dot(jnp.concatenate(rows, axis=0).astype(jnp.bfloat16), w_ref[lanes, :])
        fixed_ref[flip : flip + 1, :] = product[0:1] + product[1:2]
        shifted += product[2:3] + product[3:4]
    fixed_ref[2:3, :] = shifted
    fixed_ref[3:, :] = jnp.zeros((fixed_ref.shape[0] - 3, fixed_ref.shape[1]), jnp.float32)


def join_halves(
    far_ref, acc_ref, total_ref, square_ref, fixed_ref, gain_ref, w_ref, cos_ref, sin_ref,
    proj_ref, pieces,
):
    features = w_ref.shape[0]
    half = features // 2
    far = half_lanes(features, 1)
    total, square, scaled = centred(far_ref[...], 1.0 + gain_ref[:, far])
    near_total = total_ref[...]
    mean = (near_total + total) / features
    rate = lax.rsqrt((square_ref[...] + square) / features - mean * mean + EPSILON)
    acc = acc_ref[...] + dot(scaled, w_ref[far, :])
    acc += (near_total / half - mean) * fixed_ref[0:1, :] + (total / half - mean) * fixed_ref[1:2, :]
    places = [frame_of(i) for i in pieces]
    turn(acc * rate + fixed_ref[2:3, :], places, cos_ref, sin_ref, proj_ref)


def own_far_kernel(*refs):
    join_halves(*refs, OWN)


def other_far_kernel(own_proj_ref, *refs):
    *inputs, own_ref, other_ref, proj_ref = refs
    join_halves(*inputs, proj_ref, OTHER)
    split_mix(own_proj_ref, proj_ref, own_ref, other_ref)


def pack_kernel(*refs):
    block_refs, out_refs = refs[:-SHARES], refs[-SHARES:]
    for i, out_ref in enumerate(out_refs):
        start = 0
        for ref in block_refs:
            count = ref.shape[0] // SHARES
            out_ref[start : start + count] = ref[i * count : (i + 1) * count]
            start += count


def unpack_kernel(*refs):
    *piece_refs, out_ref = refs
    count = piece_refs[0].shape[0] // 2
    for i, ref in enumerate(piece_refs):
        out_ref[i * count : (i + 1) * count] = ref[count:]


def place_updated_kernel(*refs, chunks):
    *block_refs, out_ref = refs
    for (first, rows), own_ref, other_ref in zip(chunks, block_refs[::2], block_refs[1::2]):
        count = rows // (2 * SHARES)
        for i in range(2 * SHARES):
            ref = own_ref if i < SHARES else other_ref
            start = (i % SHARES) * count
            out_ref[piece_span(first, count, i), :] = ref[start : start + count, :]


def place_mixed_kernel(*refs, chunks):
    *own_refs, other_ref, out_ref = refs
    size = own_refs[0].shape[0] // 2
    start = 0
    for first, rows in chunks:
        count = rows // (2 * SHARES)
        for i in range(SHARES):
            out_ref[piece_span(first, count, i), :] = own_refs[i][start : start + count, :]
            low = i * size + start
            out_ref[piece_span(first, count, SHARES + i), :] = other_ref[low : low + count, :]
        start += count


def swap(value, axis, size, k):
    return lax.ppermute(value, axis, [(i, i ^ k) for i in range(size)])


def rotation_tables(frames):
    rates = 10000.0 ** (-2.0 * np.arange(HEAD_DIM // 2, dtype=np.float32) / HEAD_DIM)
    angles = np.arange(frames, dtype=np.float32)[:, None] * rates.astype(np.float32)
    cosine, sine = np.cos(angles), np.sin(angles)
    return (
        jnp.asarray(np.concatenate([cosine, cosine], axis=1), jnp.float32),
        jnp.asarray(np.concatenate([-sine, sine], axis=1), jnp.float32),
    )


def piece_pairs(n_seq, n_mlp, index):
    return [
        (s * n_mlp + m, (s ^ PARTNERS[m % 2][index]) * n_mlp + m)
        for s in range(n_seq)
        for m in range(n_mlp)
    ]


def in_hbm(array):
    return pltpu.with_memory_space_constraint(array, pltpu.HBM)


def after(value, *others):
    return lax.optimization_barrier((value,) + others)[0]


def split_on_device(
    residual, spatial_qkv, spatial_out, temporal_qkv, shift, scale, gate, *, n_seq, n_mlp
):
    frames, patches, share = residual.shape
    width = spatial_qkv.shape[-1]
    features = share * n_mlp
    both = 2 * share
    tokens = frames * patches
    bf16, f32 = jnp.bfloat16, jnp.float32
    flat_residual = residual.reshape(tokens, share)
    qkv = spatial_qkv.transpose(2, 0, 1, 3).reshape(3, tokens, width)
    gate_row = gate.reshape(1, features)
    gain_row, shift_row = scale.reshape(1, features), shift.reshape(1, features)
    cosine, sine = rotation_tables(n_seq)

    def shape(rows, columns, kind=bf16):
        return jax.ShapeDtypeStruct((rows, columns), kind)

    def send_pieces(pieces):
        return [
            lax.ppermute(piece, ("seq", "mlp"), piece_pairs(n_seq, n_mlp, i))
            for i, piece in enumerate(pieces)
        ]

    once = jnp.minimum(lax.axis_index("seq") + 1, 1)

    chunks = []
    first = 0
    for rows in CHUNK_ROWS:
        chunks.append((first, rows))
        first += rows

    (first0, rows0), (first1, rows1) = chunks
    half0, half1 = rows0 // 2, rows1 // 2
    other_heads, message, *held = call(
        functools.partial(first_spatial_kernel, first=first0),
        [
            shape(half0, width),
            shape(half0, both),
            pltpu.VMEM((width, both), bf16),
            pltpu.VMEM((1, both), f32),
            pltpu.VMEM(qkv.shape, bf16),
        ],
        inputs=3,
        far=3,
        scratch=(pltpu.SemaphoreType.DMA((4,)),),
    )(*(in_hbm(one) for one in (qkv, spatial_out, gate_row)))
    message = swap(message, "mlp", n_mlp, 1)
    own_heads, far_term = call(
        functools.partial(term_kernel, first=first0),
        [shape(half0, width), shape(half0, both, f32)],
        inputs=3,
    )(*held)
    sent = call(add_kernel, shape(half0, both), inputs=2)(far_term, message)
    arrived0 = swap(sent, "mlp", n_mlp, 2)

    def rest(own_heads, other_heads, *operands):
        message, far_term, base0, near0, base1, near1 = call(
            functools.partial(rest_kernel, firsts=(first0, first1)),
            [
                shape(half1, both),
                shape(half1, both, f32),
                shape(half0, both, f32),
                shape(half0, both),
                shape(half1, both, f32),
                shape(half1, both),
            ],
            inputs=6,
            far=4,
            scratch=(
                pltpu.VMEM((rows1, width), bf16),
                *(pltpu.VMEM(one.shape, one.dtype) for one in operands),
                pltpu.SemaphoreType.DMA((4,)),
            ),
        )(own_heads, other_heads, *(in_hbm(one) for one in operands))
        message, near0, near1 = (swap(one, "mlp", n_mlp, 1) for one in (message, near0, near1))
        sent = call(add_kernel, shape(half1, both), inputs=2)(far_term, message)
        base0, base1 = (
            call(add_kernel, shape(*base.shape, f32), inputs=2)(base, near)
            for base, near in ((base0, near0), (base1, near1))
        )
        return sent, base0, base1

    def nothing(*_):
        return (
            jnp.zeros((half1, both), bf16),
            jnp.zeros((half0, both), f32),
            jnp.zeros((half1, both), f32),
        )

    sent, base0, base1 = lax.cond(
        once > 0,
        rest,
        nothing,
        after(own_heads, sent),
        other_heads,
        qkv,
        spatial_out,
        gate_row,
        flat_residual,
    )
    arrived1 = swap(sent, "mlp", n_mlp, 2)
    arrived0 = after(arrived0, sent)

    def update(rows, base, arrived):
        half = rows // 2
        own, other, *pieces = call(
            update_kernel,
            [shape(half, share)] * 2 + [shape(half // SHARES, both)] * SHARES,
            inputs=2,
        )(base, arrived)
        return [own, swap(other, "mlp", n_mlp, 1)], pieces

    blocks0, pieces = update(rows0, base0, arrived0)
    pieces = lax.fori_loop(0, once, lambda _, pieces: send_pieces(pieces), pieces)
    near0 = jnp.concatenate(pieces, axis=0)
    blocks1, pieces = update(rows1, base1, after(arrived1, near0))

    def last_exchange(temporal_qkv, near, *pieces):
        far = swap(near, "mlp", n_mlp, 2)
        return (*send_pieces(pieces), far, hold_weights(temporal_qkv))

    def no_exchange(temporal_qkv, near, *pieces):
        return (*pieces, near, jnp.zeros((features, 3 * width), bf16))

    *pieces, far0, weights = lax.cond(
        once > 0, last_exchange, no_exchange, temporal_qkv, near0, *pieces
    )
    nears = [near0, jnp.concatenate(pieces, axis=0)]
    blocks = blocks0 + blocks1

    own_mixed, other_mixed = [], []
    for (first, rows), near in zip(chunks, nears):
        half = rows // 2
        far = swap(near, "mlp", n_mlp, 2) if own_mixed else far0
        other_near = swap(near, "mlp", n_mlp, 1)
        if not own_mixed:
            far = after(far, *nears)
        else:
            updated = call(
                functools.partial(place_updated_kernel, chunks=chunks),
                shape(tokens, share),
                inputs=len(blocks),
            )(*blocks)
            line = jax.ShapeDtypeStruct((half, 1), f32)
            own_acc, other_acc, own_total, other_total, own_square, other_square, fixed = call(
                near_kernel,
                [shape(half, 3 * width, f32)] * 2 + [line] * 4 + [shape(8, 3 * width, f32)],
                inputs=5,
            )(near, other_near, gain_row, shift_row, weights)
            far = after(far, other_mixed[-1], updated, fixed)
        other_far = swap(far, "mlp", n_mlp, 1)
        if own_mixed:
            rest_in = (fixed, gain_row, weights, cosine, sine)
            own_proj = call(own_far_kernel, shape(half, 3 * width), inputs=9)(
                far, own_acc, own_total, own_square, *rest_in
            )
            own, other = call(
                other_far_kernel,
                [shape(half, width)] * 2,
                inputs=10,
                scratch=(pltpu.VMEM((half, 3 * width), bf16),),
            )(own_proj, other_far, other_acc, other_total, other_square, *rest_in)
        else:
            rest_in = (gain_row, shift_row, weights, cosine, sine)
            own_proj = call(
                half_kernel,
                shape(half, 3 * width),
                inputs=7,
                scratch=(pltpu.VMEM((half, features), bf16),),
            )(near, far, *rest_in)
            own, other = call(
                split_temporal_kernel,
                [shape(half, width)] * 2,
                inputs=8,
                scratch=(
                    pltpu.VMEM((half, features), bf16),
                    pltpu.VMEM((half, 3 * width), bf16),
                ),
            )(own_proj, other_near, other_far, *rest_in)
        own_mixed.append(own)
        other_mixed.append(swap(other, "mlp", n_mlp, 1))
    packed = call(
        pack_kernel, [shape(2 * tokens // (2 * SHARES), width)] * SHARES, inputs=2 * len(chunks)
    )(*own_mixed, *other_mixed)
    pieces = send_pieces(packed)
    others = call(unpack_kernel, shape(tokens // 2, width), inputs=SHARES)(*pieces)
    results = pieces + [swap(others, "mlp", n_mlp, 1)]
    result = call(
        functools.partial(place_mixed_kernel, chunks=chunks),
        shape(tokens, width),
        inputs=len(results),
    )(*results)
    return updated.reshape(frames, patches, share), result.reshape(frames, patches, width)


def heads_kernel(qkv_ref, out_ref):
    for lane in range(0, out_ref.shape[-1], HEAD_DIM):
        head = slice(lane, lane + HEAD_DIM)
        (out_ref[:, head],) = attend([tuple(qkv_ref[part, :, head] for part in range(3))])


def columns_kernel(own_ref, other_ref, own_w_ref, other_w_ref, gate_ref, out_ref):
    term = dot(own_ref[...], own_w_ref[...]) + dot(other_ref[...], other_w_ref[...])
    out_ref[...] = (term * gate_ref[...]).astype(out_ref.dtype)


def temporal_kernel(
    u0, u1, u2, u3, gain_ref, shift_ref, w_ref, cos_ref, sin_ref, out_ref, normed_ref, proj_ref
):
    share = u0.shape[-1]
    frames = cos_ref.shape[0]
    count = out_ref.shape[0] // frames
    blocks = [
        (ref, pl.multiple_of((lax.axis_index("mlp") ^ k) * share, share))
        for k, ref in enumerate((u0, u1, u2, u3))
    ]
    normalize(blocks, gain_ref, shift_ref, normed_ref)
    project(normed_ref, range(frames), w_ref, cos_ref, sin_ref, proj_ref)

    def write(f, low, head, value):
        start = f * count + low
        out_ref[start : start + value.shape[0], head] = value

    mix([(proj_ref, f * count) for f in range(frames)], count, write)


def on_device(
    residual, spatial_qkv, spatial_out, temporal_qkv, shift, scale, gate, *, n_seq, n_mlp
):
    frames, patches, share = residual.shape
    width = spatial_qkv.shape[-1]
    features = share * n_mlp
    rows = frames * patches
    count = rows // n_seq
    mlp = lax.axis_index("mlp")
    bf16, f32 = jnp.bfloat16, jnp.float32
    qkv = spatial_qkv.transpose(2, 0, 1, 3).reshape(3, rows, width)
    gate_row = gate.reshape(1, features)

    def columns(array, block):
        return lax.dynamic_slice_in_dim(array, block * share, share, 1)

    heads = call(heads_kernel, jax.ShapeDtypeStruct((rows, width), bf16), inputs=1)(qkv)
    others = swap(heads, "mlp", n_mlp, 1)

    def term(block, kind):
        other_w = swap(columns(spatial_out, block ^ 1), "mlp", n_mlp, 1)
        return call(columns_kernel, jax.ShapeDtypeStruct((rows, share), kind), inputs=5)(
            heads, others, columns(spatial_out, block), other_w, columns(gate_row, block)
        )

    arrived = swap(term(mlp ^ 2, bf16), "mlp", n_mlp, 2)
    branch = term(mlp, f32) + arrived.astype(f32)
    updated = (residual.reshape(rows, share).astype(f32) + branch).astype(bf16)
    mine = lax.all_to_all(
        updated.reshape(n_seq, count, share), "seq", 0, 0, tiled=True
    ).reshape(rows, share)
    across = swap(mine, "mlp", n_mlp, 2)
    mixed = call(
        temporal_kernel,
        jax.ShapeDtypeStruct((rows, width), bf16),
        inputs=9,
        scratch=(pltpu.VMEM((rows, features), bf16), pltpu.VMEM((rows, 3 * width), bf16)),
    )(
        mine,
        swap(mine, "mlp", n_mlp, 1),
        across,
        swap(across, "mlp", n_mlp, 1),
        scale.reshape(1, features),
        shift.reshape(1, features),
        hold_weights(temporal_qkv),
        *rotation_tables(n_seq),
    )
    result = lax.all_to_all(
        mixed.reshape(n_seq, count, width), "seq", 0, 0, tiled=True
    ).reshape(rows, width)
    return updated.reshape(frames, patches, share), result.reshape(frames, patches, width)


def solution(mesh):
    sizes = dict(n_seq=mesh.shape["seq"], n_mlp=mesh.shape["mlp"])
    split = sizes["n_seq"] == 2 * SHARES and sizes["n_mlp"] == 4
    return jax.shard_map(
        functools.partial(split_on_device if split else on_device, **sizes),
        mesh=mesh,
        in_specs=(
            P("seq", None, "mlp"),
            P("seq", None, None, "mlp"),
            P("mlp", None),
            P(None, None, "mlp"),
            P(),
            P(),
            P(),
        ),
        out_specs=(P("seq", None, "mlp"), P("seq", None, "mlp")),
        check_vma=False,
    )
```
